32 devices in a mesh: section: 2 (over core), dp: 16 (over z, y, x).
Axes of the slice: x: 2, y: 2, z: 4, core: 2. Of those that a mesh axis runs over, the one named last changes fastest.
Arguments:
- stream_in: bfloat16 [4, 128, 4, 8, 512], P(None, 'dp'), may hold values from -12 to 12
- image_count: int32 [16, 4], P('dp'), may hold values from 1 to 2, 6 in all within a row
- out_grad: bfloat16 [4, 128, 1, 2, 512], P(None, 'dp'), may hold values from -6 to 6
- first_conv: bfloat16 [2, 512, 4608], P('section'), may hold values from -0.09375 to 0.09375
- second_conv: bfloat16 [2, 512, 4608], P('section'), may hold values from -0.09375 to 0.09375
- squeeze: bfloat16 [2, 3, 512, 1024], P('section'), may hold values from -0.1875 to 0.1875
- expand: bfloat16 [2, 3, 512, 512], P('section'), may hold values from -0.25 to 0.25
- task_conv: bfloat16 [2, 3, 512, 4608], P('section'), may hold values from -0.09375 to 0.09375
- norm_gain: float32 [2, 8, 512], P('section'), may hold values from 0.5 to 1.5
- norm_shift: float32 [2, 8, 512], P('section'), may hold values from -2.5 to 2.5
- squeeze_gain: float32 [2, 3, 512], P('section'), may hold values from 0.5 to 1.5
- squeeze_shift: float32 [2, 3, 512], P('section'), may hold values from -2.5 to 2.5
Outputs:
- features: bfloat16 [2, 4, 128, 2, 4, 512], P('section', None, 'dp')
- input_grad: float32 [2, 4, 128, 4, 8, 512], P('section', None, 'dp')
- first_conv_grad: float32 [2, 2359296], P('section', 'dp')
- second_conv_grad: float32 [2, 2359296], P('section', 'dp')
- squeeze_grad: float32 [2, 1572864], P('section', 'dp')
- expand_grad: float32 [2, 786432], P('section', 'dp')
- task_conv_grad: float32 [2, 7077888], P('section', 'dp')
- norm_gain_grad: float32 [2, 8, 512], P('section')
- norm_shift_grad: float32 [2, 8, 512], P('section')
- squeeze_gain_grad: float32 [2, 3, 512], P('section')
- squeeze_shift_grad: float32 [2, 3, 512], P('section')
- rms: float32 [2, 4], P('section')
The draws below stay inside these ranges and needn't reach their ends.
Inputs may be any that keep to these rules, and one draw needn't show every extreme that they name: `image_count`: each device's counts over its 4 micro-batches sum to 6.
All inputs are finite; a program needn't handle non-finite values.
Results may differ from the reference program's by a relative error of at most 0.024.
Values may be sent and summed in bfloat16 or wider, within the bound.
A program may use at most 576 MiB of HBM per device.

```python
import math
import jax
import jax.numpy as jnp
import numpy as np
from jax import lax

C = 512
R = 512
TASKS = 3
SLOT = 2
MICRO = 4
FH = 4
FW = 8
GROUPS = 16
IMAGES = 128


def draw_stream_in(key, part):
    key = jax.random.fold_in(key, 7)
    shape = (1 + TASKS, IMAGES, FH, FW, C)
    position = jnp.arange(IMAGES, dtype=jnp.float32) / (IMAGES - 1)
    values = jax.random.truncated_normal(key, -4.0, 4.0, shape, jnp.float32)
    rising = 1.0 + 2.0 * position
    return (values * rising[None, :, None, None, None]).astype(jnp.bfloat16)


def strengthened(drawn, stream_key, source, target, blocks, factor):
    def block_of(axis_at):
        return (jnp.arange(drawn.shape[axis_at]) // (drawn.shape[axis_at] // blocks)).reshape((-1,) + (1,) * (drawn.ndim - 1 - axis_at))

    near = jax.random.permutation(stream_key, blocks)[block_of(target)]
    second = (block_of(target) + blocks // 2) % blocks
    return jnp.where((block_of(source) == near) | (block_of(source) == second), factor * drawn, drawn)


def shard_levels(rng, dims, cuts, smallest, top_value):
    gain = 1.0
    for dim, parts in cuts:
        steps = jax.random.uniform(jax.random.fold_in(jax.random.fold_in(rng, 6), dim), (parts,), jnp.float32, smallest / len(cuts), top_value / len(cuts))
        gain = gain * jnp.repeat(jnp.exp(steps), dims[dim] // parts).reshape((-1,) + (1,) * (len(dims) - 1 - dim))
    return gain


def split_up(count, total, limit, slope):
    portions = [(1 << 20) // math.isqrt(rank ** slope) + 1 for rank in range(2, count + 1)]
    rest, given = total - limit - (count - 1), [1] * (count - 1)
    while rest > 0:
        movable = [i for i in range(count - 1) if given[i] < limit]
        whole, left = sum([portions[i] for i in movable]), rest
        for i in movable:
            extra = min(limit - given[i], max(1, left * portions[i] // whole), rest)
            given[i] = given[i] + extra
            rest = rest - extra
    return np.array([limit] + given)


def uneven(own_key, count, total, bound, skew):
    if count == 2:
        one = jax.random.randint(own_key, (), max(1, total - bound), min(bound, total - 1) + 1)
        return jnp.stack([one, total - one])
    tallies = jnp.asarray(split_up(count, total, bound, skew), jnp.int32)
    couples = (count - 1) // 2
    giver, receiver = tallies[1:1 + 2 * couples:2], tallies[2:2 + 2 * couples:2]
    room = jnp.minimum(giver - 1, bound - receiver)
    shifted = jax.random.randint(jax.random.fold_in(own_key, 1), (couples,), 0, 1 << 20) % (room + 1)
    tallies = tallies.at[1:1 + 2 * couples:2].set(giver - shifted).at[2:2 + 2 * couples:2].set(receiver + shifted)
    return tallies[jax.random.permutation(jax.random.fold_in(own_key, 2), count)]


def normal_values(rng, dims, scale, bound, shards=(), held_as=jnp.bfloat16):
    level = shard_levels(rng, dims, shards, -0.22, 0.18) if shards else 1.0
    values = jax.random.normal(rng, dims, jnp.float32) * scale * level
    return jnp.minimum(jnp.maximum(values, -bound), bound).astype(held_as)


def gaussian_with(key, shape, width, reach, split, heavy, kind=jnp.bfloat16):
    result = width * jax.random.normal(key, shape, jnp.float32)
    if split:
        result = result * shard_levels(key, shape, split, -0.22, 0.18)
    return jnp.clip(strengthened(result, jax.random.fold_in(key, 3), *heavy), -reach, reach).astype(kind)


def setup_inputs(seed: int = 0) -> dict:
    key_list = jax.random.split(jax.random.key(seed), 13)
    stream_in = draw_stream_in(jax.random.fold_in(key_list[12], 71), 0)
    image_count = jax.vmap(lambda own: uneven(own, MICRO, SLOT * MICRO - 2, SLOT, 0))(jax.random.split(key_list[1], GROUPS)).reshape((GROUPS, MICRO)).astype(jnp.int32)
    out_grad = gaussian_with(key_list[2], (1 + TASKS, IMAGES, FH // 4, FW // 4, C), 1.0, 6.0, ((1, 16),), (1, 4, 16, 2.0))
    first_conv = normal_values(key_list[3], (2, C, 9 * C), (9 * C) ** -0.5, 0.09375, ((0, 2),))
    second_conv = normal_values(key_list[4], (2, C, 9 * C), (9 * C) ** -0.5, 0.09375, ((0, 2),))
    squeeze = normal_values(key_list[5], (2, TASKS, R, 2 * C), (2 * C) ** -0.5, 0.1875, ((0, 2),))
    expand = normal_values(key_list[6], (2, TASKS, C, R), R ** -0.5, 0.25, ((0, 2),))
    task_conv = normal_values(key_list[7], (2, TASKS, C, 9 * C), (9 * C) ** -0.5, 0.09375, ((0, 2),))
    norm_gain = jnp.clip(1.0 + 0.1 * jax.random.normal(key_list[8], (2, 2 + 2 * TASKS, C), jnp.float32), 0.5, 1.5)
    norm_shift = normal_values(key_list[9], (2, 2 + 2 * TASKS, C), 0.5, 2.5, ((0, 2),), jnp.float32)
    squeeze_gain = jnp.clip(1.0 + 0.1 * jax.random.normal(key_list[10], (2, TASKS, R), jnp.float32), 0.5, 1.5)
    squeeze_shift = normal_values(key_list[11], (2, TASKS, R), 0.5, 2.5, ((0, 2),), jnp.float32)
    return {"stream_in": stream_in, "image_count": image_count, "out_grad": out_grad, "first_conv": first_conv, "second_conv": second_conv, "squeeze": squeeze, "expand": expand, "task_conv": task_conv, "norm_gain": norm_gain, "norm_shift": norm_shift, "squeeze_gain": squeeze_gain, "squeeze_shift": squeeze_shift}


@jax.custom_vjp
def low(v):
    return lax.optimization_barrier(v.astype(jnp.bfloat16)).astype(jnp.float32)

@jax.custom_vjp
def low_back(v):
    return v

def low_keep(v):
    return (low(v), None)

def low_pass(kept, grad):
    return (grad,)

def back_keep(v):
    return (v, None)

def back_low(kept, grad):
    return (low(grad),)
low.defvjp(low_keep, low_pass)
low_back.defvjp(back_keep, back_low)
EPSILON = 1e-05
FULL_PRECISION = lax.Precision.HIGHEST

def conv_taps(frames, weight):
    outputs = weight.shape[0]
    kernel = weight.reshape(outputs, 3, 3, -1).transpose(1, 2, 3, 0)
    return lax.conv_general_dilated(frames, kernel, (1, 1), 'SAME', dimension_numbers=('NHWC', 'HWIO', 'NHWC'), precision=FULL_PRECISION)

def batch_norm(values, scale_by, offset_by, group_live, counts):
    shaped = values.reshape((GROUPS, MICRO, SLOT) + values.shape[1:])
    masked = shaped * group_live
    totals = lax.optimization_barrier(jnp.sum(masked, axis=(0, 2, 3, 4)))
    squares = lax.optimization_barrier(jnp.sum(masked * shaped, axis=(0, 2, 3, 4)))
    average = totals / counts[:, None]
    spread = squares / counts[:, None] - average * average
    inverse = lax.rsqrt(spread + EPSILON)
    normed = (shaped - average[None, :, None, None, None, :]) * inverse[None, :, None, None, None, :]
    return (normed * scale_by + offset_by).reshape(values.shape)

def soft_pool(values):
    leading = values.shape[:-3]
    height, breadth, channels = values.shape[-3:]
    blocks = values.reshape(leading + (height // 2, 2, breadth // 2, 2, channels))
    summit = lax.optimization_barrier(jnp.max(blocks, axis=(-4, -2), keepdims=True))
    pooled = summit + jnp.log(lax.optimization_barrier(jnp.mean(jnp.exp(blocks - summit), axis=(-4, -2), keepdims=True)))
    return pooled.reshape(leading + (height // 2, breadth // 2, channels))

def encoder_block(shared, earlier, first_weight, second_weight, squeeze_weight, expand_weight, task_weight, gain_rows, shift_rows, squeeze_scale, squeeze_offset, group_live, counts, image_live):

    def normalize_rows(values, row_scale, row_offset):
        return batch_norm(values, row_scale, row_offset, group_live, counts)
    first_pre = low_back(conv_taps(shared, first_weight))
    first_output = jax.nn.silu(normalize_rows(first_pre, gain_rows[0], shift_rows[0]))
    rounded_first = low(first_output)
    second_pre = low_back(conv_taps(rounded_first, second_weight))
    shared_out = jax.nn.silu(normalize_rows(second_pre, gain_rows[1], shift_rows[1]))
    outputs = [soft_pool(shared_out)]
    for task_index in range(TASKS):
        joined = jnp.concatenate([rounded_first, earlier[task_index]], axis=-1)
        narrow = low_back(jnp.einsum('nhwc,rc->nhwr', joined, squeeze_weight[task_index], precision=FULL_PRECISION))
        hidden_act = jax.nn.silu(normalize_rows(narrow, squeeze_scale[task_index], squeeze_offset[task_index]))
        widened = low_back(jnp.einsum('nhwr,cr->nhwc', low(hidden_act), expand_weight[task_index], precision=FULL_PRECISION))
        task_mask = jax.nn.sigmoid(normalize_rows(widened, gain_rows[2 + task_index], shift_rows[2 + task_index]))
        attended = task_mask * shared_out
        task_pre = low_back(conv_taps(low(attended), task_weight[task_index]))
        task_out = jax.nn.silu(normalize_rows(task_pre, gain_rows[2 + TASKS + task_index], shift_rows[2 + TASKS + task_index]))
        outputs.append(soft_pool(task_out))
    return jnp.stack(outputs) * image_live

def reference(stream_in, image_count, out_grad, first_conv, second_conv, squeeze, expand, task_conv, norm_gain, norm_shift, squeeze_gain, squeeze_shift):
    slot_index = jnp.arange(IMAGES, dtype=jnp.int32)
    device_of = (slot_index // (MICRO * SLOT)).astype(jnp.int32)
    micro_of = (slot_index // SLOT % MICRO).astype(jnp.int32)
    live = (slot_index % SLOT < image_count[device_of, micro_of]).astype(jnp.float32)
    image_live = live.reshape(IMAGES, 1, 1, 1)
    group_live = live.reshape(GROUPS, MICRO, SLOT, 1, 1, 1)
    per_micro = lax.optimization_barrier(jnp.sum(image_count, axis=0)).astype(jnp.float32)
    stream = stream_in.astype(jnp.float32)
    link = jnp.zeros((1 + TASKS, IMAGES, FH // 2, FW // 2, C), jnp.float32)

    def whole(stream_values, link_values, first_weight, second_weight, squeeze_weight, expand_weight, task_weight, gain_rows, shift_rows, squeeze_scale, squeeze_offset):

        def run_section(section_index, inputs, counts):
            return encoder_block(inputs[0], inputs[1:], first_weight[section_index], second_weight[section_index], squeeze_weight[section_index], expand_weight[section_index], task_weight[section_index], gain_rows[section_index], shift_rows[section_index], squeeze_scale[section_index], squeeze_offset[section_index], group_live, counts, image_live)
        block_one = run_section(0, stream_values, per_micro * (FH * FW))
        sent = low_back(low(block_one) + link_values)
        block_two = run_section(1, sent, per_micro * (FH // 2 * (FW // 2)))
        return (block_two, block_one)
    block_two, pullback, block_one = jax.vjp(whole, stream, link, first_conv.astype(jnp.float32), second_conv.astype(jnp.float32), squeeze.astype(jnp.float32), expand.astype(jnp.float32), task_conv.astype(jnp.float32), norm_gain.astype(jnp.float32), norm_shift.astype(jnp.float32), squeeze_gain.astype(jnp.float32), squeeze_shift.astype(jnp.float32), has_aux=True)
    gradients = pullback(out_grad.astype(jnp.float32))
    pad_half = ((0, 0), (0, 0), (0, FH // 2), (0, FW // 2), (0, 0))
    pad_quarter = ((0, 0), (0, 0), (0, FH // 4), (0, FW // 4), (0, 0))
    input_grad = jnp.stack([gradients[0], jnp.pad(gradients[1], pad_half)])
    features = jnp.stack([block_one, jnp.pad(block_two, pad_quarter)]).astype(jnp.bfloat16)
    live_total = jnp.sum(live)

    def root_mean(block, pixels):
        return jnp.sqrt(lax.optimization_barrier(jnp.sum(block * block, axis=(1, 2, 3, 4))) / (live_total * (pixels * C)))
    root_square = jnp.stack([root_mean(block_one, FH // 2 * (FW // 2)), root_mean(block_two, FH // 4 * (FW // 4))])
    return (features, input_grad, gradients[2].reshape(2, -1), gradients[3].reshape(2, -1), gradients[4].reshape(2, -1), gradients[5].reshape(2, -1), gradients[6].reshape(2, -1), gradients[7], gradients[8], gradients[9], gradients[10], root_square)
```

```python
import functools
import types

import jax
import jax.numpy as jnp
from jax import lax
from jax.experimental import pallas as pl
from jax.experimental.pallas import tpu as pltpu
from jax.sharding import PartitionSpec as P

EPSILON = 1e-05
SUM_ROWS = 40


def stages_of(size):
    stages = []
    stride = 1
    while stride < size:
        radix = next(r for r in (4, 2, 3, 5, 7, size // stride) if (size // stride) % r == 0)
        stages.append((radix, stride))
        stride *= radix
    return stages


def sum_kernel(stages, own_ref, out_ref, *scratch):
    slots, (send_sem, recv_sem) = scratch[: len(stages)], scratch[len(stages) :]
    section = lax.axis_index("section")
    me = lax.axis_index("dp")
    barrier = pltpu.get_barrier_semaphore()
    peers = []
    for radix, stride in stages:
        digit = lax.rem(me // stride, radix)
        group = [
            me + (lax.rem(digit + step, radix) - digit) * stride for step in range(1, radix)
        ]
        peers.append((digit, group))
    total = sum(len(group) for _, group in peers)
    for _, group in peers:
        for peer in group:
            pl.semaphore_signal(
                barrier, inc=1, device_id=(section, peer), device_id_type=pl.DeviceIdType.MESH
            )
    pl.semaphore_wait(barrier, total)
    for index, (radix, stride) in enumerate(stages):
        digit, group = peers[index]
        held = slots[index]
        held[digit] = own_ref[...] if index == 0 else out_ref[...]
        copies = []
        for step, peer in enumerate(group):
            copy = pltpu.make_async_remote_copy(
                src_ref=held.at[digit],
                dst_ref=held.at[digit],
                send_sem=send_sem.at[index, step],
                recv_sem=recv_sem.at[index, step],
                device_id=(section, peer),
                device_id_type=pl.DeviceIdType.MESH,
            )
            copy.start()
            copies.append(copy)
        for copy in copies:
            copy.wait_recv()
        summed = held[0]
        for place in range(1, radix):
            summed = summed + held[place]
        out_ref[...] = summed
        for copy in copies:
            copy.wait_send()


def sum_over_groups(rows):
    stages = stages_of(lax.axis_size("dp"))
    widest = max(radix for radix, _ in stages)
    return pl.pallas_call(
        functools.partial(sum_kernel, stages),
        out_shape=jax.ShapeDtypeStruct(rows.shape, jnp.float32),
        in_specs=[pl.BlockSpec(memory_space=pltpu.VMEM)],
        out_specs=pl.BlockSpec(memory_space=pltpu.VMEM),
        scratch_shapes=[pltpu.VMEM((radix,) + rows.shape, jnp.float32) for radix, _ in stages]
        + [
            pltpu.SemaphoreType.DMA((len(stages), widest)),
            pltpu.SemaphoreType.DMA((len(stages), widest)),
        ],
        compiler_params=pltpu.CompilerParams(collective_id=0, has_side_effects=True),
        name="group_sum",
    )(rows)


def from_behind(shard, axis, by):
    size = lax.axis_size(axis)
    pairs = [(i, i + by) for i in range(size) if 0 <= i + by < size]
    return lax.ppermute(shard, axis, pairs)


def broadcast_rows(vector):
    return vector[..., None, None, None, :]


def affine_rows(normed, scale_by, offset_by):
    return normed * broadcast_rows(scale_by) + broadcast_rows(offset_by)


def silu_slope(active):
    sigmoid_of = jax.nn.sigmoid(active)
    return sigmoid_of * (1.0 + active * (1.0 - sigmoid_of))


def pixel_sums(values, pixel_weight):
    weighted = values * pixel_weight
    return jnp.stack(
        [jnp.sum(weighted, axis=(-4, -3, -2)), jnp.sum(weighted * values, axis=(-4, -3, -2))],
        axis=-2,
    )


def gradient_sums(upstream, normed, pixel_weight):
    weighted = upstream * pixel_weight
    return jnp.stack(
        [jnp.sum(weighted, axis=(-4, -3, -2)), jnp.sum(weighted * normed, axis=(-4, -3, -2))],
        axis=-2,
    )


def summed_members(members):
    rows = [member.reshape(-1, member.shape[-1]) for member in members]
    used = sum(row.shape[0] for row in rows)
    packed = jnp.concatenate(
        rows + [jnp.zeros((SUM_ROWS - used, rows[0].shape[-1]), jnp.float32)], axis=0
    )
    summed = sum_over_groups(packed)
    results = []
    offset = 0
    for member, row in zip(members, rows):
        results.append(summed[offset : offset + row.shape[0]].reshape(member.shape))
        offset += row.shape[0]
    return results


def normalize(values, moments, counted):
    average = moments[..., 0, :] / counted
    spread = moments[..., 1, :] / counted - average * average
    inverse = lax.rsqrt(spread + EPSILON)
    return ((values - broadcast_rows(average)) * broadcast_rows(inverse), inverse)


def norm_backward(upstream, normed, inverse, scale_by, sums, counted, pixel_weight):
    shift_part = broadcast_rows(sums[..., 0, :])
    scale_part = broadcast_rows(sums[..., 1, :])
    return (
        broadcast_rows(inverse * scale_by)
        * (upstream - (shift_part + normed * scale_part) / broadcast_rows(counted))
        * pixel_weight
    )


def window_blocks(values):
    leading = values.shape[:-3]
    height, breadth, channels = values.shape[-3:]
    return values.reshape(leading + (height // 2, 2, breadth // 2, 2, channels))


def soft_pool_blocks(blocks):
    summit = jnp.max(blocks, axis=(-4, -2), keepdims=True)
    return summit + jnp.log(jnp.mean(jnp.exp(blocks - summit), axis=(-4, -2), keepdims=True))


def soft_pool(values):
    pooled = soft_pool_blocks(window_blocks(values))
    return pooled.reshape(
        values.shape[:-3] + (values.shape[-3] // 2, values.shape[-2] // 2, values.shape[-1])
    )


def pool_back(upstream, values):
    blocks = window_blocks(values)
    pooled = soft_pool_blocks(blocks)
    weight_share = jnp.exp(blocks - pooled) * 0.25
    spread = upstream.reshape(pooled.shape) * weight_share
    return spread.reshape(values.shape)


def patch_columns(frames):
    height, breadth = (frames.shape[-3], frames.shape[-2])
    padding = [(0, 0)] * (frames.ndim - 3) + [(1, 1), (1, 1), (0, 0)]
    padded = jnp.pad(frames, padding)
    return jnp.concatenate(
        [
            padded[..., down_shift : down_shift + height, side_shift : side_shift + breadth, :]
            for down_shift in range(3)
            for side_shift in range(3)
        ],
        axis=-1,
    )


def columns_back(grad_columns, channels):
    height, breadth = (grad_columns.shape[-3], grad_columns.shape[-2])
    leading = [(0, 0)] * (grad_columns.ndim - 3)
    summed = None
    for tap_index in range(9):
        down_shift, side_shift = (tap_index // 3, tap_index % 3)
        piece_of = grad_columns[..., tap_index * channels : (tap_index + 1) * channels]
        placed = jnp.pad(
            piece_of, leading + [(down_shift, 2 - down_shift), (side_shift, 2 - side_shift), (0, 0)]
        )
        summed = placed if summed is None else summed + placed
    return summed[..., 1 : height + 1, 1 : breadth + 1, :]


def live_rows(pixel_weight, channels):
    live = jnp.sum(pixel_weight, axis=(-4, -3, -2, -1))
    return jnp.broadcast_to(live[:, None], (live.shape[0], channels))


def section_forward(frames, pixel_weight, weights):
    (
        first_conv,
        second_conv,
        squeeze,
        expand,
        task_conv,
        norm_gain,
        norm_shift,
        squeeze_gain,
        squeeze_shift,
    ) = weights
    channels = frames.shape[-1]
    tasks = squeeze.shape[0]
    input_columns = patch_columns(frames[0])
    first_pre = jnp.einsum(
        "mshwk,ok->mshwo", input_columns, first_conv, preferred_element_type=jnp.float32
    )
    first_moments = summed_members(
        [pixel_sums(first_pre, pixel_weight), live_rows(pixel_weight, channels)]
    )
    counted = first_moments[1] * (frames.shape[-3] * frames.shape[-2])
    first_normed, first_inverse = normalize(first_pre, first_moments[0], counted)
    first_output = jax.nn.silu(affine_rows(first_normed, norm_gain[0], norm_shift[0]))
    rounded_first = (first_output).astype(jnp.bfloat16)
    middle_columns = patch_columns(rounded_first)
    second_pre = jnp.einsum(
        "mshwk,ok->mshwo", middle_columns, second_conv, preferred_element_type=jnp.float32
    )
    earlier = frames[1:]
    narrow = jnp.einsum(
        "mshwc,trc->tmshwr",
        rounded_first,
        squeeze[:, :, :channels],
        preferred_element_type=jnp.float32,
    ) + jnp.einsum(
        "tmshwc,trc->tmshwr", earlier, squeeze[:, :, channels:], preferred_element_type=jnp.float32
    )
    middle_moments = summed_members([pixel_sums(second_pre, pixel_weight), pixel_sums(narrow, pixel_weight)])
    second_normed, second_inverse = normalize(second_pre, middle_moments[0], counted)
    narrow_normed, narrow_inverse = normalize(narrow, middle_moments[1], counted)
    shared_out = jax.nn.silu(affine_rows(second_normed, norm_gain[1], norm_shift[1]))
    rounded_hidden = jax.nn.silu(affine_rows(narrow_normed, squeeze_gain[:, None], squeeze_shift[:, None])).astype(
        jnp.bfloat16
    )
    widened = jnp.einsum(
        "tmshwr,tcr->tmshwc", rounded_hidden, expand, preferred_element_type=jnp.float32
    )
    mask_moments = summed_members([pixel_sums(widened, pixel_weight)])
    widened_normed, widened_inverse = normalize(widened, mask_moments[0], counted)
    task_mask = jax.nn.sigmoid(
        affine_rows(widened_normed, norm_gain[2 : 2 + tasks][:, None], norm_shift[2 : 2 + tasks][:, None])
    )
    rounded_attended = (task_mask * shared_out).astype(jnp.bfloat16)
    attended_columns = patch_columns(rounded_attended)
    task_pre = jnp.einsum(
        "tmshwk,tok->tmshwo", attended_columns, task_conv, preferred_element_type=jnp.float32
    )
    task_moments = summed_members([pixel_sums(task_pre, pixel_weight)])
    task_normed, task_inverse = normalize(task_pre, task_moments[0], counted)
    task_out = jax.nn.silu(
        affine_rows(task_normed, norm_gain[2 + tasks :][:, None], norm_shift[2 + tasks :][:, None])
    )
    pooled = jnp.concatenate([soft_pool(shared_out)[None], soft_pool(task_out)], axis=0)
    kept_state = (
        frames,
        counted,
        first_normed,
        first_inverse,
        rounded_first,
        second_normed,
        second_inverse,
        narrow_normed,
        narrow_inverse,
        rounded_hidden,
        widened_normed,
        widened_inverse,
        rounded_attended,
        task_normed,
        task_inverse,
    )
    return (pooled, kept_state)


def section_backward(upstream, kept_state, pixel_weight, squares, weights):
    (
        first_conv,
        second_conv,
        squeeze,
        expand,
        task_conv,
        norm_gain,
        norm_shift,
        squeeze_gain,
        squeeze_shift,
    ) = weights
    (
        frames,
        counted,
        first_normed,
        first_inverse,
        rounded_first,
        second_normed,
        second_inverse,
        narrow_normed,
        narrow_inverse,
        rounded_hidden,
        widened_normed,
        widened_inverse,
        rounded_attended,
        task_normed,
        task_inverse,
    ) = kept_state
    channels = frames.shape[-1]
    tasks = squeeze.shape[0]
    task_gain = norm_gain[2 + tasks :][:, None]
    mask_gain = norm_gain[2 : 2 + tasks][:, None]
    task_active = affine_rows(task_normed, task_gain, norm_shift[2 + tasks :][:, None])
    task_out = jax.nn.silu(task_active)
    grad_task_act = pool_back(upstream[1:], task_out) * silu_slope(task_active)
    task_sums, square_all = summed_members(
        [gradient_sums(grad_task_act, task_normed, pixel_weight), squares]
    )
    grad_task = norm_backward(
        grad_task_act, task_normed, task_inverse, task_gain, task_sums, counted, pixel_weight
    ).astype(jnp.bfloat16)
    attended_columns = patch_columns(rounded_attended)
    task_conv_grad = jnp.einsum(
        "tmshwo,tmshwk->tok", grad_task, attended_columns, preferred_element_type=jnp.float32
    )
    grad_attended = (
        columns_back(
            jnp.einsum(
                "tmshwo,tok->tmshwk", grad_task, task_conv, preferred_element_type=jnp.float32
            ),
            channels,
        )

    )
    second_active = affine_rows(second_normed, norm_gain[1], norm_shift[1])
    shared_out = jax.nn.silu(second_active)
    task_mask = jax.nn.sigmoid(affine_rows(widened_normed, mask_gain, norm_shift[2 : 2 + tasks][:, None]))
    grad_mask_act = grad_attended * shared_out * task_mask * (1.0 - task_mask)
    mask_sums = summed_members([gradient_sums(grad_mask_act, widened_normed, pixel_weight)])[0]
    grad_widened = norm_backward(
        grad_mask_act, widened_normed, widened_inverse, mask_gain, mask_sums, counted, pixel_weight
    ).astype(jnp.bfloat16)
    expand_grad = jnp.einsum(
        "tmshwc,tmshwr->tcr", grad_widened, rounded_hidden, preferred_element_type=jnp.float32
    )
    narrow_active = affine_rows(narrow_normed, squeeze_gain[:, None], squeeze_shift[:, None])
    grad_narrow_act = jnp.einsum(
        "tmshwc,tcr->tmshwr", grad_widened, expand, preferred_element_type=jnp.float32
    ) * silu_slope(narrow_active)
    grad_shared = pool_back(upstream[0], shared_out) + jnp.sum(grad_attended * task_mask, axis=0)
    grad_second_act = grad_shared * silu_slope(second_active)
    second_sums, narrow_sums = summed_members(
        [
            gradient_sums(grad_second_act, second_normed, pixel_weight),
            gradient_sums(grad_narrow_act, narrow_normed, pixel_weight),
        ]
    )
    grad_second = norm_backward(
        grad_second_act,
        second_normed,
        second_inverse,
        norm_gain[1],
        second_sums,
        counted,
        pixel_weight,
    ).astype(jnp.bfloat16)
    grad_narrow = norm_backward(
        grad_narrow_act,
        narrow_normed,
        narrow_inverse,
        squeeze_gain[:, None],
        narrow_sums,
        counted,
        pixel_weight,
    ).astype(jnp.bfloat16)
    middle_columns = patch_columns(rounded_first)
    second_conv_grad = jnp.einsum(
        "mshwo,mshwk->ok", grad_second, middle_columns, preferred_element_type=jnp.float32
    )
    earlier = frames[1:]
    squeeze_grad = jnp.concatenate(
        [
            jnp.einsum(
                "tmshwr,mshwc->trc", grad_narrow, rounded_first, preferred_element_type=jnp.float32
            ),
            jnp.einsum(
                "tmshwr,tmshwc->trc", grad_narrow, earlier, preferred_element_type=jnp.float32
            ),
        ],
        axis=-1,
    )
    grad_joined = jnp.einsum(
        "tmshwr,trc->tmshwc", grad_narrow, squeeze, preferred_element_type=jnp.float32
    )
    grad_first_out = (
        columns_back(
            jnp.einsum(
                "mshwo,ok->mshwk", grad_second, second_conv, preferred_element_type=jnp.float32
            ),
            channels,
        )
        + jnp.sum(grad_joined[..., :channels], axis=0)
    )
    grad_earlier = grad_joined[..., channels:]
    first_active = affine_rows(first_normed, norm_gain[0], norm_shift[0])
    grad_first_act = grad_first_out * silu_slope(first_active)
    first_sums = summed_members([gradient_sums(grad_first_act, first_normed, pixel_weight)])[0]
    grad_first = norm_backward(
        grad_first_act, first_normed, first_inverse, norm_gain[0], first_sums, counted, pixel_weight
    ).astype(jnp.bfloat16)
    input_columns = patch_columns(frames[0])
    first_conv_grad = jnp.einsum(
        "mshwo,mshwk->ok", grad_first, input_columns, preferred_element_type=jnp.float32
    )
    grad_shared_in = (
        columns_back(
            jnp.einsum("mshwo,ok->mshwk", grad_first, first_conv, preferred_element_type=jnp.float32),
            channels,
        )

    )
    grad_frames = jnp.concatenate([grad_shared_in[None], grad_earlier], axis=0)
    first_norm, second_norm, mask_norm, task_norm, narrow_norm = (
        jnp.sum(sums, axis=-3)
        for sums in (first_sums, second_sums, mask_sums, task_sums, narrow_sums)
    )
    norm_rows = jnp.concatenate(
        [first_norm[None], second_norm[None], mask_norm, task_norm], axis=0
    )
    weight_terms = (first_conv_grad, second_conv_grad, squeeze_grad, expand_grad, task_conv_grad)
    norm_terms = (norm_rows[:, 1], norm_rows[:, 0], narrow_norm[:, 1], narrow_norm[:, 0])
    return (grad_frames, weight_terms, norm_terms, square_all)


def shards(
    stream_in,
    image_count,
    out_grad,
    first_conv,
    second_conv,
    squeeze,
    expand,
    task_conv,
    norm_gain,
    norm_shift,
    squeeze_gain,
    squeeze_shift,
):
    weights = (
        first_conv[0],
        second_conv[0],
        squeeze[0],
        expand[0],
        task_conv[0],
        norm_gain[0],
        norm_shift[0],
        squeeze_gain[0],
        squeeze_shift[0],
    )
    maps_count, images, height, breadth, channels = stream_in.shape
    micro_count = image_count.shape[1]
    slot_count = images // micro_count
    leading_section = lax.axis_index("section") == 0
    live = jnp.arange(slot_count)[None, :] < image_count[0][:, None]
    pixel_weight = live.astype(jnp.float32)[:, :, None, None, None]

    def by_micro(maps):
        return maps.reshape((maps_count, micro_count, slot_count) + maps.shape[2:])

    def whole_pool(pooled):
        masked = pooled * pixel_weight
        squares = jnp.sum(masked * masked, axis=(1, 2, 3, 4, 5))
        return masked.astype(jnp.bfloat16), jnp.broadcast_to(squares[:, None], (maps_count, channels))

    one_pooled, one_state = section_forward(by_micro(stream_in), pixel_weight, weights)
    one_features, one_squares = whole_pool(one_pooled)
    arrived = from_behind(one_features, "section", 1)
    two_pooled, two_state = section_forward(arrived, pixel_weight, weights)
    two_features, two_squares = whole_pool(two_pooled)
    two_upstream = by_micro(out_grad).astype(jnp.float32) * pixel_weight
    two_back = section_backward(two_upstream, two_state, pixel_weight, two_squares, weights)
    sendback = two_back[0].astype(jnp.bfloat16)
    returned = from_behind(sendback, "section", -1)
    one_upstream = returned.astype(jnp.float32) * pixel_weight
    one_back = section_backward(one_upstream, one_state, pixel_weight, one_squares, weights)

    half = ((0, 0),) * 3 + ((0, height // 4), (0, breadth // 4), (0, 0))
    full = ((0, 0),) * 3 + ((0, height // 2), (0, breadth // 2), (0, 0))
    feature_out = jnp.where(leading_section, one_features, jnp.pad(two_features, half))
    feature_out = feature_out.reshape((maps_count, images) + feature_out.shape[3:])
    recorded = lax.optimization_barrier(sendback).astype(jnp.float32)
    input_grad_out = jnp.where(leading_section, one_back[0], jnp.pad(recorded, full))
    input_grad_out = input_grad_out.reshape((maps_count, images) + input_grad_out.shape[3:])
    reduced = tuple(
        lax.psum_scatter(
            jnp.where(leading_section, one, two).reshape(-1).astype(jnp.bfloat16),
            "dp",
            scatter_dimension=0,
            tiled=True,
        ).astype(jnp.float32)
        for one, two in zip(one_back[1], two_back[1])
    )
    norm_sums = tuple(
        jnp.where(leading_section, one, two) for one, two in zip(one_back[2], two_back[2])
    )
    live_images = jnp.sum(one_state[1][:, 0]) / (height * breadth)
    feature_pixels = jnp.where(leading_section, height * breadth // 4, height * breadth // 16)
    root_square = jnp.sqrt(
        jnp.where(leading_section, one_back[3], two_back[3])[:, 0]
        / (live_images * feature_pixels * channels)
    )
    return (
        feature_out[None],
        input_grad_out[None],
        reduced[0][None],
        reduced[1][None],
        reduced[2][None],
        reduced[3][None],
        reduced[4][None],
        norm_sums[0][None],
        norm_sums[1][None],
        norm_sums[2][None],
        norm_sums[3][None],
        root_square[None],
    )


TAPS = 9
MESH = pl.DeviceIdType.MESH
FIRST, SECOND, MASK, TASK, NARROW = 0, 1, 2, 5, 8
NORMS = 11
(F_FIRST, F_SECOND, B_FIRST, F_NARROW, F_MASK, F_TASK, B_NARROW, B_TASK, B_MASK) = range(9)
GROUPS_OF_SUMS = 9
(
    P_FIRST, P_OWN, P_NARROW, P_HIDDEN, P_MASK, P_MASKED, P_TASK, P_TASKED, P_SUMMED, P_POOL,
    P_ATTENDED,
    P_START, P_STARTED, P_SUMS, P_BACK, P_MASK_START, P_MASK_SUMS, P_MASK_BACK, P_FIRST_START,
    P_FIRST_SUMS,
) = range(20)
KIND_CORE = (0, 0, 1, 1, 0)


def sigmoid(active):
    return 0.5 * jnp.tanh(0.5 * active) + 0.5


def silu_parts(active):
    sigmoid_of = sigmoid(active)
    return active * sigmoid_of, sigmoid_of * (1.0 + active * (1.0 - sigmoid_of))


def dot_nt(left, right):
    return lax.dot_general(
        left, right, (((1,), (1,)), ((), ())), preferred_element_type=jnp.float32
    )


def dot_nn(left, right):
    return lax.dot_general(
        left, right, (((1,), (0,)), ((), ())), preferred_element_type=jnp.float32
    )


def loop(count, body, start=0):
    lax.fori_loop(start, count, lambda i, _: (body(i), 0)[1], 0)


def main_kernel(plan, *refs):
    (
        count_ref, stream, cotangent, gain_in, shift_in, narrow_gain, narrow_shift,
        w1, w2, sq, ex, tc,
        o_out, ig_out, norm_out, total_out, a_one, a_two, d_one, d_two,
        r_first, r_second, r_squeeze, r_expand, r_task,
        w1s, w2s, sqs, exs, tcs, params, params_away, x_one, x_two, og_ref, sg_ref,
        pads_one, pads_two, xh_one, xh_two, aux_one, aux_two, share_one, share_two,
        p_one, p_two, ub_one, ub_two, ab_one, ab_two, nb_one, nb_two,
        ex_in, ex_away, turned_one, turned_two, ig_one, ig_two, o_two,
        norm_one, norm_two, masks_one, masks_two, inv_one, inv_two, osq_one, osq_two,
        dr, gp, gpad, rows, tot, counts, wide, tbuf, square_kept, slots_one, slots_three, slots_four,
        held, dbuf, cols, stage, stage_flat,
        w_load, w_away, p_recv, p_send, sync_send, sync_recv, f_send, f_recv, b_send, b_recv,
        a_send, a_recv, d_send, d_recv, out_send, out_recv, t_send, t_own, r_recv, load_sem,
    ) = refs
    lines, mates, tasks, c = plan["lines"], plan["mates"], plan["tasks"], plan["channels"]
    high, across, live = plan["high"], plan["across"], plan["live"]
    hc = c // 2
    acc = dr.at[0]
    stage_squeeze, stage_expand = stage_flat, stage_flat.at[:, pl.ds(0, c)]
    micro = masks_one.shape[0]
    section = lax.axis_index("section")
    other = 1 - section
    me = lax.axis_index("dp")
    z, j = me // mates, lax.rem(me, mates)
    unit = c // lines
    pieces = unit // mates
    task_rows = tasks * c // lines
    kinds = (
        (0, unit), (unit, unit), (2 * unit, task_rows), (2 * unit + task_rows, task_rows),
        (2 * unit + 2 * task_rows, task_rows),
    )
    mine = pl.ds(pl.multiple_of(section * hc, hc), hc)
    theirs = pl.ds(pl.multiple_of(other * hc, hc), hc)

    def plane_tasks(line):
        return (task_rows * line) // c, (task_rows * (line + 1) - 1) // c

    def plane_needs(line, task):
        first, last = plane_tasks(line)
        return (first <= task) & (task <= last)

    def mate(step):
        return z * mates + lax.rem(j + step, mates)

    def liner(step):
        return lax.rem(z + step, lines) * mates + j

    def remote(source, target, send, recv, to, device):
        return pltpu.make_async_remote_copy(
            src_ref=source, dst_ref=target, send_sem=send, recv_sem=recv,
            device_id=(to, device), device_id_type=MESH,
        )

    def got(some, recv):
        remote(some, some, sync_send.at[0, 0], recv, section, me).wait_recv()

    def sent(some, send):
        remote(some, some, send, sync_recv.at[0, 0], section, me).wait_send()

    def push(source, target, send, recv, to, device, own=None):
        same = (section == to) & (me == device)

        @pl.when(same)
        def _():
            pltpu.make_async_copy(source, target, recv if own is None else own).start()

        @pl.when(jnp.logical_not(same))
        def _():
            remote(source, target, send, recv, to, device).start()

    def pushed(some, send, to, device, own=None):
        same = (section == to) & (me == device)

        @pl.when(jnp.logical_not(same))
        def _():
            sent(some, send)

        if own is not None:

            @pl.when(same)
            def _():
                pltpu.make_async_copy(some, some, own).wait()

    def across_cores(source, target, send, recv):
        remote(source, target, send, recv, other, me).start()

    def sums_at(block, group):
        if group < 3:
            ref, at, count = slots_one, 3 * block + group, 2 if group + block == 0 else 1
        elif group < 7:
            ref, at, count = slots_three, 4 * block + group - 3, 3
        else:
            ref, at, count = slots_four, 2 * block + group - 7, 4
        return ref.at[at], count, GROUPS_OF_SUMS * block + group

    def sums_place(block, group, stage, digits):
        ref, count, _ = sums_at(block, group)
        return ref.at[stage, digits, pl.ds(0, count)]

    def sums_send(block, group, stage, digit, devices):
        at = sums_at(block, group)[2]
        here = sums_place(block, group, stage, digit)
        for device in devices:
            remote(
                here, here, sync_send.at[at, stage], sync_recv.at[at, stage], section, device
            ).start()

    def sums_got(block, group, stage, digits):
        ref, count, at = sums_at(block, group)
        got(sums_place(block, group, stage, pl.ds(0, digits - 1)), sync_recv.at[at, stage])
        summed = ref[stage, 0, pl.ds(0, count)]
        for digit in range(1, digits):
            summed = summed + ref[stage, digit, pl.ds(0, count)]
        return summed

    def sums_start(block, group):
        sums_send(block, group, 0, j, [mate(step) for step in range(1, mates)])

    def sums_mid(block, group):
        ref, count, _ = sums_at(block, group)
        ref[1, z, pl.ds(0, count)] = sums_got(block, group, 0, mates)
        sums_send(block, group, 1, z, [liner(step) for step in range(1, lines)])

    def sums_end(block, group):
        count = sums_at(block, group)[1]
        tot[pl.ds(0, count)] = sums_got(block, group, 1, lines)

    def sums_sent(block, group):
        at = sums_at(block, group)[2]
        for stage, digits in enumerate((mates, lines)):
            sent(
                sums_place(block, group, stage, pl.ds(0, digits - 1)), sync_send.at[at, stage]
            )

    half_rows = pl.ds(pl.multiple_of(section * hc, hc), hc)
    away_rows = pl.ds(pl.multiple_of(other * hc, hc), hc)
    third = 3 * c
    W_SQUEEZE, W_SECOND, W_EXPAND, W_TASK = 3, 4, 5, 6
    W_COUNT = W_TASK + tasks

    def weight_refs(index, block, which):
        if index < 3:
            lanes = pl.ds(index * third, third)
            return w1.at[which, lanes], w1s.at[block, :, lanes]
        if index >= W_TASK:
            return tc.at[index - W_TASK, which], tcs.at[block, index - W_TASK]
        source, target = {
            W_SQUEEZE: (sq, sqs), W_SECOND: (w2, w2s), W_EXPAND: (ex, exs),
        }[index]
        if index == W_SECOND:
            return source.at[which], target.at[block]
        return source.at[:, which], target.at[block]

    def load_weights(index):
        source, target = weight_refs(index, section, half_rows)
        pltpu.make_async_copy(source, target, w_load.at[section, index]).start()
        source, target = weight_refs(index, section, away_rows)
        across_cores(source, target, w_away.at[index], w_load.at[section, index])

    def weights_got(index, block):
        got(weight_refs(index, block, half_rows)[1], w_load.at[block, index])

    def make_block(b):
        leading = b == 0
        rows_high, rows_across, images = (
            (high, across, live) if leading else (high // 2, across // 2, 8)
        )
        per_row = images * rows_across
        n = rows_high * per_row
        wide_n = plan["wide"] if leading else 128
        pixels = float(rows_high * rows_across)
        half = per_row // 2
        pick = 0 if leading else 1
        (
            source, pads, xh, aux, share, p_act, ub, ab, nb, turned, ig,
            norm_sums, masks, inv, osq, a_ref, d_ref,
        ) = tuple(
            pair[pick]
            for pair in (
                (x_one, x_two), (pads_one, pads_two), (xh_one, xh_two), (aux_one, aux_two),
                (share_one, share_two), (p_one, p_two), (ub_one, ub_two), (ab_one, ab_two),
                (nb_one, nb_two),
                (turned_one, turned_two), (ig_one, ig_two), (norm_one, norm_two),
                (masks_one, masks_two), (inv_one, inv_two), (osq_one, osq_two),
                (a_one, a_two), (d_one, d_two),
            )
        )
        position = lax.rem(
            lax.broadcasted_iota(jnp.int32, (per_row, hc), 0), jnp.int32(rows_across)
        )
        even = lax.rem(position, jnp.int32(2)) == 0
        span = pl.ds(0, n)
        used = pl.ds(0, per_row)

        def each(body):
            for h in range(rows_high):
                body(h)

        def part(h):
            return pl.ds(h * per_row, per_row)

        def shifted(values):
            left = jnp.where(position >= 1, pltpu.roll(values, 1, 0), 0.0)
            right = jnp.where(position <= rows_across - 2, pltpu.roll(values, per_row - 1, 0), 0.0)
            return [v.astype(jnp.bfloat16) for v in (left, values, right)]

        def put_pad(pad, h, which, values):
            for side, v in enumerate(shifted(values)):
                lanes = side * c + which * hc
                lanes = lanes if isinstance(lanes, int) else pl.multiple_of(lanes, hc)
                pad[pl.ds((h + 1) * per_row, per_row), pl.ds(lanes, hc)] = v

        def trade_pad(k, index):
            for side in range(3):
                here = pads.at[
                    k, pl.ds(per_row, n), pl.ds(pl.multiple_of(side * c + section * hc, hc), hc)
                ]
                across_cores(here, here, f_send.at[b, index], f_recv.at[b, index])

        def pad_bytes():
            return pads.at[0, pl.ds(per_row, n), pl.ds(0, 3 * hc)]

        def conv_to(pad, weight, store_at, before=None):
            total_of = None
            for dy in range(3):
                if before is not None:
                    before(dy)
                one = dot_nt(
                    pad[pl.ds(dy * per_row, n), :], weight[:, pl.ds(dy * 3 * c, 3 * c)]
                )
                total_of = one if total_of is None else total_of + one
            store_at[...] = total_of

        def conv_back_half(which, weight, store_at):
            total_of = None
            for dy in range(3):
                taps = jnp.concatenate(
                    [
                        weight[
                            :, pl.ds(pl.multiple_of((dy * 3 + side) * c + which * hc, hc), hc)
                        ]
                        for side in range(3)
                    ],
                    axis=0,
                )
                one = dot_nn(gpad[pl.ds((2 - dy) * per_row, n), :], taps)
                total_of = one if total_of is None else total_of + one
            store_at[...] = total_of

        def write_stats(group, member, first, second):
            ref = sums_at(b, group)[0]
            for k in range(micro):
                weight = masks[k]
                ref[0, j, member, pl.ds(k, 1), :] = jnp.sum(first * weight, 0, keepdims=True)
                ref[0, j, member, pl.ds(micro + k, 1), :] = jnp.sum(
                    second * weight, 0, keepdims=True
                )

        def moments(group, member, values_ref):
            first = second = None
            for h in range(rows_high):
                v = values_ref[pl.ds(h * per_row, per_row), :]
                first = v if h == 0 else first + v
                second = v * v if h == 0 else second + v * v
            write_stats(group, member, first, second)

        def start(group):
            sums_start(b, group)

        def mid(group):
            sums_mid(b, group)

        def end(group):
            sums_end(b, group)

        def row(ref, k):
            return ref[pl.ds(k, 1), :]

        def total(member, k):
            return tot[member, pl.ds(k, 1), :]

        def norm_rows(index, member):
            mean_rows = inv_rows = None
            for k in range(micro):
                n_k = row(counts, k) * pixels
                mean = total(member, k) / n_k
                spread_of = total(member, micro + k) / n_k - mean * mean
                inverse = lax.rsqrt(spread_of + EPSILON)
                inv[index, pl.ds(k, 1), :] = inverse
                weight = masks[k]
                mean_rows = weight * mean if k == 0 else mean_rows + weight * mean
                inv_rows = weight * inverse if k == 0 else inv_rows + weight * inverse
            rows[0, used, :] = mean_rows
            rows[1, used, :] = inv_rows

        def normalized(index, h, raw):
            normed = (raw - rows[0, used, :]) * rows[1, used, :]
            xh[index, part(h), :] = normed
            return normed * params[b, 0, index] + params[b, 1, index]

        def back_rows(index, member):
            norm_sums[index] = tot[member]
            scale_rows = shift_rows = slope_rows = None
            for k in range(micro):
                n_k = row(counts, k) * pixels
                weight = masks[k]
                scale = inv[index, pl.ds(k, 1), :] * params[b, 0, index]
                by_shift = total(member, k) / n_k
                by_gain = total(member, micro + k) / n_k
                scale_rows = weight * scale if k == 0 else scale_rows + weight * scale
                shift_rows = weight * by_shift if k == 0 else shift_rows + weight * by_shift
                slope_rows = weight * by_gain if k == 0 else slope_rows + weight * by_gain
            rows[0, used, :] = scale_rows
            rows[1, used, :] = shift_rows
            rows[2, used, :] = slope_rows

        def partner(v):
            return jnp.where(even, pltpu.roll(v, per_row - 1, 0), pltpu.roll(v, 1, 0))

        def soft_pool(index, read):
            squares = None
            for pair in range(rows_high // 2):
                upper, lower = read(2 * pair), read(2 * pair + 1)
                top = jnp.maximum(upper, lower)
                top = jnp.maximum(top, partner(top))
                upper, lower = jnp.exp(upper - top), jnp.exp(lower - top)
                summed = upper + lower
                summed = summed + partner(summed)
                share[index, pl.ds(2 * pair * per_row, per_row), :] = upper / summed
                share[index, pl.ds((2 * pair + 1) * per_row, per_row), :] = lower / summed
                pooled = top + jnp.log(summed * 0.25)
                for lane in range(hc // 128):
                    wide[lane, used, :] = pooled[:, lane * 128 : (lane + 1) * 128]
                pooled = jnp.concatenate(
                    [wide[lane, pl.ds(0, half, stride=2), :] for lane in range(hc // 128)], axis=1
                )
                if leading:
                    kept = pooled
                    pooled = jnp.concatenate(
                        [pooled, jnp.zeros((32 - half, hc), jnp.float32)], axis=0
                    )
                    x_two[section, index, pl.ds(32 * pair, 32), :] = pooled.astype(jnp.bfloat16)
                else:
                    alive = lax.broadcasted_iota(jnp.int32, (half, hc), 0) < live * (
                        rows_across // 2
                    )
                    kept = jnp.where(alive, pooled, 0.0)
                    o_two[index, pl.ds(half * pair, half), :] = kept.astype(jnp.bfloat16)
                square = jnp.sum(kept * kept, 0, keepdims=True)
                squares = square if squares is None else squares + square
            osq[index] = squares
            if leading:
                across_cores(
                    x_two.at[section, index], x_two.at[section, index],
                    f_send.at[b, 7 + index], f_recv.at[b, 7 + index],
                )

        def widened(index, pair):
            if leading:
                upstream = sg_ref[index, pl.ds(pl.multiple_of(32 * pair, 32), 32), :]
                upstream = upstream.astype(jnp.float32)[:half]
            else:
                upstream = og_ref[index]
            for lane in range(hc // 128):
                piece = upstream[:, lane * 128 : (lane + 1) * 128]
                wide[lane, pl.ds(0, half, stride=2), :] = piece
                wide[lane, pl.ds(1, half, stride=2), :] = piece
            return jnp.concatenate(
                [wide[lane, used, :] for lane in range(hc // 128)], axis=1
            )

        pair_at = 2 * (z // 2)
        far_at = lines - 2 - pair_at
        inner = (z == 1) | (z == 2)

        def send_shared(which):
            from_ref = source.at[section, 0] if which == 0 else ub.at[span]
            neighbour = 2 * pair_at + 1 - z
            for at, plane in enumerate((z, neighbour)):
                push(
                    from_ref, a_ref.at[which, section, z], a_send.at[b, which, at],
                    a_recv.at[b, which, 0], 0, plane * mates + j,
                )

        def pair_lines(which, first):
            return a_ref.at[which, :, pl.ds(first, 2)]

        def relay_pair(which):
            got(pair_lines(which, 0), a_recv.at[b, which, 0])

            @pl.when(inner)
            def _():
                here = pair_lines(which, pair_at)
                remote(
                    here, here, a_send.at[b, which, 2], a_recv.at[b, which, 1], 0,
                    (lines - 1 - z) * mates + j,
                ).start()

        def relay_far(which):
            @pl.when(inner)
            def _():
                got(pair_lines(which, 0), a_recv.at[b, which, 1])
                here = pair_lines(which, far_at)
                remote(
                    here, here, a_send.at[b, which, 3], a_recv.at[b, which, 1], 0,
                    (2 * pair_at + 1 - z) * mates + j,
                ).start()

        def shared_got(which):
            @pl.when(jnp.logical_not(inner))
            def _():
                got(pair_lines(which, 0), a_recv.at[b, which, 1])

        def task_planes(task):
            first = (c * task) // task_rows
            return first, first + 1

        def task_slot(kind, task, plane):
            return 2 + 2 * kind + task - plane_tasks(plane)[0]

        def task_core(kind):
            return 0 if kind == 0 else 1

        def task_source(kind, task):
            return (
                source.at[section, 1 + task] if kind == 0
                else ab.at[task, section] if kind == 1 else nb.at[task]
            )

        def send_task(kind, task):
            first, last = task_planes(task)
            near = jnp.clip(z, first, last)
            passed_on = (z < first) | (z > last)
            tensor = 2 + tasks * kind + task
            push(
                task_source(kind, task), a_ref.at[task_slot(kind, task, near), section, z],
                a_send.at[b, tensor, 0],
                a_recv.at[b, tensor, jnp.where(passed_on, jnp.int32(0), jnp.int32(1))],
                task_core(kind), near * mates + j,
            )

            @pl.when(jnp.logical_not(passed_on))
            def _():
                opposite = first + last - z
                push(
                    task_source(kind, task),
                    a_ref.at[task_slot(kind, task, opposite), section, z],
                    a_send.at[b, tensor, 1], a_recv.at[b, tensor, 1], task_core(kind),
                    opposite * mates + j,
                )

        def task_passes(kind, task):
            first, last = task_planes(task)
            passes = []
            if first > 0:
                passes.append((first, 0, first, last))
            if last < lines - 1:
                passes.append((last, last + 1, lines - 1 - last, first))
            return passes

        def relay_task(kind, task):
            tensor = 2 + tasks * kind + task
            for plane, first, count, to_plane in task_passes(kind, task):

                @pl.when(z == plane)
                def _():
                    some = pl.ds(first, count)
                    here = a_ref.at[task_slot(kind, task, plane), :, some]
                    got(here, a_recv.at[b, tensor, 0])
                    remote(
                        here, a_ref.at[task_slot(kind, task, to_plane), :, some],
                        a_send.at[b, tensor, 2], a_recv.at[b, tensor, 1], task_core(kind),
                        to_plane * mates + j,
                    ).start()

        def task_got(kind, task):
            tensor = 2 + tasks * kind + task
            first, last = task_planes(task)
            for plane, count in ((first, lines - first), (last, last + 1)):

                @pl.when(z == plane)
                def _():
                    got(a_ref.at[0, :, pl.ds(0, count)], a_recv.at[b, tensor, 1])

        def gather_sent():
            one_piece = ub.at[span]
            for which in range(2):
                for at, plane in enumerate((z, 2 * pair_at + 1 - z)):
                    pushed(one_piece, a_send.at[b, which, at], 0, plane * mates + j)

                @pl.when(inner & (section == 0))
                def _():
                    for at in (2, 3):
                        sent(pair_lines(which, 0), a_send.at[b, which, at])

            for kind in range(3):
                for task in range(tasks):
                    first, last = task_planes(task)
                    tensor = 2 + tasks * kind + task
                    near = jnp.clip(z, first, last)
                    pushed(
                        one_piece, a_send.at[b, tensor, 0], task_core(kind), near * mates + j
                    )

                    @pl.when((z == first) | (z == last))
                    def _():
                        pushed(
                            one_piece, a_send.at[b, tensor, 1], task_core(kind),
                            (first + last - z) * mates + j,
                        )

                    for plane, _, count, _ in task_passes(kind, task):

                        @pl.when((z == plane) & (section == task_core(kind)))
                        def _():
                            sent(a_ref.at[0, :, pl.ds(0, count)], a_send.at[b, tensor, 2])

        def spread_place(kind, task, k):
            offset, _ = kinds[kind]
            if kind < 2:
                return kind, 2 * section + k, offset
            number = lines * task + 2 * section + k
            at = pl.multiple_of(offset + lax.rem(number, tasks) * unit, unit)
            return 2 + tasks * (kind - 2) + task, number // tasks, at

        def spread(kind, task=0):
            for k in range(2):
                index, plane, offset = spread_place(kind, task, k)
                push(
                    turned.at[index, pl.ds(k * unit, unit)],
                    d_ref.at[z, pl.ds(offset, unit)],
                    d_send.at[b, index, k], d_recv.at[b, kind],
                    KIND_CORE[kind], plane * mates + j,
                )

        def spread_sent(kind, task=0):
            for k in range(2):
                index, plane, _ = spread_place(kind, task, k)
                pushed(
                    turned.at[index, pl.ds(k * unit, unit)], d_send.at[b, index, k],
                    KIND_CORE[kind], plane * mates + j,
                )

        def spread_got(kind):
            offset, count = kinds[kind]
            got(d_ref.at[:, pl.ds(offset, count)], d_recv.at[b, kind])

        def rounded(index, member, slot, turned_at):
            back_rows(index, member)

            def body(h):
                value = rows[0, used, :] * (
                    dr[slot, part(h), :] - rows[1, used, :] - xh[index, part(h), :] * rows[2, used, :]
                )
                tbuf[part(h), :] = value
                for side, v in enumerate(reversed(shifted(value))):
                    gpad[pl.ds((h + 1) * per_row, per_row), pl.ds(side * hc, hc)] = v

            each(body)
            turned[turned_at] = jnp.transpose(tbuf[pl.ds(0, wide_n), :]).astype(jnp.bfloat16)

        def middle():
            return gpad[pl.ds(per_row, n), pl.ds(hc, hc)]

        def give(index):
            across_cores(
                ex_away.at[index, span], ex_in.at[index, span], b_send.at[b, index], b_recv.at[b, index]
            )

        def taken(index):
            got(ex_in.at[index, span], b_recv.at[b, index])

        def center(k, lanes):
            return pads[k, pl.ds(per_row, n), lanes]

        own_center = pl.ds(pl.multiple_of(c + section * hc, hc), hc)
        other_center = pl.ds(pl.multiple_of(c + other * hc, hc), hc)

        def forward_start():
            if not leading:
                got(x_two.at[0, 0], f_recv.at[0, 7])

            def first_pad(h):
                for which in range(2):
                    put_pad(
                        pads.at[1], h, which, source[which, 0, part(h), :].astype(jnp.float32)
                    )

            each(first_pad)
            if leading:
                conv_to(
                    pads.at[1], w1s.at[b], xh.at[FIRST],
                    lambda dy: got(w1s.at[b, :, pl.ds(0, third)], w_load.at[b, dy]),
                )
            else:
                for dy in range(3):
                    got(w1s.at[b, :, pl.ds(0, third)], w_load.at[b, dy])
                conv_to(pads.at[1], w1s.at[b], xh.at[FIRST])
            moments(F_FIRST, 0, xh.at[FIRST])
            start(F_FIRST)

        def forward(pump):
            if leading:
                load_weights(W_SECOND)
            else:
                for index in range(1, 1 + tasks):
                    got(x_two.at[0, index], f_recv.at[0, 7 + index])
            weights_got(W_SQUEEZE, b)

            def outer_narrow(task):
                xh[NARROW + task] = dot_nt(
                    source[0, 1 + task], sqs[b, task, :, pl.ds(c, hc)]
                ) + dot_nt(source[1, 1 + task], sqs[b, task, :, pl.ds(c + hc, hc)])

            loop(tasks, outer_narrow)
            if leading:
                mid(F_FIRST)
            pump(P_FIRST, 0)
            end(F_FIRST)
            if leading:
                counts[...] = tot[1]
                got(params.at[0], p_recv.at[other])
            norm_rows(FIRST, 0)

            def first_act(h):
                active, slope = silu_parts(normalized(FIRST, h, xh[FIRST, part(h), :]))
                aux[FIRST, part(h), :] = slope
                ub[part(h), :] = active.astype(jnp.bfloat16)
                put_pad(pads.at[0], h, section, active)

            each(first_act)
            trade_pad(0, 0)
            if leading:
                load_weights(W_EXPAND)

            def narrow_own(task):
                pump(P_OWN, task)
                xh[NARROW + task] += dot_nt(center(0, own_center), sqs[b, task, :, mine])

            loop(tasks, narrow_own)
            got(pad_bytes(), f_recv.at[b, 0])

            def narrow(task):
                xh[NARROW + task] += dot_nt(center(0, other_center), sqs[b, task, :, theirs])
                moments(F_NARROW, task, xh.at[NARROW + task])

            loop(tasks, narrow)
            start(F_NARROW)
            if leading:
                load_weights(W_TASK)
            weights_got(W_SECOND, b)
            conv_to(pads.at[0], w2s.at[b], acc.at[span])
            mid(F_NARROW)
            moments(F_SECOND, 0, acc)
            start(F_SECOND)
            pump(P_NARROW, 0)
            weights_got(W_EXPAND, b)
            end(F_NARROW)

            def hidden(task):
                norm_rows(NARROW + task, task)

                def act(h):
                    active, slope = silu_parts(
                        normalized(NARROW + task, h, xh[NARROW + task, part(h), :])
                    )
                    aux[NARROW + task, part(h), :] = slope
                    ab[task, section, part(h), :] = active.astype(jnp.bfloat16)

                each(act)
                across_cores(
                    ab.at[task, section], ab.at[task, section],
                    f_send.at[b, 1 + task], f_recv.at[b, 1 + task],
                )
                pump(P_HIDDEN, task)

            loop(tasks, hidden)
            mid(F_SECOND)
            if leading:
                load_weights(W_TASK + 1)

            def mask_own(task):
                xh[MASK + task] = dot_nt(ab[task, section], exs[b, task, :, mine])

            loop(tasks, mask_own)

            def mask_of(task):
                got(ab.at[task, 0], f_recv.at[b, 1 + task])
                xh[MASK + task] += dot_nt(ab[task, other], exs[b, task, :, theirs])
                moments(F_MASK, task, xh.at[MASK + task])

            loop(tasks, mask_of)
            start(F_MASK)
            pump(P_MASK, 0)
            if leading:
                for index in range(W_TASK + 2, W_COUNT):
                    load_weights(index)
            end(F_SECOND)
            norm_rows(SECOND, 0)

            def second_act(h):
                active, slope = silu_parts(normalized(SECOND, h, acc[part(h), :]))
                aux[SECOND, part(h), :] = slope
                p_act[part(h), :] = active

            each(second_act)
            mid(F_MASK)
            pump(P_MASKED, 0)
            soft_pool(0, lambda h: p_act[pl.ds(h * per_row, per_row), :])
            end(F_MASK)

            def attend(task):
                norm_rows(MASK + task, task)
                pad = pads.at[1 + task]

                def act(h):
                    active = normalized(MASK + task, h, xh[MASK + task, part(h), :])
                    sigmoid_of = sigmoid(active)
                    aux[MASK + task, part(h), :] = sigmoid_of
                    attended = sigmoid_of * p_act[part(h), :]
                    nb[task, part(h), :] = attended.astype(jnp.bfloat16)
                    put_pad(pad, h, section, attended)

                each(act)
                trade_pad(1 + task, 4 + task)

            loop(tasks, attend)
            pump(P_ATTENDED, 0)

            def task_conv(task):
                got(tcs.at[b, 0], w_load.at[b, W_TASK + task])
                got(pad_bytes(), f_recv.at[b, 4 + task])
                conv_to(pads.at[1 + task], tcs.at[b, task], xh.at[TASK + task])
                moments(F_TASK, task, xh.at[TASK + task])
                pump(P_TASK, task)

            loop(tasks, task_conv)
            start(F_TASK)
            pump(P_TASKED, 0)
            mid(F_TASK)
            pump(P_SUMMED, 0)
            end(F_TASK)

            def task_pool(task):
                norm_rows(TASK + task, task)

                def act(h):
                    active, slope = silu_parts(
                        normalized(TASK + task, h, xh[TASK + task, part(h), :])
                    )
                    aux[TASK + task, part(h), :] = slope
                    acc[part(h), :] = active

                each(act)
                soft_pool(1 + task, lambda h: acc[pl.ds(h * per_row, per_row), :])
                pump(P_POOL, task)

            loop(tasks, task_pool)
            squares = sums_at(b, B_TASK)[0]
            squares[0, j, tasks] = jnp.zeros((8, hc), jnp.float32)
            for index in range(1 + tasks):
                squares[0, j, tasks, pl.ds(index, 1), :] = osq[index]

        DU, DE, DX = 2 * tasks, 2 * tasks + 1, 3 * tasks + 1

        def backward_start(pump):
            def task_start(task):
                first = second = None
                for pair in range(rows_high // 2):
                    upstream = widened(1 + task, pair)
                    for h in (2 * pair, 2 * pair + 1):
                        at = pl.ds(h * per_row, per_row)
                        up = upstream * share[1 + task, at, :] * aux[TASK + task, at, :]
                        dr[task, at, :] = up
                        by = up * xh[TASK + task, at, :]
                        first = up if first is None else first + up
                        second = by if second is None else second + by
                write_stats(B_TASK, task, first, second)
                pump(P_START, task)

            loop(tasks, task_start)
            start(B_TASK)

        def backward(pump):
            if not leading:
                mid(B_TASK)
            pump(P_SUMS, 0)
            end(B_TASK)
            square_kept[b] = tot[tasks]

            def task_back(task):
                rounded(TASK + task, task, task, 2 + task)
                spread(2, task)
                conv_back_half(other, tcs.at[b, task], ex_away.at[task, span])
                give(task)
                conv_back_half(section, tcs.at[b, task], dr.at[task, span])
                pump(P_BACK, task)

            loop(tasks, task_back)

            def task_through(task):
                taken(task)
                first = second = None
                for h in range(rows_high):
                    at = pl.ds(h * per_row, per_row)
                    grad = dr[task, at, :] + ex_in[task, at, :]
                    m, p = aux[MASK + task, at, :], p_act[at, :]
                    through = grad * m

                    @pl.when(task == 0)
                    def _():
                        gp[at, :] = through

                    @pl.when(task > 0)
                    def _():
                        gp[at, :] += through

                    up = through * p * (1.0 - m)
                    dr[task, at, :] = up
                    by = up * xh[MASK + task, at, :]
                    first = up if first is None else first + up
                    second = by if second is None else second + by
                write_stats(B_MASK, task, first, second)

            loop(tasks, task_through)
            first = second = None
            for pair in range(rows_high // 2):
                upstream = widened(0, pair)
                for h in (2 * pair, 2 * pair + 1):
                    at = pl.ds(h * per_row, per_row)
                    up = (gp[at, :] + upstream * share[0, at, :]) * aux[SECOND, at, :]
                    dr[3, at, :] = up
                    by = up * xh[SECOND, at, :]
                    first = up if first is None else first + up
                    second = by if second is None else second + by
            write_stats(B_MASK, tasks, first, second)
            start(B_MASK)
            pump(P_MASK_START, 0)
            mid(B_MASK)
            pump(P_MASK_SUMS, 0)
            end(B_MASK)

            def mask_back(task):
                rounded(MASK + task, task, task, 5 + task)
                spread(3, task)
                ex_away[tasks + task, span] = dot_nn(middle(), exs[b, task, :, theirs])
                give(tasks + task)
                dr[task, span] = dot_nn(middle(), exs[b, task, :, mine])
                pump(P_MASK_BACK, task)

            loop(tasks, mask_back)
            rounded(SECOND, tasks, 3, 1)
            spread(1)

            def mask_through(task):
                taken(tasks + task)
                first = second = None
                for h in range(rows_high):
                    at = pl.ds(h * per_row, per_row)
                    up = (dr[task, at, :] + ex_in[tasks + task, at, :]) * aux[
                        NARROW + task, at, :
                    ]
                    dr[task, at, :] = up
                    by = up * xh[NARROW + task, at, :]
                    first = up if first is None else first + up
                    second = by if second is None else second + by
                write_stats(B_NARROW, task, first, second)

            loop(tasks, mask_through)
            start(B_NARROW)
            conv_back_half(other, w2s.at[b], ex_away.at[DU, span])
            mid(B_NARROW)
            conv_back_half(section, w2s.at[b], gp.at[span])
            end(B_NARROW)

            def narrow_back(task):
                rounded(NARROW + task, task, task, 8 + task)
                spread(4, task)
                low = middle()
                ex_away[DU, span] += dot_nn(low, sqs[b, task, :, theirs])
                ex_away[DE + task, span] = dot_nn(
                    low, sqs[b, task, :, pl.ds(pl.multiple_of(c + other * hc, hc), hc)]
                )
                give(DE + task)
                gp[span, :] += dot_nn(low, sqs[b, task, :, mine])
                ig[1 + task] = dot_nn(
                    low, sqs[b, task, :, pl.ds(pl.multiple_of(c + section * hc, hc), hc)]
                )

            loop(tasks, narrow_back)
            give(DU)

            def outer_grad(index, slot):
                taken(slot)
                grad = ig[index] + ex_in[slot, span]
                if leading:
                    ig[index] = grad
                else:
                    low = grad.astype(jnp.bfloat16)
                    sg_ref[index] = low
                    ig[index] = low.astype(jnp.float32)
                push(
                    ig.at[index], ig_out.at[section, index, span], out_send.at[b, index],
                    out_recv.at[0], b, me,
                )

            loop(tasks, lambda t: outer_grad(1 + t, DE + t))
            taken(DU)
            first = second = None
            for h in range(rows_high):
                at = pl.ds(h * per_row, per_row)
                up = (gp[at, :] + ex_in[DU, at, :]) * aux[FIRST, at, :]
                dr[3, at, :] = up
                by = up * xh[FIRST, at, :]
                first = up if first is None else first + up
                second = by if second is None else second + by
            write_stats(B_FIRST, 0, first, second)
            start(B_FIRST)
            pump(P_FIRST_START, 0)
            mid(B_FIRST)
            pump(P_FIRST_SUMS, 0)
            end(B_FIRST)
            rounded(FIRST, 0, 3, 0)
            spread(0)
            conv_back_half(other, w1s.at[b], ex_away.at[DX, span])
            give(DX)
            conv_back_half(section, w1s.at[b], ig.at[0])
            outer_grad(0, DX)
            push(
                norm_sums, norm_out.at[section], out_send.at[b, 4], out_recv.at[1], b, me
            )
            push(
                square_kept.at[b], total_out.at[section, 1], out_send.at[b, 5],
                out_recv.at[2], b, me,
            )
            push(counts, total_out.at[section, 0], out_send.at[b, 6], out_recv.at[2], b, me)
            from_o = x_two.at[section] if leading else o_two
            count = 64 if leading else o_two.shape[1]
            push(
                from_o, o_out.at[section, :, pl.ds(0, count)], out_send.at[b, 7],
                out_recv.at[3], b, me,
            )

        def settle():
            gather_sent()
            for kind in range(2):
                spread_sent(kind)
            for kind in range(2, 5):
                for task in range(tasks):
                    spread_sent(kind, task)
            for index in range(1 + 2 * tasks):
                size = pad_bytes() if index == 0 or index > tasks else ab.at[0, 0]
                sent(size, f_send.at[b, index])
            if leading:
                for index in range(1 + tasks):
                    sent(x_two.at[0, 0], f_send.at[b, 7 + index])
            for group in range(GROUPS_OF_SUMS):
                sums_sent(b, group)
            for index in range(1 + tasks):
                pushed(ig.at[0], out_send.at[b, index], b, me)
            pushed(norm_sums, out_send.at[b, 4], b, me)
            pushed(counts, out_send.at[b, 5], b, me)
            pushed(counts, out_send.at[b, 6], b, me)
            pushed(x_two.at[0] if leading else o_two, out_send.at[b, 7], b, me)

        def exchanged():
            loop(NORMS, lambda index: sent(ex_away.at[0, span], b_send.at[b, index]))

        def results_got():
            got(ig_out.at[:, :, span], out_recv.at[0])
            got(norm_out, out_recv.at[1])
            got(total_out, out_recv.at[2])
            count = 64 if leading else o_two.shape[1]
            got(o_out.at[:, :, pl.ds(0, count)], out_recv.at[3])

        deep = lines * wide_n

        def fetch(from_ref, target, index):
            copy = pltpu.make_async_copy(from_ref, target, load_sem.at[index])
            copy.start()
            return copy

        def hold(at):
            return [
                fetch(
                    a_ref.at[at, which], held.at[:, span, pl.ds(which * hc, hc)], which
                )
                for which in range(2)
            ]

        def rows_held():
            return held[:, pl.ds(0, wide_n), :].reshape(deep, c)

        def slot_of(piece):
            return (task_rows * z + piece * unit) // c - plane_tasks(z)[0]

        def clear_tail():
            held[:, pl.ds(n, wide_n - n), :] = jnp.zeros((lines, wide_n - n, c), jnp.bfloat16)

        per_unit = task_rows // mates // pieces

        def piece_place(kind, piece, part):
            if kind < 2:
                return part, 0, (r_first, r_second)[kind], kind
            number = mates * piece + part
            return number // per_unit, number % per_unit, r_task, 2 + piece

        def conv_unit(kind, piece, buffer):
            offset, _ = kinds[kind]
            copies = hold(kind if kind < 2 else 2 + 2 * 2 + slot_of(piece))
            copies.append(
                fetch(
                    d_ref.at[:, pl.ds(offset + piece * unit, unit)],
                    dbuf.at[:, :, pl.ds(0, wide_n)], 2,
                )
            )
            for copy in copies:
                copy.wait()
            here = lax.rem(
                lax.broadcasted_iota(jnp.int32, (unit, wide_n), 1), jnp.int32(rows_across)
            )

            def side_terms(side):
                def line_cols(line):
                    value = dbuf[line, :, pl.ds(0, wide_n)].astype(jnp.float32)
                    if side == 0:
                        value = jnp.where(
                            here <= rows_across - 2, pltpu.roll(value, wide_n - 1, 1), 0.0
                        )
                    elif side == 2:
                        value = jnp.where(here >= 1, pltpu.roll(value, 1, 1), 0.0)
                    lanes = pl.ds(pl.multiple_of(line * wide_n, 128), wide_n)
                    for down in range(3):
                        shifted = value
                        if down == 0:
                            shifted = pltpu.roll(value, wide_n - per_row, 1)
                        elif down == 2:
                            shifted = pltpu.roll(value, per_row, 1)
                        cols[down, :, lanes] = shifted.astype(jnp.bfloat16)

                loop(lines, line_cols)

                def terms_of(down):
                    terms = dot_nn(cols[down, :, pl.ds(0, deep)], rows_held())
                    stage[buffer, :, pl.ds(pl.multiple_of((3 * down + side) * c, c), c)] = (
                        terms.astype(jnp.bfloat16)
                    )

                loop(3, terms_of)

            for side in range(3):
                side_terms(side)
            for part_at in range(mates):
                mate_at, at_row, target, index = piece_place(kind, piece, part_at)
                push(
                    stage.at[buffer, pl.ds(part_at * pieces, pieces)],
                    target.at[j, pl.ds(at_row * pieces, pieces)],
                    t_send.at[b, index, part_at], r_recv.at[index], b, z * mates + mate_at,
                    t_own.at[index, part_at],
                )

        def conv_unit_sent(kind, piece):
            for part_at in range(mates):
                mate_at, _, _, index = piece_place(kind, piece, part_at)
                pushed(
                    stage.at[0, pl.ds(0, pieces)], t_send.at[b, index, part_at], b,
                    z * mates + mate_at, t_own.at[index, part_at],
                )

        def flat_terms(kind, target, staged, index, parts):
            offset, _ = kinds[kind]
            copies = [
                fetch(
                    d_ref.at[line, pl.ds(offset + piece * unit, unit)],
                    cols.at[piece, :, pl.ds(line * wide_n, wide_n)], 3 + piece * lines + line,
                )
                for piece in range(tasks)
                for line in range(lines)
            ]
            for copy in copies:
                copy.wait()
            for at, a_kind in parts:
                if a_kind is None:
                    for copy in hold(1):
                        copy.wait()
                for piece in range(tasks):
                    if a_kind is not None:
                        for copy in hold(2 + 2 * a_kind + slot_of(piece)):
                            copy.wait()
                    terms = dot_nn(cols[piece, :, pl.ds(0, deep)], rows_held())
                    staged[pl.ds(piece * unit, unit), pl.ds(at, c)] = terms.astype(jnp.bfloat16)
            count = task_rows // mates
            for mate_at in range(mates):
                push(
                    staged.at[pl.ds(mate_at * count, count)], target.at[j],
                    t_send.at[b, index, mate_at], r_recv.at[index], b, z * mates + mate_at,
                    t_own.at[index, mate_at],
                )

        def flat_sent(staged, index):
            for mate_at in range(mates):
                pushed(
                    staged.at[pl.ds(0, task_rows // mates)], t_send.at[b, index, mate_at], b,
                    z * mates + mate_at, t_own.at[index, mate_at],
                )

        def free(name, waits):
            if name in in_use:
                in_use[name]()
            in_use[name] = waits

        def staged_conv(kind, piece, core):
            buffer = turn[core] % 2
            turn[core] += 1
            free((core, buffer), lambda: conv_unit_sent(kind, piece))
            conv_unit(kind, piece, buffer)

        def terms_second():
            spread_got(1)
            shared_got(1)
            staged_conv(1, 0, 0)

        def terms_first():
            spread_got(0)
            shared_got(0)
            staged_conv(0, 0, 0)

        def terms_squeeze():
            spread_got(4)
            for task in range(tasks):
                task_got(0, task)
            free((0, 2), lambda: flat_sent(stage_squeeze, 5))
            flat_terms(4, r_squeeze, stage_squeeze, 5, [(0, None), (c, 0)])

        def terms_expand():
            spread_got(3)
            for task in range(tasks):
                task_got(1, task)
            free((1, 2), lambda: flat_sent(stage_expand, 6))
            flat_terms(3, r_expand, stage_expand, 6, [(0, 1)])

        def terms_task(piece):
            if piece == 0:
                spread_got(2)
                for task in range(tasks):
                    task_got(2, task)
            staged_conv(2, piece, 1)

        def terms_got():
            def senders(kind):
                return pl.ds(0, mates - 1 if KIND_CORE[kind] == b else mates)

            for kind, index, target in (
                (0, 0, r_first), (1, 1, r_second), (4, 5, r_squeeze), (3, 6, r_expand)
            ):
                got(target.at[senders(kind)], r_recv.at[index])
            for piece in range(tasks):
                for mate_at in range(mates):
                    count = sum(
                        (mates * piece + part_at) // per_unit == mate_at
                        for part_at in range(mates)
                    )
                    if count:

                        @pl.when(j == mate_at)
                        def _():
                            some = r_task.at[senders(2), pl.ds(0, count * pieces)]
                            got(some, r_recv.at[2 + piece])

        def set_up():
            image = lax.div(
                lax.broadcasted_iota(jnp.int32, (per_row, hc), 0), jnp.int32(rows_across)
            )
            for k in range(micro):
                masks[k] = (
                    jnp.where(image == k, 1.0, 0.0)
                    + jnp.where(image == micro, fourth[k], 0.0)
                    + jnp.where(image == micro + 1, fifth[k], 0.0)
                )
            zero = jnp.zeros((per_row, 3 * c), jnp.bfloat16)
            for pad in range(1 + tasks):
                pads[pad, pl.ds(0, per_row), :] = zero
                pads[pad, pl.ds(n + per_row, per_row), :] = zero

        def back_set_up():
            zero = jnp.zeros((per_row, 3 * hc), jnp.bfloat16)
            gpad[pl.ds(0, per_row), :] = zero
            gpad[pl.ds(n + per_row, per_row), :] = zero
            tbuf[pl.ds(n, wide_n - n), :] = jnp.zeros((wide_n - n, hc), jnp.float32)

        return types.SimpleNamespace(
            forward_start=forward_start, forward=forward, backward_start=backward_start,
            backward=backward, settle=settle, exchanged=exchanged, results_got=results_got,
            mid=mid, set_up=set_up, back_set_up=back_set_up, clear_tail=clear_tail,
            second=terms_second, first=terms_first, squeeze=terms_squeeze, expand=terms_expand,
            task=terms_task, terms_got=terms_got, send_shared=send_shared, send_task=send_task,
            relay_pair=relay_pair, relay_far=relay_far, relay_task=relay_task,
        )

    barrier = pltpu.get_barrier_semaphore()
    greeted = (
        [(section, mate(step)) for step in range(1, mates)]
        + [(section, liner(step)) for step in range(1, lines)]
        + [(other, mate(step)) for step in range(mates)]
        + [(other, liner(step)) for step in range(1, lines)]
    )
    for device in greeted:
        pl.semaphore_signal(barrier, inc=1, device_id=device, device_id_type=MESH)
    numbers = [count_ref[0, k] for k in range(micro)]
    double = [jnp.where(number >= 2, jnp.float32(1.0), jnp.float32(0.0)) for number in numbers]
    fourth, fifth = [], []
    before = jnp.float32(0.0)
    for k in range(micro):
        fourth.append(double[k] * (1.0 - before))
        fifth.append(double[k] * before)
        before = before + double[k]
    count_slot = sums_at(0, F_FIRST)[0]
    count_slot[0, j, 1] = jnp.zeros((8, hc), jnp.float32)
    for k in range(micro):
        count_slot[0, j, 1, pl.ds(k, 1), :] = jnp.full((1, hc), 1.0) * (1.0 + double[k])
    for index in range(NORMS):
        at = pl.ds(index if index < NARROW else index - NARROW, 1)
        for which, (wider, narrower) in enumerate(
            ((gain_in, narrow_gain), (shift_in, narrow_shift))
        ):
            from_ref = wider if index < NARROW else narrower
            params[section, which, index] = from_ref[at, mine]
            params_away[which, index] = from_ref[at, theirs]
    pl.semaphore_wait(barrier, len(greeted))
    for index in range(W_SECOND):
        load_weights(index)
    across_cores(params_away, params.at[section], p_send.at[0], p_recv.at[section])
    in_use, turn = {}, [0, 0]
    one, two = make_block(0), make_block(1)

    def compact(index):
        for h in range(high):
            doubles = [
                stream[index, 2 * k + 1, h].astype(jnp.float32) for k in range(micro)
            ]
            rows_of = [stream[index, 2 * k, h].astype(jnp.float32) for k in range(micro)]
            for weight in (fourth, fifth):
                picked = doubles[0] * weight[0]
                for k in range(1, micro):
                    picked = picked + doubles[k] * weight[k]
                rows_of.append(picked)
            whole = jnp.concatenate(rows_of, axis=0).astype(jnp.bfloat16)
            at = pl.ds(h * live * across, live * across)
            for which in range(2):
                x_one[which, index, at, :] = whole[:, which * hc : (which + 1) * hc]

    one.set_up()
    loop(1 + tasks, compact)
    def on(core, *bodies):
        @pl.when(section == core)
        def _():
            for body in bodies:
                body()

    def cotangents():
        for index in range(1 + tasks):
            doubles = [cotangent[index, 2 * k + 1, 0].astype(jnp.float32) for k in range(micro)]
            rows_of = [cotangent[index, 2 * k, 0].astype(jnp.float32) for k in range(micro)]
            for weight in (fourth, fifth):
                picked = doubles[0] * weight[0]
                for k in range(1, micro):
                    picked = picked + doubles[k] * weight[k]
                rows_of.append(picked)
            og_ref[index] = jnp.zeros(og_ref.shape[1:], jnp.float32)
            for i, upstream in enumerate(rows_of):
                mine_of = jnp.where(section == 0, upstream[:, :hc], upstream[:, hc:])
                og_ref[index, pl.ds(i * (across // 4), across // 4), :] = mine_of

    def passes(block, kind):
        def run():
            for task in range(tasks):
                block.relay_task(kind, task)

        return run

    def one_forward(place, t):
        if place == P_FIRST:
            one.send_shared(0)
            two.set_up()
        elif place == P_HIDDEN:
            one.send_task(0, t)
        elif place == P_MASKED:
            on(0, lambda: one.relay_pair(0))
        elif place == P_ATTENDED:
            two.forward_start()
        elif place == P_TASKED:
            two.mid(F_FIRST)
            one.send_shared(1)
            on(0, lambda: one.relay_far(0))
        elif place == P_SUMMED:
            cotangents()
        elif place == P_POOL:
            one.send_task(1, t)

    def two_forward(place, t):
        if place == P_FIRST:
            on(0, lambda: one.relay_pair(1))
        elif place == P_NARROW:
            on(0, passes(one, 0))
        elif place == P_HIDDEN:
            one.send_task(2, t)
        elif place == P_MASK:
            on(0, lambda: one.relay_far(1))
            on(1, passes(one, 1))
        elif place == P_TASK:
            two.send_task(0, t)
        elif place == P_TASKED:
            on(1, passes(one, 2))
            two.back_set_up()
        elif place == P_SUMMED:
            two.send_shared(0)
        elif place == P_POOL:
            two.send_task(1, t)

    def two_backward(place, t):
        if place == P_SUMS:
            two.send_shared(1)
            on(0, lambda: two.relay_pair(0), passes(two, 0))
        elif place == P_BACK:
            two.send_task(2, t)
        elif place == P_MASK_START:
            on(0, lambda: two.relay_far(0), lambda: two.relay_pair(1))
            on(1, passes(two, 1))
        elif place == P_MASK_SUMS:
            on(0, lambda: two.relay_far(1))
        elif place == P_FIRST_START:
            one.backward_start(nothing)
        elif place == P_FIRST_SUMS:
            one.mid(B_TASK)
            on(1, passes(two, 2))

    def one_backward(place, t):
        if place == P_MASK_START:
            on(0, two.clear_tail, two.second)
            on(1, two.clear_tail, lambda: two.task(0))
        elif place == P_MASK_SUMS:
            on(0, two.squeeze)
            on(1, lambda: two.task(1))
        elif place == P_FIRST_START:
            on(0, two.first, one.clear_tail)
            on(1, lambda: two.task(2), two.expand, one.clear_tail)
        elif place == P_FIRST_SUMS:
            on(0, one.second)
            on(1, lambda: one.task(0))

    def nothing(place, t):
        pass

    one.forward_start()
    one.forward(one_forward)
    two.forward(two_forward)
    two.backward_start(two_backward)
    two.backward(two_backward)
    two.exchanged()
    one.back_set_up()
    one.backward(one_backward)
    on(0, one.squeeze, one.first)
    on(1, lambda: one.task(1), lambda: one.task(2), one.expand)
    for (core, _), waits in in_use.items():
        on(core, waits)
    one.exchanged()
    one.settle()
    two.settle()
    sent(params_away, p_send.at[0])
    for index in range(W_COUNT):
        sent(weight_refs(index, 0, away_rows)[1], w_away.at[index])
    on(0, one.results_got, one.terms_got)
    on(1, two.results_got, two.terms_got)


def result_kernel(plan, *refs):
    (
        count_ref, first, second, squeeze, expand, task, pooled, grads, norms, totals,
        first_out, second_out, squeeze_out, expand_out, task_out, feature_out, input_out,
        gain_out, shift_out, narrow_gain_out, narrow_shift_out, rms_out,
    ) = refs
    mates, tasks, c = plan["mates"], plan["tasks"], plan["channels"]
    section = lax.axis_index("section")
    live, micro = plan["live"], plan["micro"]
    images_of = []
    before = jnp.int32(micro)
    for k in range(micro):
        double = count_ref[0, k] >= 2
        images_of.append(jnp.where(double, before, jnp.int32(-1)))
        before = before + jnp.where(double, jnp.int32(1), jnp.int32(0))

    def joined(ref, index, at):
        return jnp.concatenate([ref[0, index, at, :], ref[1, index, at, :]], axis=1)

    def aligned(values, image, rows, used):
        start = image * rows
        values = pltpu.roll(values, values.shape[0] - start, 0) if start else values
        inside = lax.broadcasted_iota(jnp.int32, (8, c), 0) < used
        return jnp.where(inside, values[:8], 0.0)

    def by_slot(values, rows, used, store):
        two = [aligned(values, micro, rows, used), aligned(values, micro + 1, rows, used)]
        for k in range(micro):
            store(2 * k, aligned(values, k, rows, used))
            which = images_of[k]
            store(
                2 * k + 1,
                jnp.where(which == micro, two[0], jnp.where(which == micro + 1, two[1], 0.0)),
            )

    def place_out(high, across, images, leading):
        per_row = images * across
        for index in range(1 + tasks):
            for h in range(plan["high"]):

                def store(slot, values):
                    input_out[index, slot, h] = values

                if h < high:
                    at = pl.ds(h * per_row, per_row)
                    by_slot(joined(grads, index, at), across, across, store)
                else:
                    for slot in range(2 * micro):
                        store(slot, jnp.zeros((8, c), jnp.float32))
            for h in range(plan["high"] // 2):

                def store_feature(slot, values):
                    feature_out[index, slot, h] = values[: plan["across"] // 2].astype(
                        jnp.bfloat16
                    )

                if h < high // 2:
                    count = 8 * (across // 2)
                    by_slot(
                        joined(pooled, index, pl.ds(h * count, count)).astype(jnp.float32),
                        across // 2, across // 2, store_feature,
                    )
                else:
                    for slot in range(2 * micro):
                        store_feature(slot, jnp.zeros((8, c), jnp.float32))
        cells = float(high * across // 4 * c)
        live_total = jnp.sum(
            totals[0, 0, pl.ds(0, micro), pl.ds(0, 1)], axis=0, keepdims=True
        )
        lane = lax.broadcasted_iota(jnp.int32, (1, 1 + tasks), 1)
        result = jnp.zeros((1, 1 + tasks), jnp.float32)
        for index in range(1 + tasks):
            both_halves = totals[0, 1, pl.ds(index, 1), :] + totals[1, 1, pl.ds(index, 1), :]
            square = jnp.sum(both_halves, axis=1, keepdims=True)
            result = jnp.where(lane == index, jnp.sqrt(square / (live_total * cells)), result)
        rms_out[...] = result
        for index in range(NORMS):
            shift_sum = jnp.sum(
                joined(norms, index, pl.ds(0, micro)), axis=0, keepdims=True
            )
            gain_sum = jnp.sum(
                joined(norms, index, pl.ds(micro, micro)), axis=0, keepdims=True
            )
            if index < NARROW:
                gain_out[pl.ds(index, 1), :] = gain_sum
                shift_out[pl.ds(index, 1), :] = shift_sum
            else:
                narrow_gain_out[pl.ds(index - NARROW, 1), :] = gain_sum
                narrow_shift_out[pl.ds(index - NARROW, 1), :] = shift_sum

    @pl.when((pl.program_id(0) == 0) & (section == 0))
    def _():
        place_out(plan["high"], plan["across"], live, True)

    @pl.when((pl.program_id(0) == 0) & (section == 1))
    def _():
        place_out(plan["high"] // 2, plan["across"] // 2, 8, False)

    for terms, target in (
        (first, first_out), (second, second_out), (squeeze, squeeze_out),
        (expand, expand_out), (task, task_out),
    ):
        _, count, width = terms.shape
        per_row = width // 128
        for lane in range(per_row):
            at = pl.ds(lane * 128, 128)
            summed = terms[0, :, at].astype(jnp.float32)
            for place in range(1, mates):
                summed = summed + terms[place, :, at].astype(jnp.float32)
            target[pl.ds(lane, count, stride=per_row), :] = summed


def gathered_shards(
    stream_in, image_count, out_grad, first_conv, second_conv, squeeze, expand, task_conv,
    norm_gain, norm_shift, squeeze_gain, squeeze_shift,
):
    maps, images, high, across, c = stream_in.shape
    micro = image_count.shape[1]
    tasks = maps - 1
    groups = lax.axis_size("dp")
    mates = 4
    lines = groups // mates
    live = images - 2
    n = high * live * across
    wide_n = 256
    plan = {
        "lines": lines, "mates": mates, "tasks": tasks, "channels": c,
        "high": high, "across": across, "live": live, "wide": wide_n, "micro": micro,
    }
    conv_rows = c // groups
    task_rows = tasks * c // groups
    turned_rows = 2 * c + 3 * tasks * c
    bf16, f32 = jnp.bfloat16, jnp.float32
    vmem = pl.BlockSpec(memory_space=pltpu.VMEM)
    whole = pl.BlockSpec(memory_space=pl.ANY)
    shapes = (
        (conv_rows, TAPS * c), (conv_rows, TAPS * c), (task_rows, 2 * c), (task_rows, c),
        (task_rows, TAPS * c),
    )
    hc = c // 2
    small = 64
    out_shape = (
        [
            jax.ShapeDtypeStruct((2, maps, small, hc), bf16),
            jax.ShapeDtypeStruct((2, maps, n, hc), f32),
            jax.ShapeDtypeStruct((2, NORMS, 8, hc), f32),
            jax.ShapeDtypeStruct((2, 2, 8, hc), f32),
            jax.ShapeDtypeStruct((8, 2, lines, n, hc), bf16),
            jax.ShapeDtypeStruct((8, 2, lines, small, hc), bf16),
            jax.ShapeDtypeStruct((lines, turned_rows // lines, wide_n), bf16),
            jax.ShapeDtypeStruct((lines, turned_rows // lines, 128), bf16),
        ]
        + [jax.ShapeDtypeStruct((mates,) + shape, bf16) for shape in shapes]
    )
    row_one, row_two = live * across, 4 * across

    def pair(shape_of, dtype):
        return [pltpu.VMEM(shape_of(n), dtype), pltpu.VMEM(shape_of(small), dtype)]

    unit = c // lines
    scratch = (
        [
            pltpu.VMEM((2, hc, TAPS * c), bf16),
            pltpu.VMEM((2, hc, TAPS * c), bf16),
            pltpu.VMEM((2, tasks, hc, 2 * c), bf16),
            pltpu.VMEM((2, tasks, hc, c), bf16),
            pltpu.VMEM((2, tasks, hc, TAPS * c), bf16),
            pltpu.VMEM((2, 2, NORMS, 1, hc), f32),
            pltpu.VMEM((2, NORMS, 1, hc), f32),
            pltpu.VMEM((2, maps, n, hc), bf16),
            pltpu.VMEM((2, maps, small, hc), bf16),
            pltpu.VMEM((maps, 16, hc), f32),
            pltpu.VMEM((maps, small, hc), bf16),
            pltpu.VMEM((maps, (high + 2) * row_one, 3 * c), bf16),
            pltpu.VMEM((maps, (high // 2 + 2) * row_two, 3 * c), bf16),
        ]
        + pair(lambda rows: (NORMS, rows, hc), f32)
        + pair(lambda rows: (NORMS, rows, hc), f32)
        + pair(lambda rows: (maps, rows, hc), f32)
        + pair(lambda rows: (rows, hc), f32)
        + pair(lambda rows: (rows, hc), bf16)
        + pair(lambda rows: (tasks, 2, rows, hc), bf16)
        + pair(lambda rows: (tasks, rows, hc), bf16)
        + [pltpu.VMEM((NORMS, n, hc), f32), pltpu.VMEM((NORMS, n, hc), f32)]
        + [pltpu.VMEM((NORMS, hc, wide_n), bf16), pltpu.VMEM((NORMS, hc, 128), bf16)]
        + pair(lambda rows: (maps, rows, hc), f32)
        + [
            pltpu.VMEM((maps, 16, hc), bf16),
            pltpu.VMEM((NORMS, 8, hc), f32),
            pltpu.VMEM((NORMS, 8, hc), f32),
            pltpu.VMEM((micro, row_one, hc), f32),
            pltpu.VMEM((micro, row_two, hc), f32),
            pltpu.VMEM((NORMS, micro, hc), f32),
            pltpu.VMEM((NORMS, micro, hc), f32),
            pltpu.VMEM((maps, 1, hc), f32),
            pltpu.VMEM((maps, 1, hc), f32),
            pltpu.VMEM((4, n, hc), f32),
            pltpu.VMEM((n, hc), f32),
            pltpu.VMEM(((high + 2) * row_one, 3 * hc), bf16),
            pltpu.VMEM((3, row_one, hc), f32),
            pltpu.VMEM((4, 8, hc), f32),
            pltpu.VMEM((8, hc), f32),
            pltpu.VMEM((hc // 128, row_one, 128), f32),
            pltpu.VMEM((wide_n, hc), f32),
            pltpu.VMEM((2, 8, hc), f32),
            pltpu.VMEM((6, 2, 4, 2, 8, hc), f32),
            pltpu.VMEM((8, 2, 4, 3, 8, hc), f32),
            pltpu.VMEM((4, 2, 4, 4, 8, hc), f32),
            pltpu.VMEM((lines, wide_n, c), bf16),
            pltpu.VMEM((lines, unit, wide_n), bf16),
            pltpu.VMEM((3, unit, lines * wide_n), bf16),
            pltpu.VMEM((2, unit, TAPS * c), bf16),
            pltpu.VMEM((mates * task_rows, 2 * c), bf16),
        ]
        + [
            pltpu.SemaphoreType.DMA(shape)
            for shape in (
                (2, 6 + tasks), (6 + tasks,), (2,), (1,), (2 * GROUPS_OF_SUMS, 2),
                (2 * GROUPS_OF_SUMS, 2),
                (2, NORMS), (2, NORMS), (2, NORMS), (2, NORMS), (2, NORMS, lines), (2, NORMS, 2),
                (2, NORMS, 2), (2, 5), (2, 8), (4,), (2, 7, mates), (7, mates), (7,),
                (3 + tasks * lines,),
            )
        ]
    )
    results = pl.pallas_call(
        functools.partial(main_kernel, plan),
        out_shape=out_shape,
        in_specs=[pl.BlockSpec(memory_space=pltpu.SMEM)] + [vmem] * 6 + [whole] * 5,
        out_specs=[whole] * 13,
        scratch_shapes=scratch,
        compiler_params=pltpu.CompilerParams(
            collective_id=1, has_side_effects=True, vmem_limit_bytes=62 * 2**20
        ),
        name="blocks",
    )(
        image_count, stream_in, out_grad, norm_gain[0], norm_shift[0], squeeze_gain[0],
        squeeze_shift[0], first_conv[0], second_conv[0], squeeze[0], expand[0], task_conv[0],
    )
    pooled, grads, norms, totals = results[:4]
    terms = results[8:]
    steps = 2

    def flat(shape):
        return jax.ShapeDtypeStruct((shape[0] * shape[1] // 128, 128), f32)

    results = pl.pallas_call(
        functools.partial(result_kernel, plan),
        grid=(steps,),
        out_shape=[flat(shape) for shape in shapes]
        + [
            jax.ShapeDtypeStruct((maps, images, high // 2, across // 2, c), bf16),
            jax.ShapeDtypeStruct((maps, images, high, across, c), f32),
            jax.ShapeDtypeStruct((NARROW, c), f32),
            jax.ShapeDtypeStruct((NARROW, c), f32),
            jax.ShapeDtypeStruct((tasks, c), f32),
            jax.ShapeDtypeStruct((tasks, c), f32),
            jax.ShapeDtypeStruct((1, maps), f32),
        ],
        in_specs=[pl.BlockSpec(memory_space=pltpu.SMEM)]
        + [
            pl.BlockSpec((mates, shape[0] // steps, shape[1]), lambda i: (0, i, 0))
            for shape in shapes
        ]
        + [vmem] * 4,
        out_specs=[
            pl.BlockSpec((shape[0] // steps * shape[1] // 128, 128), lambda i: (i, 0))
            for shape in shapes
        ]
        + [vmem] * 7,
        compiler_params=pltpu.CompilerParams(vmem_limit_bytes=62 * 2**20),
        name="results",
    )(image_count, *terms, pooled, grads, norms, totals)
    first_g, second_g, squeeze_g, expand_g, task_g = (
        grad.reshape(1, -1) for grad in results[:5]
    )
    feature_out, input_out, gain_g, shift_g, narrow_gain_g, narrow_shift_g, rms = results[5:]
    return (
        feature_out[None], input_out[None], first_g, second_g, squeeze_g, expand_g, task_g,
        gain_g[None], shift_g[None], narrow_gain_g[None], narrow_shift_g[None], rms,
    )


def solution(mesh):
    groups = mesh.shape["dp"]
    whole_tiles = groups == 4 * 4
    return jax.shard_map(
        gathered_shards if whole_tiles else shards,
        mesh=mesh,
        in_specs=(
            P(None, "dp", None, None, None),
            P("dp", None),
            P(None, "dp", None, None, None),
            P("section", None, None),
            P("section", None, None),
            P("section", None, None, None),
            P("section", None, None, None),
            P("section", None, None, None),
            P("section", None, None),
            P("section", None, None),
            P("section", None, None),
            P("section", None, None),
        ),
        out_specs=(
            P("section", None, "dp", None, None, None),
            P("section", None, "dp", None, None, None),
            P("section", "dp"),
            P("section", "dp"),
            P("section", "dp"),
            P("section", "dp"),
            P("section", "dp"),
            P("section", None, None),
            P("section", None, None),
            P("section", None, None),
            P("section", None, None),
            P("section", None),
        ),
        check_vma=False,
    )
```

```python
import functools
import types

import jax
import jax.numpy as jnp
from jax import lax
from jax.experimental import pallas as pl
from jax.experimental.pallas import tpu as pltpu
from jax.sharding import PartitionSpec as P

EPSILON = 1e-05
SUM_ROWS = 40


def stages_of(size):
    stages = []
    stride = 1
    while stride < size:
        radix = next(r for r in (4, 2, 3, 5, 7, size // stride) if (size // stride) % r == 0)
        stages.append((radix, stride))
        stride *= radix
    return stages


def sum_kernel(stages, own_ref, out_ref, *scratch):
    slots, (send_sem, recv_sem) = scratch[: len(stages)], scratch[len(stages) :]
    section = lax.axis_index("section")
    me = lax.axis_index("dp")
    barrier = pltpu.get_barrier_semaphore()
    peers = []
    for radix, stride in stages:
        digit = lax.rem(me // stride, radix)
        group = [
            me + (lax.rem(digit + step, radix) - digit) * stride for step in range(1, radix)
        ]
        peers.append((digit, group))
    total = sum(len(group) for _, group in peers)
    for _, group in peers:
        for peer in group:
            pl.semaphore_signal(
                barrier, inc=1, device_id=(section, peer), device_id_type=pl.DeviceIdType.MESH
            )
    pl.semaphore_wait(barrier, total)
    for index, (radix, stride) in enumerate(stages):
        digit, group = peers[index]
        held = slots[index]
        held[digit] = own_ref[...] if index == 0 else out_ref[...]
        copies = []
        for step, peer in enumerate(group):
            copy = pltpu.make_async_remote_copy(
                src_ref=held.at[digit],
                dst_ref=held.at[digit],
                send_sem=send_sem.at[index, step],
                recv_sem=recv_sem.at[index, step],
                device_id=(section, peer),
                device_id_type=pl.DeviceIdType.MESH,
            )
            copy.start()
            copies.append(copy)
        for copy in copies:
            copy.wait_recv()
        summed = held[0]
        for place in range(1, radix):
            summed = summed + held[place]
        out_ref[...] = summed
        for copy in copies:
            copy.wait_send()


def sum_over_groups(rows):
    stages = stages_of(lax.axis_size("dp"))
    widest = max(radix for radix, _ in stages)
    return pl.pallas_call(
        functools.partial(sum_kernel, stages),
        out_shape=jax.ShapeDtypeStruct(rows.shape, jnp.float32),
        in_specs=[pl.BlockSpec(memory_space=pltpu.VMEM)],
        out_specs=pl.BlockSpec(memory_space=pltpu.VMEM),
        scratch_shapes=[pltpu.VMEM((radix,) + rows.shape, jnp.float32) for radix, _ in stages]
        + [
            pltpu.SemaphoreType.DMA((len(stages), widest)),
            pltpu.SemaphoreType.DMA((len(stages), widest)),
        ],
        compiler_params=pltpu.CompilerParams(collective_id=0, has_side_effects=True),
        name="group_sum",
    )(rows)


def from_behind(shard, axis, by):
    size = lax.axis_size(axis)
    pairs = [(i, i + by) for i in range(size) if 0 <= i + by < size]
    return lax.ppermute(shard, axis, pairs)


def broadcast_rows(vector):
    return vector[..., None, None, None, :]


def affine_rows(normed, scale_by, offset_by):
    return normed * broadcast_rows(scale_by) + broadcast_rows(offset_by)


def silu_slope(active):
    sigmoid_of = jax.nn.sigmoid(active)
    return sigmoid_of * (1.0 + active * (1.0 - sigmoid_of))


def pixel_sums(values, pixel_weight):
    weighted = values * pixel_weight
    return jnp.stack(
        [jnp.sum(weighted, axis=(-4, -3, -2)), jnp.sum(weighted * values, axis=(-4, -3, -2))],
        axis=-2,
    )


def gradient_sums(upstream, normed, pixel_weight):
    weighted = upstream * pixel_weight
    return jnp.stack(
        [jnp.sum(weighted, axis=(-4, -3, -2)), jnp.sum(weighted * normed, axis=(-4, -3, -2))],
        axis=-2,
    )


def summed_members(members):
    rows = [member.reshape(-1, member.shape[-1]) for member in members]
    used = sum(row.shape[0] for row in rows)
    packed = jnp.concatenate(
        rows + [jnp.zeros((SUM_ROWS - used, rows[0].shape[-1]), jnp.float32)], axis=0
    )
    summed = sum_over_groups(packed)
    results = []
    offset = 0
    for member, row in zip(members, rows):
        results.append(summed[offset : offset + row.shape[0]].reshape(member.shape))
        offset += row.shape[0]
    return results


def normalize(values, moments, counted):
    average = moments[..., 0, :] / counted
    spread = moments[..., 1, :] / counted - average * average
    inverse = lax.rsqrt(spread + EPSILON)
    return ((values - broadcast_rows(average)) * broadcast_rows(inverse), inverse)


def norm_backward(upstream, normed, inverse, scale_by, sums, counted, pixel_weight):
    shift_part = broadcast_rows(sums[..., 0, :])
    scale_part = broadcast_rows(sums[..., 1, :])
    return (
        broadcast_rows(inverse * scale_by)
        * (upstream - (shift_part + normed * scale_part) / broadcast_rows(counted))
        * pixel_weight
    )


def window_blocks(values):
    leading = values.shape[:-3]
    height, breadth, channels = values.shape[-3:]
    return values.reshape(leading + (height // 2, 2, breadth // 2, 2, channels))


def soft_pool_blocks(blocks):
    summit = jnp.max(blocks, axis=(-4, -2), keepdims=True)
    return summit + jnp.log(jnp.mean(jnp.exp(blocks - summit), axis=(-4, -2), keepdims=True))


def soft_pool(values):
    pooled = soft_pool_blocks(window_blocks(values))
    return pooled.reshape(
        values.shape[:-3] + (values.shape[-3] // 2, values.shape[-2] // 2, values.shape[-1])
    )


def pool_back(upstream, values):
    blocks = window_blocks(values)
    pooled = soft_pool_blocks(blocks)
    weight_share = jnp.exp(blocks - pooled) * 0.25
    spread = upstream.reshape(pooled.shape) * weight_share
    return spread.reshape(values.shape)


def patch_columns(frames):
    height, breadth = (frames.shape[-3], frames.shape[-2])
    padding = [(0, 0)] * (frames.ndim - 3) + [(1, 1), (1, 1), (0, 0)]
    padded = jnp.pad(frames, padding)
    return jnp.concatenate(
        [
            padded[..., down_shift : down_shift + height, side_shift : side_shift + breadth, :]
            for down_shift in range(3)
            for side_shift in range(3)
        ],
        axis=-1,
    )


def columns_back(grad_columns, channels):
    height, breadth = (grad_columns.shape[-3], grad_columns.shape[-2])
    leading = [(0, 0)] * (grad_columns.ndim - 3)
    summed = None
    for tap_index in range(9):
        down_shift, side_shift = (tap_index // 3, tap_index % 3)
        piece_of = grad_columns[..., tap_index * channels : (tap_index + 1) * channels]
        placed = jnp.pad(
            piece_of, leading + [(down_shift, 2 - down_shift), (side_shift, 2 - side_shift), (0, 0)]
        )
        summed = placed if summed is None else summed + placed
    return summed[..., 1 : height + 1, 1 : breadth + 1, :]


def live_rows(pixel_weight, channels):
    live = jnp.sum(pixel_weight, axis=(-4, -3, -2, -1))
    return jnp.broadcast_to(live[:, None], (live.shape[0], channels))


def section_forward(frames, pixel_weight, weights):
    (
        first_conv,
        second_conv,
        squeeze,
        expand,
        task_conv,
        norm_gain,
        norm_shift,
        squeeze_gain,
        squeeze_shift,
    ) = weights
    channels = frames.shape[-1]
    tasks = squeeze.shape[0]
    input_columns = patch_columns(frames[0])
    first_pre = jnp.einsum(
        "mshwk,ok->mshwo", input_columns, first_conv, preferred_element_type=jnp.float32
    )
    first_moments = summed_members(
        [pixel_sums(first_pre, pixel_weight), live_rows(pixel_weight, channels)]
    )
    counted = first_moments[1] * (frames.shape[-3] * frames.shape[-2])
    first_normed, first_inverse = normalize(first_pre, first_moments[0], counted)
    first_output = jax.nn.silu(affine_rows(first_normed, norm_gain[0], norm_shift[0]))
    rounded_first = (first_output).astype(jnp.bfloat16)
    middle_columns = patch_columns(rounded_first)
    second_pre = jnp.einsum(
        "mshwk,ok->mshwo", middle_columns, second_conv, preferred_element_type=jnp.float32
    )
    earlier = frames[1:]
    narrow = jnp.einsum(
        "mshwc,trc->tmshwr",
        rounded_first,
        squeeze[:, :, :channels],
        preferred_element_type=jnp.float32,
    ) + jnp.einsum(
        "tmshwc,trc->tmshwr", earlier, squeeze[:, :, channels:], preferred_element_type=jnp.float32
    )
    middle_moments = summed_members([pixel_sums(second_pre, pixel_weight), pixel_sums(narrow, pixel_weight)])
    second_normed, second_inverse = normalize(second_pre, middle_moments[0], counted)
    narrow_normed, narrow_inverse = normalize(narrow, middle_moments[1], counted)
    shared_out = jax.nn.silu(affine_rows(second_normed, norm_gain[1], norm_shift[1]))
    rounded_hidden = jax.nn.silu(affine_rows(narrow_normed, squeeze_gain[:, None], squeeze_shift[:, None])).astype(
        jnp.bfloat16
    )
    widened = jnp.einsum(
        "tmshwr,tcr->tmshwc", rounded_hidden, expand, preferred_element_type=jnp.float32
    )
    mask_moments = summed_members([pixel_sums(widened, pixel_weight)])
    widened_normed, widened_inverse = normalize(widened, mask_moments[0], counted)
    task_mask = jax.nn.sigmoid(
        affine_rows(widened_normed, norm_gain[2 : 2 + tasks][:, None], norm_shift[2 : 2 + tasks][:, None])
    )
    rounded_attended = (task_mask * shared_out).astype(jnp.bfloat16)
    attended_columns = patch_columns(rounded_attended)
    task_pre = jnp.einsum(
        "tmshwk,tok->tmshwo", attended_columns, task_conv, preferred_element_type=jnp.float32
    )
    task_moments = summed_members([pixel_sums(task_pre, pixel_weight)])
    task_normed, task_inverse = normalize(task_pre, task_moments[0], counted)
    task_out = jax.nn.silu(
        affine_rows(task_normed, norm_gain[2 + tasks :][:, None], norm_shift[2 + tasks :][:, None])
    )
    pooled = jnp.concatenate([soft_pool(shared_out)[None], soft_pool(task_out)], axis=0)
    kept_state = (
        frames,
        counted,
        first_normed,
        first_inverse,
        rounded_first,
        second_normed,
        second_inverse,
        narrow_normed,
        narrow_inverse,
        rounded_hidden,
        widened_normed,
        widened_inverse,
        rounded_attended,
        task_normed,
        task_inverse,
    )
    return (pooled, kept_state)


def section_backward(upstream, kept_state, pixel_weight, squares, weights):
    (
        first_conv,
        second_conv,
        squeeze,
        expand,
        task_conv,
        norm_gain,
        norm_shift,
        squeeze_gain,
        squeeze_shift,
    ) = weights
    (
        frames,
        counted,
        first_normed,
        first_inverse,
        rounded_first,
        second_normed,
        second_inverse,
        narrow_normed,
        narrow_inverse,
        rounded_hidden,
        widened_normed,
        widened_inverse,
        rounded_attended,
        task_normed,
        task_inverse,
    ) = kept_state
    channels = frames.shape[-1]
    tasks = squeeze.shape[0]
    task_gain = norm_gain[2 + tasks :][:, None]
    mask_gain = norm_gain[2 : 2 + tasks][:, None]
    task_active = affine_rows(task_normed, task_gain, norm_shift[2 + tasks :][:, None])
    task_out = jax.nn.silu(task_active)
    grad_task_act = pool_back(upstream[1:], task_out) * silu_slope(task_active)
    task_sums, square_all = summed_members(
        [gradient_sums(grad_task_act, task_normed, pixel_weight), squares]
    )
    grad_task = norm_backward(
        grad_task_act, task_normed, task_inverse, task_gain, task_sums, counted, pixel_weight
    ).astype(jnp.bfloat16)
    attended_columns = patch_columns(rounded_attended)
    task_conv_grad = jnp.einsum(
        "tmshwo,tmshwk->tok", grad_task, attended_columns, preferred_element_type=jnp.float32
    )
    grad_attended = (
        columns_back(
            jnp.einsum(
                "tmshwo,tok->tmshwk", grad_task, task_conv, preferred_element_type=jnp.float32
            ),
            channels,
        )

    )
    second_active = affine_rows(second_normed, norm_gain[1], norm_shift[1])
    shared_out = jax.nn.silu(second_active)
    task_mask = jax.nn.sigmoid(affine_rows(widened_normed, mask_gain, norm_shift[2 : 2 + tasks][:, None]))
    grad_mask_act = grad_attended * shared_out * task_mask * (1.0 - task_mask)
    mask_sums = summed_members([gradient_sums(grad_mask_act, widened_normed, pixel_weight)])[0]
    grad_widened = norm_backward(
        grad_mask_act, widened_normed, widened_inverse, mask_gain, mask_sums, counted, pixel_weight
    ).astype(jnp.bfloat16)
    expand_grad = jnp.einsum(
        "tmshwc,tmshwr->tcr", grad_widened, rounded_hidden, preferred_element_type=jnp.float32
    )
    narrow_active = affine_rows(narrow_normed, squeeze_gain[:, None], squeeze_shift[:, None])
    grad_narrow_act = jnp.einsum(
        "tmshwc,tcr->tmshwr", grad_widened, expand, preferred_element_type=jnp.float32
    ) * silu_slope(narrow_active)
    grad_shared = pool_back(upstream[0], shared_out) + jnp.sum(grad_attended * task_mask, axis=0)
    grad_second_act = grad_shared * silu_slope(second_active)
    second_sums, narrow_sums = summed_members(
        [
            gradient_sums(grad_second_act, second_normed, pixel_weight),
            gradient_sums(grad_narrow_act, narrow_normed, pixel_weight),
        ]
    )
    grad_second = norm_backward(
        grad_second_act,
        second_normed,
        second_inverse,
        norm_gain[1],
        second_sums,
        counted,
        pixel_weight,
    ).astype(jnp.bfloat16)
    grad_narrow = norm_backward(
        grad_narrow_act,
        narrow_normed,
        narrow_inverse,
        squeeze_gain[:, None],
        narrow_sums,
        counted,
        pixel_weight,
    ).astype(jnp.bfloat16)
    middle_columns = patch_columns(rounded_first)
    second_conv_grad = jnp.einsum(
        "mshwo,mshwk->ok", grad_second, middle_columns, preferred_element_type=jnp.float32
    )
    earlier = frames[1:]
    squeeze_grad = jnp.concatenate(
        [
            jnp.einsum(
                "tmshwr,mshwc->trc", grad_narrow, rounded_first, preferred_element_type=jnp.float32
            ),
            jnp.einsum(
                "tmshwr,tmshwc->trc", grad_narrow, earlier, preferred_element_type=jnp.float32
            ),
        ],
        axis=-1,
    )
    grad_joined = jnp.einsum(
        "tmshwr,trc->tmshwc", grad_narrow, squeeze, preferred_element_type=jnp.float32
    )
    grad_first_out = (
        columns_back(
            jnp.einsum(
                "mshwo,ok->mshwk", grad_second, second_conv, preferred_element_type=jnp.float32
            ),
            channels,
        )
        + jnp.sum(grad_joined[..., :channels], axis=0)
    )
    grad_earlier = grad_joined[..., channels:]
    first_active = affine_rows(first_normed, norm_gain[0], norm_shift[0])
    grad_first_act = grad_first_out * silu_slope(first_active)
    first_sums = summed_members([gradient_sums(grad_first_act, first_normed, pixel_weight)])[0]
    grad_first = norm_backward(
        grad_first_act, first_normed, first_inverse, norm_gain[0], first_sums, counted, pixel_weight
    ).astype(jnp.bfloat16)
    input_columns = patch_columns(frames[0])
    first_conv_grad = jnp.einsum(
        "mshwo,mshwk->ok", grad_first, input_columns, preferred_element_type=jnp.float32
    )
    grad_shared_in = (
        columns_back(
            jnp.einsum("mshwo,ok->mshwk", grad_first, first_conv, preferred_element_type=jnp.float32),
            channels,
        )

    )
    grad_frames = jnp.concatenate([grad_shared_in[None], grad_earlier], axis=0)
    first_norm, second_norm, mask_norm, task_norm, narrow_norm = (
        jnp.sum(sums, axis=-3)
        for sums in (first_sums, second_sums, mask_sums, task_sums, narrow_sums)
    )
    norm_rows = jnp.concatenate(
        [first_norm[None], second_norm[None], mask_norm, task_norm], axis=0
    )
    weight_terms = (first_conv_grad, second_conv_grad, squeeze_grad, expand_grad, task_conv_grad)
    norm_terms = (norm_rows[:, 1], norm_rows[:, 0], narrow_norm[:, 1], narrow_norm[:, 0])
    return (grad_frames, weight_terms, norm_terms, square_all)


def shards(
    stream_in,
    image_count,
    out_grad,
    first_conv,
    second_conv,
    squeeze,
    expand,
    task_conv,
    norm_gain,
    norm_shift,
    squeeze_gain,
    squeeze_shift,
):
    weights = (
        first_conv[0],
        second_conv[0],
        squeeze[0],
        expand[0],
        task_conv[0],
        norm_gain[0],
        norm_shift[0],
        squeeze_gain[0],
        squeeze_shift[0],
    )
    maps_count, images, height, breadth, channels = stream_in.shape
    micro_count = image_count.shape[1]
    slot_count = images // micro_count
    leading_section = lax.axis_index("section") == 0
    live = jnp.arange(slot_count)[None, :] < image_count[0][:, None]
    pixel_weight = live.astype(jnp.float32)[:, :, None, None, None]

    def by_micro(maps):
        return maps.reshape((maps_count, micro_count, slot_count) + maps.shape[2:])

    def whole_pool(pooled):
        masked = pooled * pixel_weight
        squares = jnp.sum(masked * masked, axis=(1, 2, 3, 4, 5))
        return masked.astype(jnp.bfloat16), jnp.broadcast_to(squares[:, None], (maps_count, channels))

    one_pooled, one_state = section_forward(by_micro(stream_in), pixel_weight, weights)
    one_features, one_squares = whole_pool(one_pooled)
    arrived = from_behind(one_features, "section", 1)
    two_pooled, two_state = section_forward(arrived, pixel_weight, weights)
    two_features, two_squares = whole_pool(two_pooled)
    two_upstream = by_micro(out_grad).astype(jnp.float32) * pixel_weight
    two_back = section_backward(two_upstream, two_state, pixel_weight, two_squares, weights)
    sendback = two_back[0].astype(jnp.bfloat16)
    returned = from_behind(sendback, "section", -1)
    one_upstream = returned.astype(jnp.float32) * pixel_weight
    one_back = section_backward(one_upstream, one_state, pixel_weight, one_squares, weights)

    half = ((0, 0),) * 3 + ((0, height // 4), (0, breadth // 4), (0, 0))
    full = ((0, 0),) * 3 + ((0, height // 2), (0, breadth // 2), (0, 0))
    feature_out = jnp.where(leading_section, one_features, jnp.pad(two_features, half))
    feature_out = feature_out.reshape((maps_count, images) + feature_out.shape[3:])
    recorded = lax.optimization_barrier(sendback).astype(jnp.float32)
    input_grad_out = jnp.where(leading_section, one_back[0], jnp.pad(recorded, full))
    input_grad_out = input_grad_out.reshape((maps_count, images) + input_grad_out.shape[3:])
    reduced = tuple(
        lax.psum_scatter(
            jnp.where(leading_section, one, two).reshape(-1).astype(jnp.bfloat16),
            "dp",
            scatter_dimension=0,
            tiled=True,
        ).astype(jnp.float32)
        for one, two in zip(one_back[1], two_back[1])
    )
    norm_sums = tuple(
        jnp.where(leading_section, one, two) for one, two in zip(one_back[2], two_back[2])
    )
    live_images = jnp.sum(one_state[1][:, 0]) / (height * breadth)
    feature_pixels = jnp.where(leading_section, height * breadth // 4, height * breadth // 16)
    root_square = jnp.sqrt(
        jnp.where(leading_section, one_back[3], two_back[3])[:, 0]
        / (live_images * feature_pixels * channels)
    )
    return (
        feature_out[None],
        input_grad_out[None],
        reduced[0][None],
        reduced[1][None],
        reduced[2][None],
        reduced[3][None],
        reduced[4][None],
        norm_sums[0][None],
        norm_sums[1][None],
        norm_sums[2][None],
        norm_sums[3][None],
        root_square[None],
    )


TAPS = 9
MESH = pl.DeviceIdType.MESH
FIRST, SECOND, MASK, TASK, NARROW = 0, 1, 2, 5, 8
NORMS = 11
(F_FIRST, F_SECOND, B_FIRST, F_NARROW, F_MASK, F_TASK, B_NARROW, B_TASK, B_MASK) = range(9)
GROUPS_OF_SUMS = 9
(
    P_FIRST, P_FIRST_DONE, P_NARROW_DONE, P_MASK_DONE, P_ATTENDED, P_TASKED, P_SUMMED,
    P_TASK_DONE, P_BTASK_SUMS, P_BTASK_DONE, P_BMASK_START, P_BMASK_SUMS, P_BMASK_DONE,
    P_BNARROW_DONE, P_BFIRST_START, P_BFIRST_SUMS, P_BFIRST_DONE,
) = range(17)


def sigmoid(active):
    return 0.5 * jnp.tanh(0.5 * active) + 0.5


def silu_parts(active):
    sigmoid_of = sigmoid(active)
    return active * sigmoid_of, sigmoid_of * (1.0 + active * (1.0 - sigmoid_of))


def dot_nt(left, right):
    return lax.dot_general(
        left, right, (((1,), (1,)), ((), ())), preferred_element_type=jnp.float32
    )


def dot_nn(left, right):
    return lax.dot_general(
        left, right, (((1,), (0,)), ((), ())), preferred_element_type=jnp.float32
    )


def loop(count, body, start=0):
    lax.fori_loop(start, count, lambda i, _: (body(i), 0)[1], 0)


def main_kernel(plan, *refs):
    (
        count_ref, stream, cotangent, gain_in, shift_in, narrow_gain, narrow_shift,
        w1, w2, sq, ex, tc,
        o_ref, ig_ref, norm_ref, total_ref, a_one, a_two, d_one, d_two, pair_one, pair_two,
        q_one, q_two, dq_one, dq_two, beside, r_first, r_second, r_squeeze, r_expand, r_task,
        w1s, w2s, sqs, exs, tcs, gain, shift, x_one, x_two, og_ref, sg_in, sg_out,
        masks, pad, xh, aux, share, p_act, ub, ab, nb, dr, gp, rows, inv, tot, counts, osq,
        wide, tbuf, turned, joint, slots_one, slots_three, slots_four,
        held, dbuf, cols, out, stage_flat,
        w_load, sync_send, sync_recv, h_send, h_recv, a_send, a_recv, v_send, v_recv, q_recv, s_send, s_recv, u_send, u_recv,
        d_send, d_recv, dq_send, dq_recv, t_send, t_own, r_recv, load_sem,
    ) = refs
    lines, mates, tasks, c = plan["lines"], plan["mates"], plan["tasks"], plan["channels"]
    high, across, live = plan["high"], plan["across"], plan["live"]
    hc = c // 2
    active_of = dr.at[0]
    micro = masks.shape[0]
    section = lax.axis_index("section")
    other = 1 - section
    me = lax.axis_index("dp")
    z, j = me // mates, lax.rem(me, mates)
    unit = c // lines
    pieces = unit // mates
    task_rows = tasks * c // lines
    kinds = ((0, unit), (unit, unit), (0, task_rows), None, (2 * unit, task_rows))

    def plane_tasks(line):
        return (task_rows * line) // c, (task_rows * (line + 1) - 1) // c

    def plane_needs(line, task):
        first, last = plane_tasks(line)
        return (first <= task) & (task <= last)

    def device_needs(device, task):
        own = task_rows // mates
        return ((own * device) // c <= task) & (task <= (own * device + own - 1) // c)

    def mate(step):
        return z * mates + lax.rem(j + step, mates)

    def liner(step):
        return lax.rem(z + step, lines) * mates + j

    def remote(source, target, send, recv, to, device):
        return pltpu.make_async_remote_copy(
            src_ref=source, dst_ref=target, send_sem=send, recv_sem=recv,
            device_id=(to, device), device_id_type=MESH,
        )

    def got(some, recv):
        remote(some, some, sync_send.at[0, 0], recv, section, me).wait_recv()

    def sent(some, send):
        remote(some, some, send, sync_recv.at[0, 0], section, me).wait_send()

    def push(source, target, send, recv, to, device, own=None):
        same = (section == to) & (me == device)

        @pl.when(same)
        def _():
            pltpu.make_async_copy(source, target, recv if own is None else own).start()

        @pl.when(jnp.logical_not(same))
        def _():
            remote(source, target, send, recv, to, device).start()

    def pushed(some, send, to, device, own=None):
        same = (section == to) & (me == device)

        @pl.when(jnp.logical_not(same))
        def _():
            sent(some, send)

        if own is not None:

            @pl.when(same)
            def _():
                pltpu.make_async_copy(some, some, own).wait()

    def across_cores(source, target, send, recv):
        remote(source, target, send, recv, other, me).start()

    def sums_at(group):
        if group < 3:
            ref, at, count = slots_one, group, 2 if group == F_FIRST else 1
        elif group < 7:
            ref, at, count = slots_three, group - 3, 3
        else:
            ref, at, count = slots_four, group - 7, 4
        return ref.at[at], count, group

    def sums_place(group, stage, digits):
        ref, count, _ = sums_at(group)
        return ref.at[stage, digits, pl.ds(0, count)]

    def sums_send(group, stage, digit, devices):
        at = sums_at(group)[2]
        here = sums_place(group, stage, digit)
        for device in devices:
            remote(
                here, here, sync_send.at[at, stage], sync_recv.at[at, stage], section, device
            ).start()

    def sums_got(group, stage, digits):
        ref, count, at = sums_at(group)
        got(sums_place(group, stage, pl.ds(0, digits - 1)), sync_recv.at[at, stage])
        summed = ref[stage, 0, pl.ds(0, count)]
        for digit in range(1, digits):
            summed = summed + ref[stage, digit, pl.ds(0, count)]
        return summed

    def sums_start(group):
        sums_send(group, 0, j, [mate(step) for step in range(1, mates)])

    def sums_mid(group):
        ref, count, _ = sums_at(group)
        ref[1, z, pl.ds(0, count)] = sums_got(group, 0, mates)
        sums_send(group, 1, z, [liner(step) for step in range(1, lines)])

    def sums_end(group):
        count = sums_at(group)[1]
        tot[pl.ds(0, count)] = sums_got(group, 1, lines)

    def sums_sent(group):
        at = sums_at(group)[2]
        for stage, digits in enumerate((mates, lines)):
            sent(
                sums_place(group, stage, pl.ds(0, digits - 1)), sync_send.at[at, stage]
            )

    W_FIRST, W_SQUEEZE, W_SECOND, W_EXPAND, W_TASK = range(5)

    def weight_copy(index):
        if index >= W_TASK:
            source, target = tc.at[index - W_TASK], tcs.at[index - W_TASK]
        else:
            source, target = ((w1, w1s), (sq, sqs), (w2, w2s), (ex, exs))[index]
        return pltpu.make_async_copy(source, target, w_load.at[index])

    def make_block(b):
        leading = b == 0
        rows_high, rows_across, images = (
            (high, across, live) if leading else (high // 2, across // 2, 8)
        )
        per_row = images * rows_across
        n = rows_high * per_row
        wide_n = plan["wide"] if leading else 128
        pixels = float(rows_high * rows_across)
        half = per_row // 2
        source = x_one if leading else x_two
        a_ref, d_ref, pair_ref, q_ref, dq_ref = (
            (a_one, d_one, pair_one, q_one, dq_one) if leading
            else (a_two, d_two, pair_two, q_two, dq_two)
        )
        position = lax.rem(
            lax.broadcasted_iota(jnp.int32, (per_row, c), 0), jnp.int32(rows_across)
        )
        even = lax.rem(position, jnp.int32(2)) == 0
        span = pl.ds(0, n)
        used = pl.ds(0, per_row)

        def each(body):
            for h in range(rows_high):
                body(h)

        def part(h):
            return pl.ds(h * per_row, per_row)

        def shifted(values):
            left = jnp.where(position >= 1, pltpu.roll(values, 1, 0), 0.0)
            right = jnp.where(position <= rows_across - 2, pltpu.roll(values, per_row - 1, 0), 0.0)
            return [v.astype(jnp.bfloat16) for v in (left, values, right)]

        def put_pad(h, values, backward=False):
            sides = shifted(values)
            for side, v in enumerate(reversed(sides) if backward else sides):
                pad[pl.ds((h + 1) * per_row, per_row), pl.ds(side * c, c)] = v

        def conv_to(weight, store_at):
            for out in range(2):
                total_of = None
                for dy in range(3):
                    one = dot_nt(
                        pad[pl.ds(dy * per_row, n), :],
                        weight[pl.ds(out * hc, hc), pl.ds(dy * 3 * c, 3 * c)],
                    )
                    total_of = one if total_of is None else total_of + one
                store_at[:, pl.ds(out * hc, hc)] = total_of

        def conv_back_to(weight, store_at):
            for out in range(2):
                total_of = None
                for dy in range(3):
                    for side in range(3):
                        one = dot_nn(
                            pad[pl.ds((2 - dy) * per_row, n), pl.ds(side * c, c)],
                            weight[:, pl.ds((dy * 3 + side) * c + out * hc, hc)],
                        )
                        total_of = one if total_of is None else total_of + one
                store_at[:, pl.ds(out * hc, hc)] = total_of

        def write_stats(group, member, first, second):
            ref = sums_at(group)[0]
            for k in range(micro):
                weight = masks[k, used, :]
                ref[0, j, member, pl.ds(k, 1), :] = jnp.sum(first * weight, 0, keepdims=True)
                ref[0, j, member, pl.ds(micro + k, 1), :] = jnp.sum(
                    second * weight, 0, keepdims=True
                )

        def moments(group, member, values_ref):
            first = second = None
            for h in range(rows_high):
                v = values_ref[pl.ds(h * per_row, per_row), :]
                first = v if h == 0 else first + v
                second = v * v if h == 0 else second + v * v
            write_stats(group, member, first, second)

        def start(group):
            sums_start(group)

        def mid(group):
            sums_mid(group)

        def end(group):
            sums_end(group)

        def row(ref, k):
            return ref[pl.ds(k, 1), :]

        def total(member, k):
            return tot[member, pl.ds(k, 1), :]

        def norm_rows(index, member):
            mean_rows = inv_rows = None
            for k in range(micro):
                n_k = row(counts, k) * pixels
                mean = total(member, k) / n_k
                spread_of = total(member, micro + k) / n_k - mean * mean
                inverse = lax.rsqrt(spread_of + EPSILON)
                inv[index, pl.ds(k, 1), :] = inverse
                weight = masks[k, used, :]
                mean_rows = weight * mean if k == 0 else mean_rows + weight * mean
                inv_rows = weight * inverse if k == 0 else inv_rows + weight * inverse
            rows[0, used, :] = mean_rows
            rows[1, used, :] = inv_rows

        def normalized(index, h, raw):
            normed = (raw - rows[0, used, :]) * rows[1, used, :]
            xh[index, part(h), :] = normed
            return normed * gain[index] + shift[index]

        def back_rows(index, member):
            norm_ref[index] = tot[member]
            scale_rows = shift_rows = slope_rows = None
            for k in range(micro):
                n_k = row(counts, k) * pixels
                weight = masks[k, used, :]
                scale = inv[index, pl.ds(k, 1), :] * gain[index]
                by_shift = total(member, k) / n_k
                by_gain = total(member, micro + k) / n_k
                scale_rows = weight * scale if k == 0 else scale_rows + weight * scale
                shift_rows = weight * by_shift if k == 0 else shift_rows + weight * by_shift
                slope_rows = weight * by_gain if k == 0 else slope_rows + weight * by_gain
            rows[0, used, :] = scale_rows
            rows[1, used, :] = shift_rows
            rows[2, used, :] = slope_rows

        def partner(v):
            return jnp.where(even, pltpu.roll(v, per_row - 1, 0), pltpu.roll(v, 1, 0))

        def soft_pool(index, read):
            squares = None
            for pair in range(rows_high // 2):
                upper, lower = read(2 * pair), read(2 * pair + 1)
                top = jnp.maximum(upper, lower)
                top = jnp.maximum(top, partner(top))
                upper, lower = jnp.exp(upper - top), jnp.exp(lower - top)
                summed = upper + lower
                summed = summed + partner(summed)
                share[index, pl.ds(2 * pair * per_row, per_row), :] = upper / summed
                share[index, pl.ds((2 * pair + 1) * per_row, per_row), :] = lower / summed
                pooled = top + jnp.log(summed * 0.25)
                for lane in range(c // 128):
                    wide[lane, used, :] = pooled[:, lane * 128 : (lane + 1) * 128]
                pooled = jnp.concatenate(
                    [wide[lane, pl.ds(0, half, stride=2), :] for lane in range(c // 128)], axis=1
                )
                if leading:
                    kept = pooled
                    pooled = jnp.concatenate(
                        [pooled, jnp.zeros((32 - half, c), jnp.float32)], axis=0
                    )
                    o_ref[index, pl.ds(32 * pair, 32), :] = pooled.astype(jnp.bfloat16)
                else:
                    alive = lax.broadcasted_iota(jnp.int32, (half, c), 0) < live * (
                        rows_across // 2
                    )
                    kept = jnp.where(alive, pooled, 0.0)
                    o_ref[index, pl.ds(half * pair, half), :] = kept.astype(jnp.bfloat16)
                square = jnp.sum(kept * kept, 0, keepdims=True)
                squares = square if squares is None else squares + square
            osq[index] = squares
            if leading:
                across_cores(
                    o_ref.at[index], x_two.at[index], h_send.at[index], h_recv.at[index]
                )

        def widened(index, pair):
            if leading:
                upstream = sg_in[index, pl.ds(pl.multiple_of(32 * pair, 32), 32), :]
                upstream = upstream.astype(jnp.float32)[:half]
            else:
                upstream = og_ref[index]
            for lane in range(c // 128):
                piece = upstream[:, lane * 128 : (lane + 1) * 128]
                wide[lane, pl.ds(0, half, stride=2), :] = piece
                wide[lane, pl.ds(1, half, stride=2), :] = piece
            return jnp.concatenate(
                [wide[lane, used, :] for lane in range(c // 128)], axis=1
            )

        pair_at = 2 * (z // 2)
        far_at = lines - 2 - pair_at
        inner = (z == 1) | (z == 2)

        def send_shared(which):
            from_ref = shared_source(which)
            neighbour = 2 * pair_at + 1 - z
            for at, plane in enumerate((z, neighbour)):
                push(
                    from_ref, a_ref.at[which, z], a_send.at[b, which, at],
                    a_recv.at[b, which, 0], 0, plane * mates + j,
                )

        def shared_source(which):
            if leading:
                return source.at[0] if which == 0 else ub.at[span]
            return o_ref.at[0] if which == 0 else beside.at[0]

        def pair_lines(which, first):
            return a_ref.at[which, pl.ds(first, 2)]

        def relay_pair(which):
            got(pair_lines(which, 0), a_recv.at[b, which, 0])

            @pl.when(inner)
            def _():
                here = pair_lines(which, pair_at)
                remote(
                    here, here, a_send.at[b, which, 2], a_recv.at[b, which, 1], 0,
                    (lines - 1 - z) * mates + j,
                ).start()

        def relay_far(which):
            got(pair_lines(which, 0), a_recv.at[b, which, 1])

            @pl.when(inner)
            def _():
                here = pair_lines(which, far_at)
                remote(
                    here, here, a_send.at[b, which, 3], a_recv.at[b, which, 1], 0,
                    (2 * pair_at + 1 - z) * mates + j,
                ).start()

        def task_planes(task):
            first = (c * task) // task_rows
            return first, first + 1

        def task_slot(kind, task, plane):
            return 2 + 2 * kind + task - plane_tasks(plane)[0]

        def task_source(kind, task):
            if leading:
                return (
                    source.at[1 + task] if kind == 0
                    else ab.at[task, span] if kind == 1 else nb.at[task, span]
                )
            return o_ref.at[1 + task] if kind == 0 else beside.at[tasks * kind - 2 + task]

        def send_task(kind, task):
            first, last = task_planes(task)
            near = jnp.clip(z, first, last)
            passed_on = (z < first) | (z > last)
            tensor = 2 + tasks * kind + task
            push(
                task_source(kind, task), a_ref.at[task_slot(kind, task, near), z],
                a_send.at[b, tensor, 0],
                a_recv.at[b, tensor, jnp.where(passed_on, jnp.int32(0), jnp.int32(1))],
                0, near * mates + j,
            )

            @pl.when(jnp.logical_not(passed_on))
            def _():
                opposite = first + last - z
                push(
                    task_source(kind, task), a_ref.at[task_slot(kind, task, opposite), z],
                    a_send.at[b, tensor, 1], a_recv.at[b, tensor, 1], 0, opposite * mates + j,
                )

        def task_passes(task):
            first, last = task_planes(task)
            passes = []
            if first > 0:
                passes.append((first, 0, first, last))
            if last < lines - 1:
                passes.append((last, last + 1, lines - 1 - last, first))
            return passes

        def relay_task(kind, task):
            tensor = 2 + tasks * kind + task
            for plane, first, count, to_plane in task_passes(task):

                @pl.when(z == plane)
                def _():
                    some = pl.ds(first, count)
                    here = a_ref.at[task_slot(kind, task, plane), some]
                    got(here, a_recv.at[b, tensor, 0])
                    remote(
                        here, a_ref.at[task_slot(kind, task, to_plane), some],
                        a_send.at[b, tensor, 2], a_recv.at[b, tensor, 1], 0,
                        to_plane * mates + j,
                    ).start()

        def core_of(kind):
            return 0 if leading and kind < 2 else 1

        def deliver(at, slot, task=None):
            for step in range(mates):

                def send():
                    push(
                        a_ref.at[at], q_ref.at[slot, j], v_send.at[b, at, step],
                        q_recv.at[b, slot], core_of(at), mate(step),
                    )

                if task is None:
                    send()
                else:
                    pl.when(device_needs(mate(step), task))(send)

        def delivered(at, task=None):
            for step in range(mates):

                def wait():
                    pushed(a_ref.at[0], v_send.at[b, at, step], core_of(at), mate(step))

                if task is None:
                    wait()
                else:
                    pl.when(device_needs(mate(step), task))(wait)

        def task_done(kind, task):
            tensor = 2 + tasks * kind + task
            first, last = task_planes(task)
            for plane, count in ((first, lines - first), (last, last + 1)):

                @pl.when(z == plane)
                def _():
                    got(a_ref.at[0, pl.ds(0, count)], a_recv.at[b, tensor, 1])
                    at = task_slot(kind, task, plane)
                    if kind == 2:
                        deliver(at, at - 4, task)
                    else:
                        across_cores(
                            a_ref.at[at], a_ref.at[at], v_send.at[b, at, 0], v_recv.at[b, at]
                        )

        def task_got(kind, task):
            for plane in task_planes(task):
                at = task_slot(kind, task, plane)
                if kind == 2:

                    @pl.when((z == plane) & device_needs(me, task))
                    def _():
                        got(q_ref.at[0], q_recv.at[b, at - 4])

                else:

                    @pl.when(z == plane)
                    def _():
                        got(a_ref.at[0], v_recv.at[b, at])

        def shared_got(which):
            got(q_ref.at[0], q_recv.at[b, which])

        def relays(kind):
            for task in range(tasks):
                relay_task(kind, task)

        def done(kind):
            for task in range(tasks):
                task_done(kind, task)

        def exchange_activations():
            def here(index):
                if not leading:
                    got(beside.at[0], s_recv.at[index])

            def send_tasks(kind):
                for task in range(tasks):
                    if kind:
                        here(tasks * kind - 2 + task)
                    send_task(kind, task)

            send_shared(0)
            send_tasks(0)
            here(0)
            send_shared(1)
            relay_pair(0)
            relays(0)
            relay_pair(1)
            send_tasks(1)
            relay_far(0)
            deliver(0, 0)
            done(0)
            relays(1)
            relay_far(1)
            deliver(1, 1)
            if leading:
                across_cores(a_ref.at[1], q_ref.at[1, j], u_send.at[0], u_recv.at[0])
            send_tasks(2)
            done(1)
            relays(2)
            done(2)

        def exchange_sent():
            one_piece = a_ref.at[0, 0]
            for which in range(2):
                for at, plane in enumerate((z, 2 * pair_at + 1 - z)):
                    pushed(one_piece, a_send.at[b, which, at], 0, plane * mates + j)

                @pl.when(inner)
                def _():
                    for at in (2, 3):
                        sent(pair_lines(which, 0), a_send.at[b, which, at])

                delivered(which)
            if leading:
                sent(a_ref.at[0], u_send.at[0])
            for kind in range(3):
                for task in range(tasks):
                    first, last = task_planes(task)
                    tensor = 2 + tasks * kind + task
                    near = jnp.clip(z, first, last)
                    pushed(one_piece, a_send.at[b, tensor, 0], 0, near * mates + j)

                    @pl.when((z == first) | (z == last))
                    def _():
                        pushed(
                            one_piece, a_send.at[b, tensor, 1], 0, (first + last - z) * mates + j
                        )

                    for plane, _, count, _ in task_passes(task):

                        @pl.when(z == plane)
                        def _():
                            sent(a_ref.at[0, pl.ds(0, count)], a_send.at[b, tensor, 2])

                    for plane in (first, last):

                        @pl.when(z == plane)
                        def _():
                            at = task_slot(kind, task, plane)
                            if kind == 2:
                                delivered(at, task)
                            else:
                                sent(a_ref.at[0], v_send.at[b, at, 0])

        def spread_place(kind, task, k):
            offset, _ = kinds[kind]
            if kind < 2:
                return kind, k, offset
            number = lines * task + k
            at = pl.multiple_of(offset + lax.rem(number, tasks) * unit, unit)
            return (2 if kind == 4 else 0) + task, number // tasks, at

        def spread_refs(kind):
            return (joint, pair_ref) if kind == 2 else (turned, d_ref)

        def spread_lanes(kind):
            return pl.ds(0, 2 * n if kind == 2 else wide_n)

        def spread(kind, task=0):
            from_ref, target = spread_refs(kind)
            for k in range(lines):
                index, plane, offset = spread_place(kind, task, k)
                push(
                    from_ref.at[index, pl.ds(k * unit, unit), spread_lanes(kind)],
                    target.at[z, pl.ds(offset, unit)],
                    d_send.at[kind, task, k], d_recv.at[b, kind], core_of(kind), plane * mates + j,
                )

        def spread_sent(kind, task=0):
            from_ref, _ = spread_refs(kind)
            for k in range(lines):
                _, plane, _ = spread_place(kind, task, k)
                pushed(
                    from_ref.at[0, pl.ds(k * unit, unit), spread_lanes(kind)],
                    d_send.at[kind, task, k], core_of(kind), plane * mates + j,
                )

        def spread_got(kind):
            offset, count = kinds[kind]
            got(spread_refs(kind)[1].at[:, pl.ds(offset, count)], d_recv.at[b, kind])

        def rounded(index, member, slot, target, before=None):
            back_rows(index, member)
            first = 0 if before is None else n

            def body(h):
                value = rows[0, used, :] * (
                    dr[slot, part(h), :] - rows[1, used, :] - xh[index, part(h), :] * rows[2, used, :]
                )
                if target is None:
                    xh[index, part(h), :] = value
                else:
                    tbuf[pl.ds(first + h * per_row, per_row), :] = value
                put_pad(h, value, True)

            each(body)
            if target is None:
                return
            if before is None:
                tbuf[pl.ds(n, wide_n - n), :] = jnp.zeros((wide_n - n, c), jnp.float32)
                count = wide_n
            else:
                tbuf[span, :] = before[...]
                count = 2 * n
            target[:, pl.ds(0, count)] = jnp.transpose(tbuf[pl.ds(0, count), :]).astype(jnp.bfloat16)

        def middle():
            return pad[pl.ds(per_row, n), pl.ds(c, c)]

        def beside_core(from_ref, index):
            if not leading:
                across_cores(from_ref, beside.at[index], s_send.at[index], s_recv.at[index])

        def forward_start():
            if not leading:
                got(x_two.at[0], h_recv.at[0])
            each(lambda h: put_pad(h, source[0, part(h), :].astype(jnp.float32)))
            weight_copy(W_FIRST).wait()
            conv_to(w1s, xh.at[FIRST, span])
            moments(F_FIRST, 0, xh.at[FIRST])
            start(F_FIRST)

        def forward():
            for index in range(W_SECOND, W_TASK + tasks):
                weight_copy(index).start()
            if not leading:
                for index in range(1, 1 + tasks):
                    got(x_two.at[0], h_recv.at[index])
            weight_copy(W_SQUEEZE).wait()

            def outer_narrow(task):
                xh[NARROW + task, span] = dot_nt(source[1 + task], sqs[task, :, pl.ds(c, c)])

            outer_narrow(0)
            mid(F_FIRST)
            loop(tasks, outer_narrow, 1)
            end(F_FIRST)
            counts[...] = tot[1]
            total_ref[0] = tot[1]
            norm_rows(FIRST, 0)

            def first_act(h):
                active, slope = silu_parts(normalized(FIRST, h, xh[FIRST, part(h), :]))
                aux[FIRST, part(h), :] = slope
                ub[part(h), :] = active.astype(jnp.bfloat16)
                put_pad(h, active)

            each(first_act)
            beside_core(ub.at[span], 0)

            def narrow(task):
                xh[NARROW + task, span] += dot_nt(middle(), sqs[task, :, pl.ds(0, c)])
                moments(F_NARROW, task, xh.at[NARROW + task])

            loop(tasks, narrow)
            start(F_NARROW)
            weight_copy(W_SECOND).wait()
            conv_to(w2s, xh.at[SECOND, span])
            mid(F_NARROW)
            moments(F_SECOND, 0, xh.at[SECOND])
            start(F_SECOND)
            weight_copy(W_EXPAND).wait()
            end(F_NARROW)

            def mask_of(task):
                norm_rows(NARROW + task, task)

                def act(h):
                    active, slope = silu_parts(
                        normalized(NARROW + task, h, xh[NARROW + task, part(h), :])
                    )
                    aux[NARROW + task, part(h), :] = slope
                    ab[task, part(h), :] = active.astype(jnp.bfloat16)

                each(act)
                beside_core(ab.at[task, span], 1 + task)
                xh[MASK + task, span] = dot_nt(ab[task, span], exs[task])
                moments(F_MASK, task, xh.at[MASK + task])

            mask_of(0)
            mid(F_SECOND)
            loop(tasks, mask_of, 1)
            start(F_MASK)
            end(F_SECOND)
            norm_rows(SECOND, 0)

            def second_act(h):
                active, slope = silu_parts(normalized(SECOND, h, xh[SECOND, part(h), :]))
                aux[SECOND, part(h), :] = slope
                p_act[part(h), :] = active

            each(second_act)
            mid(F_MASK)
            soft_pool(0, lambda h: p_act[part(h), :])
            end(F_MASK)

            def task_conv(task):
                norm_rows(MASK + task, task)

                def act(h):
                    active = normalized(MASK + task, h, xh[MASK + task, part(h), :])
                    sigmoid_of = sigmoid(active)
                    aux[MASK + task, part(h), :] = sigmoid_of
                    attended = sigmoid_of * p_act[part(h), :]
                    nb[task, part(h), :] = attended.astype(jnp.bfloat16)
                    put_pad(h, attended)

                each(act)
                beside_core(nb.at[task, span], 1 + tasks + task)
                pltpu.make_async_copy(tc.at[task], tcs.at[task], w_load.at[W_TASK + task]).wait()
                conv_to(tcs.at[task], xh.at[TASK + task, span])
                moments(F_TASK, task, xh.at[TASK + task])

            loop(tasks, task_conv)
            start(F_TASK)
            mid(F_TASK)
            end(F_TASK)

            def task_pool(task):
                norm_rows(TASK + task, task)

                def act(h):
                    active, slope = silu_parts(
                        normalized(TASK + task, h, xh[TASK + task, part(h), :])
                    )
                    aux[TASK + task, part(h), :] = slope
                    active_of[part(h), :] = active

                each(act)
                soft_pool(1 + task, lambda h: active_of[part(h), :])

            loop(tasks, task_pool)
            squares = sums_at(B_TASK)[0]
            squares[0, j, tasks] = jnp.zeros((8, c), jnp.float32)
            for index in range(1 + tasks):
                squares[0, j, tasks, pl.ds(index, 1), :] = osq[index]

        def handed(index):
            if leading:
                got(sg_in.at[0], h_recv.at[1 + tasks + index])

        def backward():
            def task_start(task):
                handed(1 + task)
                first = second = None
                for pair in range(rows_high // 2):
                    upstream = widened(1 + task, pair)
                    for h in (2 * pair, 2 * pair + 1):
                        at = part(h)
                        up = upstream * share[1 + task, at, :] * aux[TASK + task, at, :]
                        dr[task, at, :] = up
                        by = up * xh[TASK + task, at, :]
                        first = up if first is None else first + up
                        second = by if second is None else second + by
                write_stats(B_TASK, task, first, second)

            loop(tasks, task_start)
            start(B_TASK)
            mid(B_TASK)
            end(B_TASK)
            total_ref[1] = tot[tasks]

            def task_back(task):
                rounded(TASK + task, task, task, None)
                conv_back_to(tcs.at[task], dr.at[task, span])
                first = second = None
                for h in range(rows_high):
                    at = part(h)
                    m, p = aux[MASK + task, at, :], p_act[at, :]
                    through = dr[task, at, :] * m

                    @pl.when(task == 0)
                    def _():
                        gp[at, :] = through

                    @pl.when(task > 0)
                    def _():
                        gp[at, :] += through

                    up = through * p * (1.0 - m)
                    dr[task, at, :] = up
                    by = up * xh[MASK + task, at, :]
                    first = up if first is None else first + up
                    second = by if second is None else second + by
                write_stats(B_MASK, task, first, second)

            loop(tasks, task_back)
            handed(0)
            first = second = None
            for pair in range(rows_high // 2):
                upstream = widened(0, pair)
                for h in (2 * pair, 2 * pair + 1):
                    at = part(h)
                    up = (gp[at, :] + upstream * share[0, at, :]) * aux[SECOND, at, :]
                    dr[3, at, :] = up
                    by = up * xh[SECOND, at, :]
                    first = up if first is None else first + up
                    second = by if second is None else second + by
            write_stats(B_MASK, tasks, first, second)
            start(B_MASK)
            mid(B_MASK)
            end(B_MASK)

            def mask_back(task):
                rounded(MASK + task, task, task, joint.at[task], xh.at[TASK + task, span])
                spread(2, task)
                dr[task, span] = dot_nn(middle(), exs[task])
                first = second = None
                for h in range(rows_high):
                    at = part(h)
                    up = dr[task, at, :] * aux[NARROW + task, at, :]
                    dr[task, at, :] = up
                    by = up * xh[NARROW + task, at, :]
                    first = up if first is None else first + up
                    second = by if second is None else second + by
                write_stats(B_NARROW, task, first, second)

            loop(tasks, mask_back)
            start(B_NARROW)
            rounded(SECOND, tasks, 3, turned.at[1])
            spread(1)
            mid(B_NARROW)
            conv_back_to(w2s, gp.at[span])
            end(B_NARROW)

            def narrow_back(task):
                rounded(NARROW + task, task, task, turned.at[2 + task])
                spread(4, task)
                gp[span, :] += dot_nn(middle(), sqs[task, :, pl.ds(0, c)])
                grad = dot_nn(middle(), sqs[task, :, pl.ds(c, c)])
                outer_grad(1 + task, grad)

            def outer_grad(index, grad):
                if leading:
                    ig_ref[index, span, :] = grad
                else:
                    low = grad.astype(jnp.bfloat16)
                    sg_out[index] = low
                    ig_ref[index, span, :] = low.astype(jnp.float32)
                    at = 1 + tasks + index
                    across_cores(
                        sg_out.at[index], sg_in.at[index], h_send.at[at], h_recv.at[at]
                    )

            loop(tasks, narrow_back)
            first = second = None
            for h in range(rows_high):
                at = part(h)
                up = gp[at, :] * aux[FIRST, at, :]
                dr[3, at, :] = up
                by = up * xh[FIRST, at, :]
                first = up if first is None else first + up
                second = by if second is None else second + by
            write_stats(B_FIRST, 0, first, second)
            start(B_FIRST)
            mid(B_FIRST)
            end(B_FIRST)
            rounded(FIRST, 0, 3, turned.at[0])
            if leading:
                spread(0)
            conv_back_to(w1s, dr.at[0, span])
            outer_grad(0, dr[0, span, :])
            if not leading:
                spread(0)

        def settle():
            if not leading:
                loop(1 + 2 * tasks, lambda i: sent(beside.at[0], s_send.at[i]))
            for kind in range(2):
                spread_sent(kind)
            for kind in (2, 4):
                for task in range(tasks):
                    spread_sent(kind, task)
            for group in range(GROUPS_OF_SUMS):
                sums_sent(group)
            for index in range(1 + tasks):
                if leading:
                    sent(o_ref.at[0], h_send.at[index])
                else:
                    sent(sg_out.at[0], h_send.at[1 + tasks + index])

        deep = lines * wide_n

        def fetch(from_ref, target, index):
            copy = pltpu.make_async_copy(from_ref, target, load_sem.at[index])
            copy.start()
            return copy

        def rows_held(buffer):
            return held[buffer, :, pl.ds(0, wide_n), :].reshape(deep, c)

        def slot_of(piece):
            return (task_rows * z + piece * unit) // c - plane_tasks(z)[0]

        def clear_tail():
            for buffer in range(2):
                held[buffer, :, pl.ds(n, wide_n - n), :] = jnp.zeros(
                    (lines, wide_n - n, c), jnp.bfloat16
                )

        second_at = n % 128
        own_rows = task_rows // mates

        def dealt(kind):
            return (pieces * kind, pieces) if kind < 2 else (2 * pieces, own_rows)

        def deal(kind):
            spread_got(kind)
            offset, _ = kinds[kind]
            at, count = dealt(kind)
            for step in range(mates):
                first = pl.multiple_of(offset + lax.rem(j + step, mates) * count, pieces)
                push(
                    spread_refs(kind)[1].at[:, pl.ds(first, count), pl.ds(0, wide_n)],
                    dq_ref.at[j, :, pl.ds(at, count)], dq_send.at[b, kind, step],
                    dq_recv.at[b, kind], core_of(kind), mate(step),
                )

        def deal_sent(kind):
            _, count = dealt(kind)
            for step in range(mates):
                pushed(
                    dq_ref.at[0, :, pl.ds(0, count)], dq_send.at[b, kind, step], core_of(kind),
                    mate(step),
                )

        def deal_got(kind):
            at, count = dealt(kind)
            got(dq_ref.at[:, :, pl.ds(at, count)], dq_recv.at[b, kind])

        def conv_unit(number, slot, buffer):
            def copies(column):
                which = lax.rem(column, 2)
                return (
                    pltpu.make_async_copy(
                        q_ref.at[slot, column], held.at[which, :, pl.ds(0, n)],
                        load_sem.at[which],
                    ),
                    pltpu.make_async_copy(
                        dq_ref.at[column, :, pl.ds(number * pieces, pieces)],
                        dbuf.at[which, :, :, pl.ds(0, wide_n)], load_sem.at[2 + which],
                    ),
                )

            for copy in copies(jnp.int32(0)):
                copy.start()
            lane = lax.broadcasted_iota(jnp.int32, (lines * pieces, wide_n), 1)
            here = lax.rem(lane, jnp.int32(rows_across))

            def column_terms(column):
                which = lax.rem(column, 2)

                @pl.when(column < mates - 1)
                def _():
                    for copy in copies(column + 1):
                        copy.start()

                for copy in copies(column):
                    copy.wait()
                values = dbuf[which, :, :, pl.ds(0, wide_n)].astype(jnp.float32)
                values = values.reshape(lines * pieces, wide_n)
                if number >= 2:
                    values = jnp.where(lane < n, values, 0.0)
                for side in range(3):
                    moved = values
                    if side == 0:
                        moved = jnp.where(
                            here <= rows_across - 2, pltpu.roll(values, wide_n - 1, 1), 0.0
                        )
                    elif side == 2:
                        moved = jnp.where(here >= 1, pltpu.roll(values, 1, 1), 0.0)
                    for down in range(3):
                        by = moved
                        if down == 0:
                            by = pltpu.roll(moved, wide_n - per_row, 1)
                        elif down == 2:
                            by = pltpu.roll(moved, per_row, 1)
                        by = by.astype(jnp.bfloat16)
                        at = pl.ds((3 * down + side) * pieces, pieces)
                        for line in range(lines):
                            cols[at, pl.ds(line * wide_n, wide_n)] = by[
                                line * pieces : (line + 1) * pieces
                            ]
                terms = dot_nn(cols[pl.ds(0, TAPS * pieces), pl.ds(0, deep)], rows_held(which))

                @pl.when(column == 0)
                def _():
                    for tap in range(TAPS):
                        out[buffer, :, pl.ds(tap * c, c)] = terms[
                            tap * pieces : (tap + 1) * pieces
                        ]

                @pl.when(column > 0)
                def _():
                    for tap in range(TAPS):
                        out[buffer, :, pl.ds(tap * c, c)] += terms[
                            tap * pieces : (tap + 1) * pieces
                        ]

            loop(mates, column_terms)

        def staged_conv(number, slot):
            buffer = turn[0] % 2
            turn[0] += 1
            target = (
                (r_first, r_second)[number] if number < 2
                else r_task.at[pl.ds((number - 2) * pieces, pieces)]
            )
            free(
                buffer,
                lambda: pushed(
                    out.at[buffer], t_send.at[b, number, 0], b, me, t_own.at[number, 0]
                ),
            )
            conv_unit(number, slot, buffer)
            push(
                out.at[buffer], target, t_send.at[b, number, 0], r_recv.at[number], b, me,
                t_own.at[number, 0],
            )

        def flat_terms(kind, staged, parts, lanes, first):
            offset, _ = kinds[kind]
            from_ref = spread_refs(kind)[1]
            copies = [
                fetch(
                    from_ref.at[line, pl.ds(offset + piece * unit, unit), lanes],
                    cols.at[pl.ds(piece * unit, unit), pl.ds(line * wide_n, wide_n)],
                    4 + piece * lines + line,
                )
                for piece in range(tasks)
                for line in range(lines)
            ]
            loads = []
            for at, a_kind in parts:
                for piece in range(tasks):
                    if a_kind is not None:
                        loads.append(a_ref.at[2 + 2 * a_kind + slot_of(piece)])
                    elif piece == 0:
                        loads.append(q_ref.at[1, j])

            def load(number):
                return pltpu.make_async_copy(
                    loads[number], held.at[number % 2, :, pl.ds(first, n)],
                    load_sem.at[number % 2],
                )

            load(0).start()
            for copy in copies:
                copy.wait()
            number = -1
            for at, a_kind in parts:
                for piece in range(tasks):
                    if a_kind is not None or piece == 0:
                        number += 1
                        load(number).wait()
                        if number + 1 < len(loads):
                            load(number + 1).start()
                    terms = dot_nn(
                        cols[pl.ds(piece * unit, unit), pl.ds(0, deep)], rows_held(number % 2)
                    )
                    staged[pl.ds(piece * unit, unit), pl.ds(at, c)] = terms.astype(jnp.bfloat16)

        def flat_push(target, staged, index):
            for mate_at in range(mates):
                push(
                    staged.at[pl.ds(mate_at * own_rows, own_rows)], target.at[j],
                    t_send.at[b, index, mate_at], r_recv.at[index], b, z * mates + mate_at,
                    t_own.at[index, mate_at],
                )

        def flat_sent(staged, index):
            for mate_at in range(mates):
                pushed(
                    staged.at[pl.ds(0, own_rows)], t_send.at[b, index, mate_at], b,
                    z * mates + mate_at, t_own.at[index, mate_at],
                )

        def free(name, waits):
            if name in in_use:
                in_use[name]()
            in_use[name] = waits

        def terms_second():
            deal_got(1)
            shared_got(1)
            staged_conv(1, 1)

        def terms_first():
            deal_got(0)
            shared_got(0)
            staged_conv(0, 0)

        def terms_squeeze():
            spread_got(4)
            if leading:
                got(a_ref.at[0], u_recv.at[0])
            for task in range(tasks):
                task_got(0, task)
            free(2, lambda: flat_sent(stage_flat, 5))
            flat_terms(4, stage_flat, [(0, None), (c, 0)], pl.ds(0, wide_n), 0)
            flat_push(r_squeeze, stage_flat, 5)

        def terms_expand():
            for task in range(tasks):
                task_got(1, task)
            staged = stage_flat.at[:, pl.ds(0, c)]
            free(2, lambda: flat_sent(staged, 6))
            for buffer in range(2):
                held[buffer, :, pl.ds(0, second_at), :] = jnp.zeros(
                    (lines, second_at, c), jnp.bfloat16
                )
            flat_terms(2, staged, [(0, 1)], pl.ds(n - second_at, wide_n), second_at)
            flat_push(r_expand, staged, 6)
            clear_tail()

        def terms_tasks():
            deal_got(2)
            for task in range(tasks):
                task_got(2, task)
            for number in range(own_rows // pieces):
                task = (own_rows * me + number * pieces) // c
                staged_conv(2 + number, 2 + task - plane_tasks(z)[0])

        def terms_got():
            if leading:
                for number in range(own_rows // pieces):
                    got(r_first, r_recv.at[2 + number])
            senders = pl.ds(0, mates if leading else mates - 1)
            for index, target in ((5, r_squeeze), (6, r_expand)):
                got(target.at[senders], r_recv.at[index])

        def set_up():
            image = lax.div(
                lax.broadcasted_iota(jnp.int32, (per_row, c), 0), jnp.int32(rows_across)
            )
            for k in range(micro):
                masks[k, used, :] = (
                    jnp.where(image == k, 1.0, 0.0)
                    + jnp.where(image == micro, fourth[k], 0.0)
                    + jnp.where(image == micro + 1, fifth[k], 0.0)
                )
            zero = jnp.zeros((per_row, 3 * c), jnp.bfloat16)
            pad[pl.ds(0, per_row), :] = zero
            pad[pl.ds(n + per_row, per_row), :] = zero

        return types.SimpleNamespace(
            forward_start=forward_start, forward=forward, backward=backward, settle=settle,
            set_up=set_up, clear_tail=clear_tail, exchange=exchange_activations,
            exchange_sent=exchange_sent,
            second=terms_second, first=terms_first, squeeze=terms_squeeze, expand=terms_expand,
            task_terms=terms_tasks, terms_got=terms_got, deal=deal, deal_sent=deal_sent,
        )

    weight_copy(W_FIRST).start()
    weight_copy(W_SQUEEZE).start()
    barrier = pltpu.get_barrier_semaphore()
    greeted = (
        [(section, mate(step)) for step in range(1, mates)]
        + [(section, liner(step)) for step in range(1, lines)]
        + [(other, mate(step)) for step in range(mates)]
        + [(other, liner(step)) for step in range(1, lines)]
    )
    for device in greeted:
        pl.semaphore_signal(barrier, inc=1, device_id=device, device_id_type=MESH)
    numbers = [count_ref[0, k] for k in range(micro)]
    double = [jnp.where(number >= 2, jnp.float32(1.0), jnp.float32(0.0)) for number in numbers]
    fourth, fifth = [], []
    before = jnp.float32(0.0)
    for k in range(micro):
        fourth.append(double[k] * (1.0 - before))
        fifth.append(double[k] * before)
        before = before + double[k]
    count_slot = sums_at(F_FIRST)[0]
    count_slot[0, j, 1] = jnp.zeros((8, c), jnp.float32)
    for k in range(micro):
        count_slot[0, j, 1, pl.ds(k, 1), :] = jnp.full((1, c), 1.0) * (1.0 + double[k])
    for index in range(NORMS):
        at = pl.ds(index if index < NARROW else index - NARROW, 1)
        gain[index] = (gain_in if index < NARROW else narrow_gain)[at, :]
        shift[index] = (shift_in if index < NARROW else narrow_shift)[at, :]
    in_use, turn = {}, [0]
    one, two = make_block(0), make_block(1)

    def picked_rows(values, index, h):
        doubles = [values[index, 2 * k + 1, h].astype(jnp.float32) for k in range(micro)]
        rows_of = [values[index, 2 * k, h].astype(jnp.float32) for k in range(micro)]
        for weight in (fourth, fifth):
            picked = doubles[0] * weight[0]
            for k in range(1, micro):
                picked = picked + doubles[k] * weight[k]
            rows_of.append(picked)
        return rows_of

    def compact(index):
        for h in range(high):
            x_one[index, pl.ds(h * live * across, live * across), :] = jnp.concatenate(
                picked_rows(stream, index, h), axis=0
            ).astype(jnp.bfloat16)

    def cotangents():
        for index in range(1 + tasks):
            og_ref[index] = jnp.zeros(og_ref.shape[1:], jnp.float32)
            for i, upstream in enumerate(picked_rows(cotangent, index, 0)):
                og_ref[index, pl.ds(i * (across // 4), across // 4), :] = upstream

    @pl.when(section == 0)
    def _():
        one.set_up()
        loop(1 + tasks, compact)
        pl.semaphore_wait(barrier, len(greeted))
        one.forward_start()
        one.forward()
        one.exchange()
        two.exchange()
        one.clear_tail()
        one.backward()
        one.deal(1)
        one.deal(0)
        one.second()
        one.first()
        for waits in in_use.values():
            waits()
        in_use.clear()
        for kind in range(2):
            one.deal_sent(kind)
        one.exchange_sent()
        two.exchange_sent()
        one.settle()
        one.terms_got()

    @pl.when(section == 1)
    def _():
        two.set_up()
        cotangents()
        pl.semaphore_wait(barrier, len(greeted))
        two.forward_start()
        two.forward()
        two.backward()
        for kind in range(3):
            two.deal(kind)
        two.clear_tail()
        two.expand()
        two.second()
        two.squeeze()
        two.task_terms()
        two.first()
        one.deal(2)
        one.clear_tail()
        one.expand()
        one.task_terms()
        one.squeeze()
        for waits in in_use.values():
            waits()
        one.deal_sent(2)
        for kind in range(3):
            two.deal_sent(kind)
        two.settle()
        two.terms_got()


def result_kernel(plan, *refs):
    (
        count_ref, first, second, squeeze, expand, task, pooled, grads, norms, totals,
        first_out, second_out, squeeze_out, expand_out, task_out, feature_out, input_out,
        gain_out, shift_out, narrow_gain_out, narrow_shift_out, rms_out,
    ) = refs
    mates, tasks, c = plan["mates"], plan["tasks"], plan["channels"]
    section = lax.axis_index("section")
    live, micro = plan["live"], plan["micro"]
    images_of = []
    before = jnp.int32(micro)
    for k in range(micro):
        double = count_ref[0, k] >= 2
        images_of.append(jnp.where(double, before, jnp.int32(-1)))
        before = before + jnp.where(double, jnp.int32(1), jnp.int32(0))

    def aligned(values, image, rows, used):
        start = image * rows
        values = pltpu.roll(values, values.shape[0] - start, 0) if start else values
        inside = lax.broadcasted_iota(jnp.int32, (8, c), 0) < used
        return jnp.where(inside, values[:8], 0.0)

    def by_slot(values, rows, used, store):
        two = [aligned(values, micro, rows, used), aligned(values, micro + 1, rows, used)]
        for k in range(micro):
            store(2 * k, aligned(values, k, rows, used))
            which = images_of[k]
            store(
                2 * k + 1,
                jnp.where(which == micro, two[0], jnp.where(which == micro + 1, two[1], 0.0)),
            )

    def place_out(high, across, images, leading):
        per_row = images * across
        for index in range(1 + tasks):
            for h in range(plan["high"]):

                def store(slot, values):
                    input_out[index, slot, h] = values

                if h < high:
                    by_slot(grads[index, pl.ds(h * per_row, per_row), :], across, across, store)
                else:
                    for slot in range(2 * micro):
                        store(slot, jnp.zeros((8, c), jnp.float32))
            for h in range(plan["high"] // 2):

                def store_feature(slot, values):
                    feature_out[index, slot, h] = values[: plan["across"] // 2].astype(
                        jnp.bfloat16
                    )

                if h < high // 2:
                    count = 8 * (across // 2)
                    by_slot(
                        pooled[index, pl.ds(h * count, count), :].astype(jnp.float32),
                        across // 2, across // 2, store_feature,
                    )
                else:
                    for slot in range(2 * micro):
                        store_feature(slot, jnp.zeros((8, c), jnp.float32))
        cells = float(high * across // 4 * c)
        live_total = jnp.sum(totals[0, pl.ds(0, micro), pl.ds(0, 1)], axis=0, keepdims=True)
        lane = lax.broadcasted_iota(jnp.int32, (1, 1 + tasks), 1)
        result = jnp.zeros((1, 1 + tasks), jnp.float32)
        for index in range(1 + tasks):
            square = jnp.sum(totals[1, pl.ds(index, 1), :], axis=1, keepdims=True)
            result = jnp.where(lane == index, jnp.sqrt(square / (live_total * cells)), result)
        rms_out[...] = result
        for index in range(NORMS):
            shift_sum = jnp.sum(norms[index, pl.ds(0, micro), :], axis=0, keepdims=True)
            gain_sum = jnp.sum(norms[index, pl.ds(micro, micro), :], axis=0, keepdims=True)
            if index < NARROW:
                gain_out[pl.ds(index, 1), :] = gain_sum
                shift_out[pl.ds(index, 1), :] = shift_sum
            else:
                narrow_gain_out[pl.ds(index - NARROW, 1), :] = gain_sum
                narrow_shift_out[pl.ds(index - NARROW, 1), :] = shift_sum

    @pl.when((pl.program_id(0) == 0) & (section == 0))
    def _():
        place_out(plan["high"], plan["across"], live, True)

    @pl.when((pl.program_id(0) == 0) & (section == 1))
    def _():
        place_out(plan["high"] // 2, plan["across"] // 2, 8, False)

    for terms, target in (
        (first, first_out), (second, second_out), (squeeze, squeeze_out),
        (expand, expand_out), (task, task_out),
    ):
        count, width = terms.shape[-2:]
        per_row = width // 128
        for lane in range(per_row):
            at = pl.ds(lane * 128, 128)
            if len(terms.shape) == 2:
                summed = terms[:, at]
            else:
                summed = terms[0, :, at].astype(jnp.float32)
                for place in range(1, mates):
                    summed = summed + terms[place, :, at].astype(jnp.float32)
            target[pl.ds(lane, count, stride=per_row), :] = summed


def gathered_shards(
    stream_in, image_count, out_grad, first_conv, second_conv, squeeze, expand, task_conv,
    norm_gain, norm_shift, squeeze_gain, squeeze_shift,
):
    maps, images, high, across, c = stream_in.shape
    micro = image_count.shape[1]
    tasks = maps - 1
    groups = lax.axis_size("dp")
    mates = 4
    lines = groups // mates
    live = images - 2
    n = high * live * across
    wide_n = 256
    plan = {
        "lines": lines, "mates": mates, "tasks": tasks, "channels": c,
        "high": high, "across": across, "live": live, "wide": wide_n, "micro": micro,
    }
    conv_rows = c // groups
    task_rows = tasks * c // groups
    bf16, f32 = jnp.bfloat16, jnp.float32
    vmem = pl.BlockSpec(memory_space=pltpu.VMEM)
    whole = pl.BlockSpec(memory_space=pl.ANY)
    shapes = (
        (conv_rows, TAPS * c), (conv_rows, TAPS * c), (task_rows, 2 * c), (task_rows, c),
        (task_rows, TAPS * c),
    )
    formed = (True, True, False, False, True)
    small = 64
    single_rows = (2 + tasks) * c // lines
    out_shape = (
        [
            jax.ShapeDtypeStruct((maps, small, c), bf16),
            jax.ShapeDtypeStruct((maps, n, c), f32),
            jax.ShapeDtypeStruct((NORMS, 8, c), f32),
            jax.ShapeDtypeStruct((2, 8, c), f32),
            jax.ShapeDtypeStruct((8, lines, n, c), bf16),
            jax.ShapeDtypeStruct((8, lines, small, c), bf16),
            jax.ShapeDtypeStruct((lines, single_rows, wide_n), bf16),
            jax.ShapeDtypeStruct((lines, single_rows, 128), bf16),
            jax.ShapeDtypeStruct((lines, mates * task_rows, 2 * n), bf16),
            jax.ShapeDtypeStruct((lines, mates * task_rows, 2 * small), bf16),
        ]
        + [
            jax.ShapeDtypeStruct((4, mates, lines, n, c), bf16),
            jax.ShapeDtypeStruct((4, mates, lines, small, c), bf16),
            jax.ShapeDtypeStruct((mates, lines, 2 * conv_rows + task_rows, wide_n), bf16),
            jax.ShapeDtypeStruct((mates, lines, 2 * conv_rows + task_rows, 128), bf16),
            jax.ShapeDtypeStruct((1 + 2 * tasks, small, c), bf16),
        ]
        + [
            jax.ShapeDtypeStruct(shape, f32) if whole_terms
            else jax.ShapeDtypeStruct((mates,) + shape, bf16)
            for shape, whole_terms in zip(shapes, formed)
        ]
    )
    row = live * across
    scratch = [
        pltpu.VMEM(shape, dtype)
        for shape, dtype in (
            ((c, TAPS * c), bf16),
            ((c, TAPS * c), bf16),
            ((tasks, c, 2 * c), bf16),
            ((tasks, c, c), bf16),
            ((tasks, c, TAPS * c), bf16),
            ((NORMS, 1, c), f32),
            ((NORMS, 1, c), f32),
            ((maps, n, c), bf16),
            ((maps, small, c), bf16),
            ((maps, 16, c), f32),
            ((maps, small, c), bf16),
            ((maps, small, c), bf16),
            ((micro, row, c), f32),
            (((high + 2) * row, 3 * c), bf16),
            ((NORMS, n, c), f32),
            ((NORMS, n, c), f32),
            ((maps, n, c), f32),
            ((n, c), f32),
            ((n, c), bf16),
            ((tasks, n, c), bf16),
            ((tasks, n, c), bf16),
            ((4, n, c), f32),
            ((n, c), f32),
            ((3, row, c), f32),
            ((NORMS, micro, c), f32),
            ((4, 8, c), f32),
            ((8, c), f32),
            ((maps, 1, c), f32),
            ((c // 128, row, 128), f32),
            ((2 * n, c), f32),
            ((2 + tasks, c, wide_n), bf16),
            ((tasks, c, 2 * n), bf16),
            ((3, 2, 4, 2, 8, c), f32),
            ((4, 2, 4, 3, 8, c), f32),
            ((2, 2, 4, 4, 8, c), f32),
            ((2, lines, wide_n, c), bf16),
            ((2, lines, conv_rows, wide_n), bf16),
            ((3 * c // lines, lines * wide_n), bf16),
            ((2, conv_rows, TAPS * c), f32),
            ((mates * task_rows, 2 * c), bf16),
        )
    ] + [
        pltpu.SemaphoreType.DMA(shape)
        for shape in (
            (4 + tasks,), (GROUPS_OF_SUMS, 2), (GROUPS_OF_SUMS, 2), (2 * maps,), (2 * maps,),
            (2, NORMS, 4), (2, NORMS, 2), (2, 8, mates), (2, 8), (2, 4), (1 + 2 * tasks,),
            (1 + 2 * tasks,), (1,), (1,), (5, tasks, lines), (2, 5),
            (2, 3, mates), (2, 3), (2, 7, mates),
            (7, mates), (7,), (4 + tasks * lines,),
        )
    ]
    results = pl.pallas_call(
        functools.partial(main_kernel, plan),
        out_shape=out_shape,
        in_specs=[pl.BlockSpec(memory_space=pltpu.SMEM)] + [vmem] * 6 + [whole] * 5,
        out_specs=[vmem] * 4 + [whole] * 16,
        scratch_shapes=scratch,
        compiler_params=pltpu.CompilerParams(
            collective_id=1, has_side_effects=True, vmem_limit_bytes=62 * 2**20
        ),
        name="blocks",
    )(
        image_count, stream_in, out_grad, norm_gain[0], norm_shift[0], squeeze_gain[0],
        squeeze_shift[0], first_conv[0], second_conv[0], squeeze[0], expand[0], task_conv[0],
    )
    pooled, grads, norms, totals = results[:4]
    terms = results[15:]
    steps = 2

    def flat(shape):
        return jax.ShapeDtypeStruct((shape[0] * shape[1] // 128, 128), f32)

    results = pl.pallas_call(
        functools.partial(result_kernel, plan),
        grid=(steps,),
        out_shape=[flat(shape) for shape in shapes]
        + [
            jax.ShapeDtypeStruct((maps, images, high // 2, across // 2, c), bf16),
            jax.ShapeDtypeStruct((maps, images, high, across, c), f32),
            jax.ShapeDtypeStruct((NARROW, c), f32),
            jax.ShapeDtypeStruct((NARROW, c), f32),
            jax.ShapeDtypeStruct((tasks, c), f32),
            jax.ShapeDtypeStruct((tasks, c), f32),
            jax.ShapeDtypeStruct((1, maps), f32),
        ],
        in_specs=[pl.BlockSpec(memory_space=pltpu.SMEM)]
        + [
            pl.BlockSpec((shape[0] // steps, shape[1]), lambda i: (i, 0)) if whole_terms
            else pl.BlockSpec((mates, shape[0] // steps, shape[1]), lambda i: (0, i, 0))
            for shape, whole_terms in zip(shapes, formed)
        ]
        + [vmem] * 4,
        out_specs=[
            pl.BlockSpec((shape[0] // steps * shape[1] // 128, 128), lambda i: (i, 0))
            for shape in shapes
        ]
        + [vmem] * 7,
        compiler_params=pltpu.CompilerParams(vmem_limit_bytes=62 * 2**20),
        name="results",
    )(image_count, *terms, pooled, grads, norms, totals)
    first_g, second_g, squeeze_g, expand_g, task_g = (
        grad.reshape(1, -1) for grad in results[:5]
    )
    feature_out, input_out, gain_g, shift_g, narrow_gain_g, narrow_shift_g, rms = results[5:]
    return (
        feature_out[None], input_out[None], first_g, second_g, squeeze_g, expand_g, task_g,
        gain_g[None], shift_g[None], narrow_gain_g[None], narrow_shift_g[None], rms,
    )


def solution(mesh):
    groups = mesh.shape["dp"]
    whole_tiles = groups == 4 * 4
    return jax.shard_map(
        gathered_shards if whole_tiles else shards,
        mesh=mesh,
        in_specs=(
            P(None, "dp", None, None, None),
            P("dp", None),
            P(None, "dp", None, None, None),
            P("section", None, None),
            P("section", None, None),
            P("section", None, None, None),
            P("section", None, None, None),
            P("section", None, None, None),
            P("section", None, None),
            P("section", None, None),
            P("section", None, None),
            P("section", None, None),
        ),
        out_specs=(
            P("section", None, "dp", None, None, None),
            P("section", None, "dp", None, None, None),
            P("section", "dp"),
            P("section", "dp"),
            P("section", "dp"),
            P("section", "dp"),
            P("section", "dp"),
            P("section", None, None),
            P("section", None, None),
            P("section", None, None),
            P("section", None, None),
            P("section", None),
        ),
        check_vma=False,
    )
```

```python
import functools
import types

import jax
import jax.numpy as jnp
from jax import lax
from jax.experimental import pallas as pl
from jax.experimental.pallas import tpu as pltpu
from jax.sharding import PartitionSpec as P

EPSILON = 1e-05
SUM_ROWS = 40


def stages_of(size):
    stages = []
    stride = 1
    while stride < size:
        radix = next(r for r in (4, 2, 3, 5, 7, size // stride) if (size // stride) % r == 0)
        stages.append((radix, stride))
        stride *= radix
    return stages


def sum_kernel(stages, own_ref, out_ref, *scratch):
    slots, (send_sem, recv_sem) = scratch[: len(stages)], scratch[len(stages) :]
    section = lax.axis_index("section")
    me = lax.axis_index("dp")
    barrier = pltpu.get_barrier_semaphore()
    peers = []
    for radix, stride in stages:
        digit = lax.rem(me // stride, radix)
        group = [
            me + (lax.rem(digit + step, radix) - digit) * stride for step in range(1, radix)
        ]
        peers.append((digit, group))
    total = sum(len(group) for _, group in peers)
    for _, group in peers:
        for peer in group:
            pl.semaphore_signal(
                barrier, inc=1, device_id=(section, peer), device_id_type=pl.DeviceIdType.MESH
            )
    pl.semaphore_wait(barrier, total)
    for index, (radix, stride) in enumerate(stages):
        digit, group = peers[index]
        held = slots[index]
        held[digit] = own_ref[...] if index == 0 else out_ref[...]
        copies = []
        for step, peer in enumerate(group):
            copy = pltpu.make_async_remote_copy(
                src_ref=held.at[digit],
                dst_ref=held.at[digit],
                send_sem=send_sem.at[index, step],
                recv_sem=recv_sem.at[index, step],
                device_id=(section, peer),
                device_id_type=pl.DeviceIdType.MESH,
            )
            copy.start()
            copies.append(copy)
        for copy in copies:
            copy.wait_recv()
        summed = held[0]
        for place in range(1, radix):
            summed = summed + held[place]
        out_ref[...] = summed
        for copy in copies:
            copy.wait_send()


def sum_over_groups(rows):
    stages = stages_of(lax.axis_size("dp"))
    widest = max(radix for radix, _ in stages)
    return pl.pallas_call(
        functools.partial(sum_kernel, stages),
        out_shape=jax.ShapeDtypeStruct(rows.shape, jnp.float32),
        in_specs=[pl.BlockSpec(memory_space=pltpu.VMEM)],
        out_specs=pl.BlockSpec(memory_space=pltpu.VMEM),
        scratch_shapes=[pltpu.VMEM((radix,) + rows.shape, jnp.float32) for radix, _ in stages]
        + [
            pltpu.SemaphoreType.DMA((len(stages), widest)),
            pltpu.SemaphoreType.DMA((len(stages), widest)),
        ],
        compiler_params=pltpu.CompilerParams(collective_id=0, has_side_effects=True),
        name="group_sum",
    )(rows)


def from_behind(shard, axis, by):
    size = lax.axis_size(axis)
    pairs = [(i, i + by) for i in range(size) if 0 <= i + by < size]
    return lax.ppermute(shard, axis, pairs)


def broadcast_rows(vector):
    return vector[..., None, None, None, :]


def affine_rows(normed, scale_by, offset_by):
    return normed * broadcast_rows(scale_by) + broadcast_rows(offset_by)


def silu_slope(active):
    sigmoid_of = jax.nn.sigmoid(active)
    return sigmoid_of * (1.0 + active * (1.0 - sigmoid_of))


def pixel_sums(values, pixel_weight):
    weighted = values * pixel_weight
    return jnp.stack(
        [jnp.sum(weighted, axis=(-4, -3, -2)), jnp.sum(weighted * values, axis=(-4, -3, -2))],
        axis=-2,
    )


def gradient_sums(upstream, normed, pixel_weight):
    weighted = upstream * pixel_weight
    return jnp.stack(
        [jnp.sum(weighted, axis=(-4, -3, -2)), jnp.sum(weighted * normed, axis=(-4, -3, -2))],
        axis=-2,
    )


def summed_members(members):
    rows = [member.reshape(-1, member.shape[-1]) for member in members]
    used = sum(row.shape[0] for row in rows)
    packed = jnp.concatenate(
        rows + [jnp.zeros((SUM_ROWS - used, rows[0].shape[-1]), jnp.float32)], axis=0
    )
    summed = sum_over_groups(packed)
    results = []
    offset = 0
    for member, row in zip(members, rows):
        results.append(summed[offset : offset + row.shape[0]].reshape(member.shape))
        offset += row.shape[0]
    return results


def normalize(values, moments, counted):
    average = moments[..., 0, :] / counted
    spread = moments[..., 1, :] / counted - average * average
    inverse = lax.rsqrt(spread + EPSILON)
    return ((values - broadcast_rows(average)) * broadcast_rows(inverse), inverse)


def norm_backward(upstream, normed, inverse, scale_by, sums, counted, pixel_weight):
    shift_part = broadcast_rows(sums[..., 0, :])
    scale_part = broadcast_rows(sums[..., 1, :])
    return (
        broadcast_rows(inverse * scale_by)
        * (upstream - (shift_part + normed * scale_part) / broadcast_rows(counted))
        * pixel_weight
    )


def window_blocks(values):
    leading = values.shape[:-3]
    height, breadth, channels = values.shape[-3:]
    return values.reshape(leading + (height // 2, 2, breadth // 2, 2, channels))


def soft_pool_blocks(blocks):
    summit = jnp.max(blocks, axis=(-4, -2), keepdims=True)
    return summit + jnp.log(jnp.mean(jnp.exp(blocks - summit), axis=(-4, -2), keepdims=True))


def soft_pool(values):
    pooled = soft_pool_blocks(window_blocks(values))
    return pooled.reshape(
        values.shape[:-3] + (values.shape[-3] // 2, values.shape[-2] // 2, values.shape[-1])
    )


def pool_back(upstream, values):
    blocks = window_blocks(values)
    pooled = soft_pool_blocks(blocks)
    weight_share = jnp.exp(blocks - pooled) * 0.25
    spread = upstream.reshape(pooled.shape) * weight_share
    return spread.reshape(values.shape)


def patch_columns(frames):
    height, breadth = (frames.shape[-3], frames.shape[-2])
    padding = [(0, 0)] * (frames.ndim - 3) + [(1, 1), (1, 1), (0, 0)]
    padded = jnp.pad(frames, padding)
    return jnp.concatenate(
        [
            padded[..., down_shift : down_shift + height, side_shift : side_shift + breadth, :]
            for down_shift in range(3)
            for side_shift in range(3)
        ],
        axis=-1,
    )


def columns_back(grad_columns, channels):
    height, breadth = (grad_columns.shape[-3], grad_columns.shape[-2])
    leading = [(0, 0)] * (grad_columns.ndim - 3)
    summed = None
    for tap_index in range(9):
        down_shift, side_shift = (tap_index // 3, tap_index % 3)
        piece_of = grad_columns[..., tap_index * channels : (tap_index + 1) * channels]
        placed = jnp.pad(
            piece_of, leading + [(down_shift, 2 - down_shift), (side_shift, 2 - side_shift), (0, 0)]
        )
        summed = placed if summed is None else summed + placed
    return summed[..., 1 : height + 1, 1 : breadth + 1, :]


def live_rows(pixel_weight, channels):
    live = jnp.sum(pixel_weight, axis=(-4, -3, -2, -1))
    return jnp.broadcast_to(live[:, None], (live.shape[0], channels))


def section_forward(frames, pixel_weight, weights):
    (
        first_conv,
        second_conv,
        squeeze,
        expand,
        task_conv,
        norm_gain,
        norm_shift,
        squeeze_gain,
        squeeze_shift,
    ) = weights
    channels = frames.shape[-1]
    tasks = squeeze.shape[0]
    input_columns = patch_columns(frames[0])
    first_pre = jnp.einsum(
        "mshwk,ok->mshwo", input_columns, first_conv, preferred_element_type=jnp.float32
    )
    first_moments = summed_members(
        [pixel_sums(first_pre, pixel_weight), live_rows(pixel_weight, channels)]
    )
    counted = first_moments[1] * (frames.shape[-3] * frames.shape[-2])
    first_normed, first_inverse = normalize(first_pre, first_moments[0], counted)
    first_output = jax.nn.silu(affine_rows(first_normed, norm_gain[0], norm_shift[0]))
    rounded_first = (first_output).astype(jnp.bfloat16)
    middle_columns = patch_columns(rounded_first)
    second_pre = jnp.einsum(
        "mshwk,ok->mshwo", middle_columns, second_conv, preferred_element_type=jnp.float32
    )
    earlier = frames[1:]
    narrow = jnp.einsum(
        "mshwc,trc->tmshwr",
        rounded_first,
        squeeze[:, :, :channels],
        preferred_element_type=jnp.float32,
    ) + jnp.einsum(
        "tmshwc,trc->tmshwr", earlier, squeeze[:, :, channels:], preferred_element_type=jnp.float32
    )
    middle_moments = summed_members([pixel_sums(second_pre, pixel_weight), pixel_sums(narrow, pixel_weight)])
    second_normed, second_inverse = normalize(second_pre, middle_moments[0], counted)
    narrow_normed, narrow_inverse = normalize(narrow, middle_moments[1], counted)
    shared_out = jax.nn.silu(affine_rows(second_normed, norm_gain[1], norm_shift[1]))
    rounded_hidden = jax.nn.silu(affine_rows(narrow_normed, squeeze_gain[:, None], squeeze_shift[:, None])).astype(
        jnp.bfloat16
    )
    widened = jnp.einsum(
        "tmshwr,tcr->tmshwc", rounded_hidden, expand, preferred_element_type=jnp.float32
    )
    mask_moments = summed_members([pixel_sums(widened, pixel_weight)])
    widened_normed, widened_inverse = normalize(widened, mask_moments[0], counted)
    task_mask = jax.nn.sigmoid(
        affine_rows(widened_normed, norm_gain[2 : 2 + tasks][:, None], norm_shift[2 : 2 + tasks][:, None])
    )
    rounded_attended = (task_mask * shared_out).astype(jnp.bfloat16)
    attended_columns = patch_columns(rounded_attended)
    task_pre = jnp.einsum(
        "tmshwk,tok->tmshwo", attended_columns, task_conv, preferred_element_type=jnp.float32
    )
    task_moments = summed_members([pixel_sums(task_pre, pixel_weight)])
    task_normed, task_inverse = normalize(task_pre, task_moments[0], counted)
    task_out = jax.nn.silu(
        affine_rows(task_normed, norm_gain[2 + tasks :][:, None], norm_shift[2 + tasks :][:, None])
    )
    pooled = jnp.concatenate([soft_pool(shared_out)[None], soft_pool(task_out)], axis=0)
    kept_state = (
        frames,
        counted,
        first_normed,
        first_inverse,
        rounded_first,
        second_normed,
        second_inverse,
        narrow_normed,
        narrow_inverse,
        rounded_hidden,
        widened_normed,
        widened_inverse,
        rounded_attended,
        task_normed,
        task_inverse,
    )
    return (pooled, kept_state)


def section_backward(upstream, kept_state, pixel_weight, squares, weights):
    (
        first_conv,
        second_conv,
        squeeze,
        expand,
        task_conv,
        norm_gain,
        norm_shift,
        squeeze_gain,
        squeeze_shift,
    ) = weights
    (
        frames,
        counted,
        first_normed,
        first_inverse,
        rounded_first,
        second_normed,
        second_inverse,
        narrow_normed,
        narrow_inverse,
        rounded_hidden,
        widened_normed,
        widened_inverse,
        rounded_attended,
        task_normed,
        task_inverse,
    ) = kept_state
    channels = frames.shape[-1]
    tasks = squeeze.shape[0]
    task_gain = norm_gain[2 + tasks :][:, None]
    mask_gain = norm_gain[2 : 2 + tasks][:, None]
    task_active = affine_rows(task_normed, task_gain, norm_shift[2 + tasks :][:, None])
    task_out = jax.nn.silu(task_active)
    grad_task_act = pool_back(upstream[1:], task_out) * silu_slope(task_active)
    task_sums, square_all = summed_members(
        [gradient_sums(grad_task_act, task_normed, pixel_weight), squares]
    )
    grad_task = norm_backward(
        grad_task_act, task_normed, task_inverse, task_gain, task_sums, counted, pixel_weight
    ).astype(jnp.bfloat16)
    attended_columns = patch_columns(rounded_attended)
    task_conv_grad = jnp.einsum(
        "tmshwo,tmshwk->tok", grad_task, attended_columns, preferred_element_type=jnp.float32
    )
    grad_attended = (
        columns_back(
            jnp.einsum(
                "tmshwo,tok->tmshwk", grad_task, task_conv, preferred_element_type=jnp.float32
            ),
            channels,
        )

    )
    second_active = affine_rows(second_normed, norm_gain[1], norm_shift[1])
    shared_out = jax.nn.silu(second_active)
    task_mask = jax.nn.sigmoid(affine_rows(widened_normed, mask_gain, norm_shift[2 : 2 + tasks][:, None]))
    grad_mask_act = grad_attended * shared_out * task_mask * (1.0 - task_mask)
    mask_sums = summed_members([gradient_sums(grad_mask_act, widened_normed, pixel_weight)])[0]
    grad_widened = norm_backward(
        grad_mask_act, widened_normed, widened_inverse, mask_gain, mask_sums, counted, pixel_weight
    ).astype(jnp.bfloat16)
    expand_grad = jnp.einsum(
        "tmshwc,tmshwr->tcr", grad_widened, rounded_hidden, preferred_element_type=jnp.float32
    )
    narrow_active = affine_rows(narrow_normed, squeeze_gain[:, None], squeeze_shift[:, None])
    grad_narrow_act = jnp.einsum(
        "tmshwc,tcr->tmshwr", grad_widened, expand, preferred_element_type=jnp.float32
    ) * silu_slope(narrow_active)
    grad_shared = pool_back(upstream[0], shared_out) + jnp.sum(grad_attended * task_mask, axis=0)
    grad_second_act = grad_shared * silu_slope(second_active)
    second_sums, narrow_sums = summed_members(
        [
            gradient_sums(grad_second_act, second_normed, pixel_weight),
            gradient_sums(grad_narrow_act, narrow_normed, pixel_weight),
        ]
    )
    grad_second = norm_backward(
        grad_second_act,
        second_normed,
        second_inverse,
        norm_gain[1],
        second_sums,
        counted,
        pixel_weight,
    ).astype(jnp.bfloat16)
    grad_narrow = norm_backward(
        grad_narrow_act,
        narrow_normed,
        narrow_inverse,
        squeeze_gain[:, None],
        narrow_sums,
        counted,
        pixel_weight,
    ).astype(jnp.bfloat16)
    middle_columns = patch_columns(rounded_first)
    second_conv_grad = jnp.einsum(
        "mshwo,mshwk->ok", grad_second, middle_columns, preferred_element_type=jnp.float32
    )
    earlier = frames[1:]
    squeeze_grad = jnp.concatenate(
        [
            jnp.einsum(
                "tmshwr,mshwc->trc", grad_narrow, rounded_first, preferred_element_type=jnp.float32
            ),
            jnp.einsum(
                "tmshwr,tmshwc->trc", grad_narrow, earlier, preferred_element_type=jnp.float32
            ),
        ],
        axis=-1,
    )
    grad_joined = jnp.einsum(
        "tmshwr,trc->tmshwc", grad_narrow, squeeze, preferred_element_type=jnp.float32
    )
    grad_first_out = (
        columns_back(
            jnp.einsum(
                "mshwo,ok->mshwk", grad_second, second_conv, preferred_element_type=jnp.float32
            ),
            channels,
        )
        + jnp.sum(grad_joined[..., :channels], axis=0)
    )
    grad_earlier = grad_joined[..., channels:]
    first_active = affine_rows(first_normed, norm_gain[0], norm_shift[0])
    grad_first_act = grad_first_out * silu_slope(first_active)
    first_sums = summed_members([gradient_sums(grad_first_act, first_normed, pixel_weight)])[0]
    grad_first = norm_backward(
        grad_first_act, first_normed, first_inverse, norm_gain[0], first_sums, counted, pixel_weight
    ).astype(jnp.bfloat16)
    input_columns = patch_columns(frames[0])
    first_conv_grad = jnp.einsum(
        "mshwo,mshwk->ok", grad_first, input_columns, preferred_element_type=jnp.float32
    )
    grad_shared_in = (
        columns_back(
            jnp.einsum("mshwo,ok->mshwk", grad_first, first_conv, preferred_element_type=jnp.float32),
            channels,
        )

    )
    grad_frames = jnp.concatenate([grad_shared_in[None], grad_earlier], axis=0)
    first_norm, second_norm, mask_norm, task_norm, narrow_norm = (
        jnp.sum(sums, axis=-3)
        for sums in (first_sums, second_sums, mask_sums, task_sums, narrow_sums)
    )
    norm_rows = jnp.concatenate(
        [first_norm[None], second_norm[None], mask_norm, task_norm], axis=0
    )
    weight_terms = (first_conv_grad, second_conv_grad, squeeze_grad, expand_grad, task_conv_grad)
    norm_terms = (norm_rows[:, 1], norm_rows[:, 0], narrow_norm[:, 1], narrow_norm[:, 0])
    return (grad_frames, weight_terms, norm_terms, square_all)


def shards(
    stream_in,
    image_count,
    out_grad,
    first_conv,
    second_conv,
    squeeze,
    expand,
    task_conv,
    norm_gain,
    norm_shift,
    squeeze_gain,
    squeeze_shift,
):
    weights = (
        first_conv[0],
        second_conv[0],
        squeeze[0],
        expand[0],
        task_conv[0],
        norm_gain[0],
        norm_shift[0],
        squeeze_gain[0],
        squeeze_shift[0],
    )
    maps_count, images, height, breadth, channels = stream_in.shape
    micro_count = image_count.shape[1]
    slot_count = images // micro_count
    leading_section = lax.axis_index("section") == 0
    live = jnp.arange(slot_count)[None, :] < image_count[0][:, None]
    pixel_weight = live.astype(jnp.float32)[:, :, None, None, None]

    def by_micro(maps):
        return maps.reshape((maps_count, micro_count, slot_count) + maps.shape[2:])

    def whole_pool(pooled):
        masked = pooled * pixel_weight
        squares = jnp.sum(masked * masked, axis=(1, 2, 3, 4, 5))
        return masked.astype(jnp.bfloat16), jnp.broadcast_to(squares[:, None], (maps_count, channels))

    one_pooled, one_state = section_forward(by_micro(stream_in), pixel_weight, weights)
    one_features, one_squares = whole_pool(one_pooled)
    arrived = from_behind(one_features, "section", 1)
    two_pooled, two_state = section_forward(arrived, pixel_weight, weights)
    two_features, two_squares = whole_pool(two_pooled)
    two_upstream = by_micro(out_grad).astype(jnp.float32) * pixel_weight
    two_back = section_backward(two_upstream, two_state, pixel_weight, two_squares, weights)
    sendback = two_back[0].astype(jnp.bfloat16)
    returned = from_behind(sendback, "section", -1)
    one_upstream = returned.astype(jnp.float32) * pixel_weight
    one_back = section_backward(one_upstream, one_state, pixel_weight, one_squares, weights)

    half = ((0, 0),) * 3 + ((0, height // 4), (0, breadth // 4), (0, 0))
    full = ((0, 0),) * 3 + ((0, height // 2), (0, breadth // 2), (0, 0))
    feature_out = jnp.where(leading_section, one_features, jnp.pad(two_features, half))
    feature_out = feature_out.reshape((maps_count, images) + feature_out.shape[3:])
    recorded = lax.optimization_barrier(sendback).astype(jnp.float32)
    input_grad_out = jnp.where(leading_section, one_back[0], jnp.pad(recorded, full))
    input_grad_out = input_grad_out.reshape((maps_count, images) + input_grad_out.shape[3:])
    reduced = tuple(
        lax.psum_scatter(
            jnp.where(leading_section, one, two).reshape(-1).astype(jnp.bfloat16),
            "dp",
            scatter_dimension=0,
            tiled=True,
        ).astype(jnp.float32)
        for one, two in zip(one_back[1], two_back[1])
    )
    norm_sums = tuple(
        jnp.where(leading_section, one, two) for one, two in zip(one_back[2], two_back[2])
    )
    live_images = jnp.sum(one_state[1][:, 0]) / (height * breadth)
    feature_pixels = jnp.where(leading_section, height * breadth // 4, height * breadth // 16)
    root_square = jnp.sqrt(
        jnp.where(leading_section, one_back[3], two_back[3])[:, 0]
        / (live_images * feature_pixels * channels)
    )
    return (
        feature_out[None],
        input_grad_out[None],
        reduced[0][None],
        reduced[1][None],
        reduced[2][None],
        reduced[3][None],
        reduced[4][None],
        norm_sums[0][None],
        norm_sums[1][None],
        norm_sums[2][None],
        norm_sums[3][None],
        root_square[None],
    )


TAPS = 9
MESH = pl.DeviceIdType.MESH
FIRST, SECOND, MASK, TASK, NARROW = 0, 1, 2, 5, 8
NORMS = 11
(F_FIRST, F_SECOND, B_FIRST, F_NARROW, F_MASK, F_TASK, B_NARROW, B_TASK, B_MASK) = range(9)
GROUPS_OF_SUMS = 9
(
    P_FIRST, P_FIRST_DONE, P_NARROW_DONE, P_MASK_DONE, P_ATTENDED, P_TASKED, P_SUMMED,
    P_TASK_DONE, P_BTASK_SUMS, P_BTASK_DONE, P_BMASK_START, P_BMASK_SUMS, P_BMASK_DONE,
    P_BNARROW_DONE, P_BFIRST_START, P_BFIRST_SUMS, P_BFIRST_DONE,
) = range(17)


def sigmoid(active):
    return 0.5 * jnp.tanh(0.5 * active) + 0.5


def silu_parts(active):
    sigmoid_of = sigmoid(active)
    return active * sigmoid_of, sigmoid_of * (1.0 + active * (1.0 - sigmoid_of))


def dot_nt(left, right):
    return lax.dot_general(
        left, right, (((1,), (1,)), ((), ())), preferred_element_type=jnp.float32
    )


def dot_nn(left, right):
    return lax.dot_general(
        left, right, (((1,), (0,)), ((), ())), preferred_element_type=jnp.float32
    )


def loop(count, body, start=0):
    lax.fori_loop(start, count, lambda i, _: (body(i), 0)[1], 0)


def main_kernel(plan, *refs):
    (
        count_ref, stream, cotangent, gain_in, shift_in, narrow_gain, narrow_shift,
        w1, w2, sq, ex, tc,
        o_ref, ig_ref, norm_ref, total_ref, a_one, a_two, d_one, d_two, pair_one, pair_two,
        q_one, q_two, dq_one, dq_two, beside, r_first, r_second, r_squeeze, r_expand, r_task,
        w1s, w2s, sqs, exs, tcs, gain, shift, x_one, x_two, og_ref, sg_in, sg_out,
        masks, pad, xh, aux, share, p_act, ub, ab, nb, dr, gp, rows, inv, tot, counts, osq,
        wide, tbuf, turned, joint, slots_one, slots_three, slots_four,
        held, dbuf, cols, out, stage_flat,
        w_load, sync_send, sync_recv, h_send, h_recv, a_send, a_recv, v_send, v_recv, q_recv, s_send, s_recv, u_send, u_recv,
        d_send, d_recv, dq_send, dq_recv, t_send, t_own, r_recv, load_sem,
    ) = refs
    lines, mates, tasks, c = plan["lines"], plan["mates"], plan["tasks"], plan["channels"]
    high, across, live = plan["high"], plan["across"], plan["live"]
    hc = c // 2
    active_of = dr.at[0]
    micro = masks.shape[0]
    section = lax.axis_index("section")
    other = 1 - section
    me = lax.axis_index("dp")
    z, j = me // mates, lax.rem(me, mates)
    unit = c // lines
    pieces = unit // mates
    task_rows = tasks * c // lines
    kinds = ((0, unit), (unit, unit), (0, task_rows), None, (2 * unit, task_rows))

    def plane_tasks(line):
        return (task_rows * line) // c, (task_rows * (line + 1) - 1) // c

    def plane_needs(line, task):
        first, last = plane_tasks(line)
        return (first <= task) & (task <= last)

    def device_needs(device, task):
        own = task_rows // mates
        return ((own * device) // c <= task) & (task <= (own * device + own - 1) // c)

    def mate(step):
        return z * mates + lax.rem(j + step, mates)

    def liner(step):
        return lax.rem(z + step, lines) * mates + j

    def remote(source, target, send, recv, to, device):
        return pltpu.make_async_remote_copy(
            src_ref=source, dst_ref=target, send_sem=send, recv_sem=recv,
            device_id=(to, device), device_id_type=MESH,
        )

    def got(some, recv):
        remote(some, some, sync_send.at[0, 0], recv, section, me).wait_recv()

    def sent(some, send):
        remote(some, some, send, sync_recv.at[0, 0], section, me).wait_send()

    def push(source, target, send, recv, to, device, own=None):
        same = (section == to) & (me == device)

        @pl.when(same)
        def _():
            pltpu.make_async_copy(source, target, recv if own is None else own).start()

        @pl.when(jnp.logical_not(same))
        def _():
            remote(source, target, send, recv, to, device).start()

    def pushed(some, send, to, device, own=None):
        same = (section == to) & (me == device)

        @pl.when(jnp.logical_not(same))
        def _():
            sent(some, send)

        if own is not None:

            @pl.when(same)
            def _():
                pltpu.make_async_copy(some, some, own).wait()

    def across_cores(source, target, send, recv):
        remote(source, target, send, recv, other, me).start()

    def sums_at(group):
        if group < 3:
            ref, at, count = slots_one, group, 2 if group == F_FIRST else 1
        elif group < 7:
            ref, at, count = slots_three, group - 3, 3
        else:
            ref, at, count = slots_four, group - 7, 4
        return ref.at[at], count, group

    def sums_place(group, stage, digits):
        ref, count, _ = sums_at(group)
        return ref.at[stage, digits, pl.ds(0, count)]

    def sums_send(group, stage, digit, devices):
        at = sums_at(group)[2]
        here = sums_place(group, stage, digit)
        for device in devices:
            remote(
                here, here, sync_send.at[at, stage], sync_recv.at[at, stage], section, device
            ).start()

    def sums_got(group, stage, digits):
        ref, count, at = sums_at(group)
        got(sums_place(group, stage, pl.ds(0, digits - 1)), sync_recv.at[at, stage])
        summed = ref[stage, 0, pl.ds(0, count)]
        for digit in range(1, digits):
            summed = summed + ref[stage, digit, pl.ds(0, count)]
        return summed

    def sums_start(group):
        sums_send(group, 0, j, [mate(step) for step in range(1, mates)])

    def sums_mid(group):
        ref, count, _ = sums_at(group)
        ref[1, z, pl.ds(0, count)] = sums_got(group, 0, mates)
        sums_send(group, 1, z, [liner(step) for step in range(1, lines)])

    def sums_end(group):
        count = sums_at(group)[1]
        tot[pl.ds(0, count)] = sums_got(group, 1, lines)

    def sums_sent(group):
        at = sums_at(group)[2]
        for stage, digits in enumerate((mates, lines)):
            sent(
                sums_place(group, stage, pl.ds(0, digits - 1)), sync_send.at[at, stage]
            )

    W_FIRST, W_SQUEEZE, W_SECOND, W_EXPAND, W_TASK = range(5)

    def weight_copy(index):
        if index >= W_TASK:
            source, target = tc.at[index - W_TASK], tcs.at[index - W_TASK]
        else:
            source, target = ((w1, w1s), (sq, sqs), (w2, w2s), (ex, exs))[index]
        return pltpu.make_async_copy(source, target, w_load.at[index])

    def make_block(b):
        leading = b == 0
        rows_high, rows_across, images = (
            (high, across, live) if leading else (high // 2, across // 2, 8)
        )
        per_row = images * rows_across
        n = rows_high * per_row
        wide_n = plan["wide"] if leading else 128
        pixels = float(rows_high * rows_across)
        half = per_row // 2
        source = x_one if leading else x_two
        a_ref, d_ref, pair_ref, q_ref, dq_ref = (
            (a_one, d_one, pair_one, q_one, dq_one) if leading
            else (a_two, d_two, pair_two, q_two, dq_two)
        )
        position = lax.rem(
            lax.broadcasted_iota(jnp.int32, (per_row, c), 0), jnp.int32(rows_across)
        )
        even = lax.rem(position, jnp.int32(2)) == 0
        span = pl.ds(0, n)
        used = pl.ds(0, per_row)

        def each(body):
            for h in range(rows_high):
                body(h)

        def part(h):
            return pl.ds(h * per_row, per_row)

        def shifted(values):
            left = jnp.where(position >= 1, pltpu.roll(values, 1, 0), 0.0)
            right = jnp.where(position <= rows_across - 2, pltpu.roll(values, per_row - 1, 0), 0.0)
            return [v.astype(jnp.bfloat16) for v in (left, values, right)]

        def put_pad(h, values, backward=False):
            sides = shifted(values)
            for side, v in enumerate(reversed(sides) if backward else sides):
                pad[pl.ds((h + 1) * per_row, per_row), pl.ds(side * c, c)] = v

        def conv_to(weight, store_at):
            for out in range(2):
                total_of = None
                for dy in range(3):
                    one = dot_nt(
                        pad[pl.ds(dy * per_row, n), :],
                        weight[pl.ds(out * hc, hc), pl.ds(dy * 3 * c, 3 * c)],
                    )
                    total_of = one if total_of is None else total_of + one
                store_at[:, pl.ds(out * hc, hc)] = total_of

        def conv_back_to(weight, store_at):
            for out in range(2):
                total_of = None
                for dy in range(3):
                    for side in range(3):
                        one = dot_nn(
                            pad[pl.ds((2 - dy) * per_row, n), pl.ds(side * c, c)],
                            weight[:, pl.ds((dy * 3 + side) * c + out * hc, hc)],
                        )
                        total_of = one if total_of is None else total_of + one
                store_at[:, pl.ds(out * hc, hc)] = total_of

        def write_stats(group, member, first, second):
            ref = sums_at(group)[0]
            for k in range(micro):
                weight = masks[k, used, :]
                ref[0, j, member, pl.ds(k, 1), :] = jnp.sum(first * weight, 0, keepdims=True)
                ref[0, j, member, pl.ds(micro + k, 1), :] = jnp.sum(
                    second * weight, 0, keepdims=True
                )

        def moments(group, member, values_ref):
            first = second = None
            for h in range(rows_high):
                v = values_ref[pl.ds(h * per_row, per_row), :]
                first = v if h == 0 else first + v
                second = v * v if h == 0 else second + v * v
            write_stats(group, member, first, second)

        def start(group):
            sums_start(group)

        def mid(group):
            sums_mid(group)

        def end(group):
            sums_end(group)

        def row(ref, k):
            return ref[pl.ds(k, 1), :]

        def total(member, k):
            return tot[member, pl.ds(k, 1), :]

        def norm_rows(index, member):
            mean_rows = inv_rows = None
            for k in range(micro):
                n_k = row(counts, k) * pixels
                mean = total(member, k) / n_k
                spread_of = total(member, micro + k) / n_k - mean * mean
                inverse = lax.rsqrt(spread_of + EPSILON)
                inv[index, pl.ds(k, 1), :] = inverse
                weight = masks[k, used, :]
                mean_rows = weight * mean if k == 0 else mean_rows + weight * mean
                inv_rows = weight * inverse if k == 0 else inv_rows + weight * inverse
            rows[0, used, :] = mean_rows
            rows[1, used, :] = inv_rows

        def normalized(index, h, raw):
            normed = (raw - rows[0, used, :]) * rows[1, used, :]
            xh[index, part(h), :] = normed
            return normed * gain[index] + shift[index]

        def back_rows(index, member):
            norm_ref[index] = tot[member]
            scale_rows = shift_rows = slope_rows = None
            for k in range(micro):
                n_k = row(counts, k) * pixels
                weight = masks[k, used, :]
                scale = inv[index, pl.ds(k, 1), :] * gain[index]
                by_shift = total(member, k) / n_k
                by_gain = total(member, micro + k) / n_k
                scale_rows = weight * scale if k == 0 else scale_rows + weight * scale
                shift_rows = weight * by_shift if k == 0 else shift_rows + weight * by_shift
                slope_rows = weight * by_gain if k == 0 else slope_rows + weight * by_gain
            rows[0, used, :] = scale_rows
            rows[1, used, :] = shift_rows
            rows[2, used, :] = slope_rows

        def partner(v):
            return jnp.where(even, pltpu.roll(v, per_row - 1, 0), pltpu.roll(v, 1, 0))

        def soft_pool(index, read):
            squares = None
            for pair in range(rows_high // 2):
                upper, lower = read(2 * pair), read(2 * pair + 1)
                top = jnp.maximum(upper, lower)
                top = jnp.maximum(top, partner(top))
                upper, lower = jnp.exp(upper - top), jnp.exp(lower - top)
                summed = upper + lower
                summed = summed + partner(summed)
                share[index, pl.ds(2 * pair * per_row, per_row), :] = upper / summed
                share[index, pl.ds((2 * pair + 1) * per_row, per_row), :] = lower / summed
                pooled = top + jnp.log(summed * 0.25)
                for lane in range(c // 128):
                    wide[lane, used, :] = pooled[:, lane * 128 : (lane + 1) * 128]
                pooled = jnp.concatenate(
                    [wide[lane, pl.ds(0, half, stride=2), :] for lane in range(c // 128)], axis=1
                )
                if leading:
                    kept = pooled
                    pooled = jnp.concatenate(
                        [pooled, jnp.zeros((32 - half, c), jnp.float32)], axis=0
                    )
                    o_ref[index, pl.ds(32 * pair, 32), :] = pooled.astype(jnp.bfloat16)
                else:
                    alive = lax.broadcasted_iota(jnp.int32, (half, c), 0) < live * (
                        rows_across // 2
                    )
                    kept = jnp.where(alive, pooled, 0.0)
                    o_ref[index, pl.ds(half * pair, half), :] = kept.astype(jnp.bfloat16)
                square = jnp.sum(kept * kept, 0, keepdims=True)
                squares = square if squares is None else squares + square
            osq[index] = squares
            if leading:
                across_cores(
                    o_ref.at[index], x_two.at[index], h_send.at[index], h_recv.at[index]
                )

        def widened(index, pair):
            if leading:
                upstream = sg_in[index, pl.ds(pl.multiple_of(32 * pair, 32), 32), :]
                upstream = upstream.astype(jnp.float32)[:half]
            else:
                upstream = og_ref[index]
            for lane in range(c // 128):
                piece = upstream[:, lane * 128 : (lane + 1) * 128]
                wide[lane, pl.ds(0, half, stride=2), :] = piece
                wide[lane, pl.ds(1, half, stride=2), :] = piece
            return jnp.concatenate(
                [wide[lane, used, :] for lane in range(c // 128)], axis=1
            )

        pair_at = 2 * (z // 2)
        far_at = lines - 2 - pair_at
        inner = (z == 1) | (z == 2)

        def send_shared(which):
            from_ref = shared_source(which)
            neighbour = 2 * pair_at + 1 - z
            for at, plane in enumerate((z, neighbour)):
                push(
                    from_ref, a_ref.at[which, z], a_send.at[b, which, at],
                    a_recv.at[b, which, 0], 0, plane * mates + j,
                )

        def shared_source(which):
            if leading:
                return source.at[0] if which == 0 else ub.at[span]
            return o_ref.at[0] if which == 0 else beside.at[0]

        def pair_lines(which, first):
            return a_ref.at[which, pl.ds(first, 2)]

        def relay_pair(which):
            got(pair_lines(which, 0), a_recv.at[b, which, 0])

            @pl.when(inner)
            def _():
                here = pair_lines(which, pair_at)
                remote(
                    here, here, a_send.at[b, which, 2], a_recv.at[b, which, 1], 0,
                    (lines - 1 - z) * mates + j,
                ).start()

        def relay_far(which):
            got(pair_lines(which, 0), a_recv.at[b, which, 1])

            @pl.when(inner)
            def _():
                here = pair_lines(which, far_at)
                remote(
                    here, here, a_send.at[b, which, 3], a_recv.at[b, which, 1], 0,
                    (2 * pair_at + 1 - z) * mates + j,
                ).start()

        def task_planes(task):
            first = (c * task) // task_rows
            return first, first + 1

        def task_slot(kind, task, plane):
            return 2 + 2 * kind + task - plane_tasks(plane)[0]

        def task_source(kind, task):
            if leading:
                return (
                    source.at[1 + task] if kind == 0
                    else ab.at[task, span] if kind == 1 else nb.at[task, span]
                )
            return o_ref.at[1 + task] if kind == 0 else beside.at[tasks * kind - 2 + task]

        def send_task(kind, task):
            first, last = task_planes(task)
            near = jnp.clip(z, first, last)
            passed_on = (z < first) | (z > last)
            tensor = 2 + tasks * kind + task
            push(
                task_source(kind, task), a_ref.at[task_slot(kind, task, near), z],
                a_send.at[b, tensor, 0],
                a_recv.at[b, tensor, jnp.where(passed_on, jnp.int32(0), jnp.int32(1))],
                0, near * mates + j,
            )

            @pl.when(jnp.logical_not(passed_on))
            def _():
                opposite = first + last - z
                push(
                    task_source(kind, task), a_ref.at[task_slot(kind, task, opposite), z],
                    a_send.at[b, tensor, 1], a_recv.at[b, tensor, 1], 0, opposite * mates + j,
                )

        def task_passes(task):
            first, last = task_planes(task)
            passes = []
            if first > 0:
                passes.append((first, 0, first, last))
            if last < lines - 1:
                passes.append((last, last + 1, lines - 1 - last, first))
            return passes

        def relay_task(kind, task):
            tensor = 2 + tasks * kind + task
            for plane, first, count, to_plane in task_passes(task):

                @pl.when(z == plane)
                def _():
                    some = pl.ds(first, count)
                    here = a_ref.at[task_slot(kind, task, plane), some]
                    got(here, a_recv.at[b, tensor, 0])
                    remote(
                        here, a_ref.at[task_slot(kind, task, to_plane), some],
                        a_send.at[b, tensor, 2], a_recv.at[b, tensor, 1], 0,
                        to_plane * mates + j,
                    ).start()

        def core_of(kind):
            return 0 if kind < 2 else 1

        def deliver(at, slot, task=None):
            for step in range(mates):

                def send():
                    push(
                        a_ref.at[at], q_ref.at[slot, j], v_send.at[b, at, step],
                        q_recv.at[b, slot], core_of(at), mate(step),
                    )

                if task is None:
                    send()
                else:
                    pl.when(device_needs(mate(step), task))(send)

        def delivered(at, task=None):
            for step in range(mates):

                def wait():
                    pushed(a_ref.at[0], v_send.at[b, at, step], core_of(at), mate(step))

                if task is None:
                    wait()
                else:
                    pl.when(device_needs(mate(step), task))(wait)

        def task_done(kind, task):
            tensor = 2 + tasks * kind + task
            first, last = task_planes(task)
            for plane, count in ((first, lines - first), (last, last + 1)):

                @pl.when(z == plane)
                def _():
                    got(a_ref.at[0, pl.ds(0, count)], a_recv.at[b, tensor, 1])
                    at = task_slot(kind, task, plane)
                    if kind == 2:
                        deliver(at, at - 4, task)
                    else:
                        across_cores(
                            a_ref.at[at], a_ref.at[at], v_send.at[b, at, 0], v_recv.at[b, at]
                        )

        def task_got(kind, task):
            for plane in task_planes(task):
                at = task_slot(kind, task, plane)
                if kind == 2:

                    @pl.when((z == plane) & device_needs(me, task))
                    def _():
                        got(q_ref.at[0], q_recv.at[b, at - 4])

                else:

                    @pl.when(z == plane)
                    def _():
                        got(a_ref.at[0], v_recv.at[b, at])

        def shared_got(which):
            got(q_ref.at[0], q_recv.at[b, which])

        def relays(kind):
            for task in range(tasks):
                relay_task(kind, task)

        def done(kind):
            for task in range(tasks):
                task_done(kind, task)

        def exchange_activations():
            def here(index):
                if not leading:
                    got(beside.at[0], s_recv.at[index])

            def send_tasks(kind):
                for task in range(tasks):
                    if kind:
                        here(tasks * kind - 2 + task)
                    send_task(kind, task)

            send_shared(0)
            send_tasks(0)
            here(0)
            send_shared(1)
            relay_pair(0)
            relays(0)
            relay_pair(1)
            send_tasks(1)
            relay_far(0)
            deliver(0, 0)
            done(0)
            relays(1)
            relay_far(1)
            deliver(1, 1)
            across_cores(a_ref.at[1], q_ref.at[1, j], u_send.at[b], u_recv.at[b])
            send_tasks(2)
            done(1)
            relays(2)
            done(2)

        def exchange_sent():
            one_piece = a_ref.at[0, 0]
            for which in range(2):
                for at, plane in enumerate((z, 2 * pair_at + 1 - z)):
                    pushed(one_piece, a_send.at[b, which, at], 0, plane * mates + j)

                @pl.when(inner)
                def _():
                    for at in (2, 3):
                        sent(pair_lines(which, 0), a_send.at[b, which, at])

                delivered(which)
            sent(a_ref.at[0], u_send.at[b])
            for kind in range(3):
                for task in range(tasks):
                    first, last = task_planes(task)
                    tensor = 2 + tasks * kind + task
                    near = jnp.clip(z, first, last)
                    pushed(one_piece, a_send.at[b, tensor, 0], 0, near * mates + j)

                    @pl.when((z == first) | (z == last))
                    def _():
                        pushed(
                            one_piece, a_send.at[b, tensor, 1], 0, (first + last - z) * mates + j
                        )

                    for plane, _, count, _ in task_passes(task):

                        @pl.when(z == plane)
                        def _():
                            sent(a_ref.at[0, pl.ds(0, count)], a_send.at[b, tensor, 2])

                    for plane in (first, last):

                        @pl.when(z == plane)
                        def _():
                            at = task_slot(kind, task, plane)
                            if kind == 2:
                                delivered(at, task)
                            else:
                                sent(a_ref.at[0], v_send.at[b, at, 0])

        def spread_place(kind, task, k):
            offset, _ = kinds[kind]
            if kind < 2:
                return kind, k, offset
            number = lines * task + k
            at = pl.multiple_of(offset + lax.rem(number, tasks) * unit, unit)
            return (2 if kind == 4 else 0) + task, number // tasks, at

        def spread_refs(kind):
            return (joint, pair_ref) if kind == 2 else (turned, d_ref)

        def spread_lanes(kind):
            return pl.ds(0, 2 * n if kind == 2 else wide_n)

        def spread(kind, task=0):
            from_ref, target = spread_refs(kind)
            for k in range(lines):
                index, plane, offset = spread_place(kind, task, k)
                push(
                    from_ref.at[index, pl.ds(k * unit, unit), spread_lanes(kind)],
                    target.at[z, pl.ds(offset, unit)],
                    d_send.at[kind, task, k], d_recv.at[b, kind], core_of(kind), plane * mates + j,
                )

        def spread_sent(kind, task=0):
            from_ref, _ = spread_refs(kind)
            for k in range(lines):
                _, plane, _ = spread_place(kind, task, k)
                pushed(
                    from_ref.at[0, pl.ds(k * unit, unit), spread_lanes(kind)],
                    d_send.at[kind, task, k], core_of(kind), plane * mates + j,
                )

        def spread_got(kind):
            offset, count = kinds[kind]
            got(spread_refs(kind)[1].at[:, pl.ds(offset, count)], d_recv.at[b, kind])

        def rounded(index, member, slot, target, before=None):
            back_rows(index, member)
            first = 0 if before is None else n

            def body(h):
                value = rows[0, used, :] * (
                    dr[slot, part(h), :] - rows[1, used, :] - xh[index, part(h), :] * rows[2, used, :]
                )
                if target is None:
                    xh[index, part(h), :] = value
                else:
                    tbuf[pl.ds(first + h * per_row, per_row), :] = value
                put_pad(h, value, True)

            each(body)
            if target is None:
                return
            if before is None:
                tbuf[pl.ds(n, wide_n - n), :] = jnp.zeros((wide_n - n, c), jnp.float32)
                count = wide_n
            else:
                tbuf[span, :] = before[...]
                count = 2 * n
            target[:, pl.ds(0, count)] = jnp.transpose(tbuf[pl.ds(0, count), :]).astype(jnp.bfloat16)

        def middle():
            return pad[pl.ds(per_row, n), pl.ds(c, c)]

        def beside_core(from_ref, index):
            if not leading:
                across_cores(from_ref, beside.at[index], s_send.at[index], s_recv.at[index])

        def forward_start():
            if not leading:
                got(x_two.at[0], h_recv.at[0])
            each(lambda h: put_pad(h, source[0, part(h), :].astype(jnp.float32)))
            weight_copy(W_FIRST).wait()
            conv_to(w1s, xh.at[FIRST, span])
            moments(F_FIRST, 0, xh.at[FIRST])
            start(F_FIRST)

        def forward():
            for index in range(W_SECOND, W_TASK + tasks):
                weight_copy(index).start()
            if not leading:
                for index in range(1, 1 + tasks):
                    got(x_two.at[0], h_recv.at[index])
            weight_copy(W_SQUEEZE).wait()

            def outer_narrow(task):
                xh[NARROW + task, span] = dot_nt(source[1 + task], sqs[task, :, pl.ds(c, c)])

            outer_narrow(0)
            mid(F_FIRST)
            loop(tasks, outer_narrow, 1)
            end(F_FIRST)
            counts[...] = tot[1]
            total_ref[0] = tot[1]
            norm_rows(FIRST, 0)

            def first_act(h):
                active, slope = silu_parts(normalized(FIRST, h, xh[FIRST, part(h), :]))
                aux[FIRST, part(h), :] = slope
                ub[part(h), :] = active.astype(jnp.bfloat16)
                put_pad(h, active)

            each(first_act)
            beside_core(ub.at[span], 0)

            def narrow(task):
                xh[NARROW + task, span] += dot_nt(middle(), sqs[task, :, pl.ds(0, c)])
                moments(F_NARROW, task, xh.at[NARROW + task])

            loop(tasks, narrow)
            start(F_NARROW)
            weight_copy(W_SECOND).wait()
            conv_to(w2s, xh.at[SECOND, span])
            mid(F_NARROW)
            moments(F_SECOND, 0, xh.at[SECOND])
            start(F_SECOND)
            weight_copy(W_EXPAND).wait()
            end(F_NARROW)

            def mask_of(task):
                norm_rows(NARROW + task, task)

                def act(h):
                    active, slope = silu_parts(
                        normalized(NARROW + task, h, xh[NARROW + task, part(h), :])
                    )
                    aux[NARROW + task, part(h), :] = slope
                    ab[task, part(h), :] = active.astype(jnp.bfloat16)

                each(act)
                beside_core(ab.at[task, span], 1 + task)
                xh[MASK + task, span] = dot_nt(ab[task, span], exs[task])
                moments(F_MASK, task, xh.at[MASK + task])

            mask_of(0)
            mid(F_SECOND)
            loop(tasks, mask_of, 1)
            start(F_MASK)
            end(F_SECOND)
            norm_rows(SECOND, 0)

            def second_act(h):
                active, slope = silu_parts(normalized(SECOND, h, xh[SECOND, part(h), :]))
                aux[SECOND, part(h), :] = slope
                p_act[part(h), :] = active

            each(second_act)
            mid(F_MASK)
            soft_pool(0, lambda h: p_act[part(h), :])
            end(F_MASK)

            def task_conv(task):
                norm_rows(MASK + task, task)

                def act(h):
                    active = normalized(MASK + task, h, xh[MASK + task, part(h), :])
                    sigmoid_of = sigmoid(active)
                    aux[MASK + task, part(h), :] = sigmoid_of
                    attended = sigmoid_of * p_act[part(h), :]
                    nb[task, part(h), :] = attended.astype(jnp.bfloat16)
                    put_pad(h, attended)

                each(act)
                beside_core(nb.at[task, span], 1 + tasks + task)
                pltpu.make_async_copy(tc.at[task], tcs.at[task], w_load.at[W_TASK + task]).wait()
                conv_to(tcs.at[task], xh.at[TASK + task, span])
                moments(F_TASK, task, xh.at[TASK + task])

            loop(tasks, task_conv)
            start(F_TASK)
            mid(F_TASK)
            end(F_TASK)

            def task_pool(task):
                norm_rows(TASK + task, task)

                def act(h):
                    active, slope = silu_parts(
                        normalized(TASK + task, h, xh[TASK + task, part(h), :])
                    )
                    aux[TASK + task, part(h), :] = slope
                    active_of[part(h), :] = active

                each(act)
                soft_pool(1 + task, lambda h: active_of[part(h), :])

            loop(tasks, task_pool)
            squares = sums_at(B_TASK)[0]
            squares[0, j, tasks] = jnp.zeros((8, c), jnp.float32)
            for index in range(1 + tasks):
                squares[0, j, tasks, pl.ds(index, 1), :] = osq[index]

        def handed(index):
            if leading:
                got(sg_in.at[0], h_recv.at[1 + tasks + index])

        def backward(work):
            def task_start(task):
                handed(1 + task)
                first = second = None
                for pair in range(rows_high // 2):
                    upstream = widened(1 + task, pair)
                    for h in (2 * pair, 2 * pair + 1):
                        at = part(h)
                        up = upstream * share[1 + task, at, :] * aux[TASK + task, at, :]
                        dr[task, at, :] = up
                        by = up * xh[TASK + task, at, :]
                        first = up if first is None else first + up
                        second = by if second is None else second + by
                write_stats(B_TASK, task, first, second)

            loop(tasks, task_start)
            start(B_TASK)
            work(0)
            mid(B_TASK)
            work(1)
            end(B_TASK)
            total_ref[1] = tot[tasks]

            def task_back(task):
                rounded(TASK + task, task, task, None)
                conv_back_to(tcs.at[task], dr.at[task, span])
                first = second = None
                for h in range(rows_high):
                    at = part(h)
                    m, p = aux[MASK + task, at, :], p_act[at, :]
                    through = dr[task, at, :] * m

                    @pl.when(task == 0)
                    def _():
                        gp[at, :] = through

                    @pl.when(task > 0)
                    def _():
                        gp[at, :] += through

                    up = through * p * (1.0 - m)
                    dr[task, at, :] = up
                    by = up * xh[MASK + task, at, :]
                    first = up if first is None else first + up
                    second = by if second is None else second + by
                write_stats(B_MASK, task, first, second)

            loop(tasks, task_back)
            handed(0)
            first = second = None
            for pair in range(rows_high // 2):
                upstream = widened(0, pair)
                for h in (2 * pair, 2 * pair + 1):
                    at = part(h)
                    up = (gp[at, :] + upstream * share[0, at, :]) * aux[SECOND, at, :]
                    dr[3, at, :] = up
                    by = up * xh[SECOND, at, :]
                    first = up if first is None else first + up
                    second = by if second is None else second + by
            write_stats(B_MASK, tasks, first, second)
            start(B_MASK)
            work(2)
            mid(B_MASK)
            work(3)
            end(B_MASK)

            def mask_back(task):
                rounded(MASK + task, task, task, joint.at[task], xh.at[TASK + task, span])
                spread(2, task)
                dr[task, span] = dot_nn(middle(), exs[task])
                first = second = None
                for h in range(rows_high):
                    at = part(h)
                    up = dr[task, at, :] * aux[NARROW + task, at, :]
                    dr[task, at, :] = up
                    by = up * xh[NARROW + task, at, :]
                    first = up if first is None else first + up
                    second = by if second is None else second + by
                write_stats(B_NARROW, task, first, second)

            loop(tasks, mask_back)
            start(B_NARROW)
            rounded(SECOND, tasks, 3, turned.at[1])
            spread(1)
            mid(B_NARROW)
            conv_back_to(w2s, gp.at[span])
            end(B_NARROW)

            def narrow_back(task):
                rounded(NARROW + task, task, task, turned.at[2 + task])
                spread(4, task)
                gp[span, :] += dot_nn(middle(), sqs[task, :, pl.ds(0, c)])
                grad = dot_nn(middle(), sqs[task, :, pl.ds(c, c)])
                outer_grad(1 + task, grad)

            def outer_grad(index, grad):
                if leading:
                    ig_ref[index, span, :] = grad
                else:
                    low = grad.astype(jnp.bfloat16)
                    sg_out[index] = low
                    ig_ref[index, span, :] = low.astype(jnp.float32)
                    at = 1 + tasks + index
                    across_cores(
                        sg_out.at[index], sg_in.at[index], h_send.at[at], h_recv.at[at]
                    )

            loop(tasks, narrow_back)
            first = second = None
            for h in range(rows_high):
                at = part(h)
                up = gp[at, :] * aux[FIRST, at, :]
                dr[3, at, :] = up
                by = up * xh[FIRST, at, :]
                first = up if first is None else first + up
                second = by if second is None else second + by
            write_stats(B_FIRST, 0, first, second)
            start(B_FIRST)
            work(4)
            mid(B_FIRST)
            work(5)
            end(B_FIRST)
            rounded(FIRST, 0, 3, turned.at[0])
            if leading:
                spread(0)
            conv_back_to(w1s, dr.at[0, span])
            outer_grad(0, dr[0, span, :])
            if not leading:
                spread(0)

        def settle():
            if not leading:
                loop(1 + 2 * tasks, lambda i: sent(beside.at[0], s_send.at[i]))
            for kind in range(2):
                spread_sent(kind)
            for kind in (2, 4):
                for task in range(tasks):
                    spread_sent(kind, task)
            for group in range(GROUPS_OF_SUMS):
                sums_sent(group)
            for index in range(1 + tasks):
                if leading:
                    sent(o_ref.at[0], h_send.at[index])
                else:
                    sent(sg_out.at[0], h_send.at[1 + tasks + index])

        deep = lines * wide_n

        def fetch(from_ref, target, index):
            copy = pltpu.make_async_copy(from_ref, target, load_sem.at[index])
            copy.start()
            return copy

        def rows_held(buffer):
            return held[buffer, :, pl.ds(0, wide_n), :].reshape(deep, c)

        def slot_of(piece):
            return (task_rows * z + piece * unit) // c - plane_tasks(z)[0]

        def clear_tail():
            for buffer in range(2):
                held[buffer, :, pl.ds(n, wide_n - n), :] = jnp.zeros(
                    (lines, wide_n - n, c), jnp.bfloat16
                )

        second_at = n % 128
        own_rows = task_rows // mates

        def dealt(kind):
            return (pieces * kind, pieces) if kind < 2 else (2 * pieces, own_rows)

        def deal(kind):
            spread_got(kind)
            offset, _ = kinds[kind]
            at, count = dealt(kind)
            for step in range(mates):
                first = pl.multiple_of(offset + lax.rem(j + step, mates) * count, pieces)
                push(
                    spread_refs(kind)[1].at[:, pl.ds(first, count), pl.ds(0, wide_n)],
                    dq_ref.at[j, :, pl.ds(at, count)], dq_send.at[b, kind, step],
                    dq_recv.at[b, kind], core_of(kind), mate(step),
                )

        def deal_sent(kind):
            _, count = dealt(kind)
            for step in range(mates):
                pushed(
                    dq_ref.at[0, :, pl.ds(0, count)], dq_send.at[b, kind, step], core_of(kind),
                    mate(step),
                )

        def deal_got(kind):
            at, count = dealt(kind)
            got(dq_ref.at[:, :, pl.ds(at, count)], dq_recv.at[b, kind])

        def conv_unit(number, slot, buffer):
            def copies(column):
                which = lax.rem(column, 2)
                return (
                    pltpu.make_async_copy(
                        q_ref.at[slot, column], held.at[which, :, pl.ds(0, n)],
                        load_sem.at[which],
                    ),
                    pltpu.make_async_copy(
                        dq_ref.at[column, :, pl.ds(number * pieces, pieces)],
                        dbuf.at[which, :, :, pl.ds(0, wide_n)], load_sem.at[2 + which],
                    ),
                )

            for copy in copies(jnp.int32(0)):
                copy.start()
            lane = lax.broadcasted_iota(jnp.int32, (lines * pieces, wide_n), 1)
            here = lax.rem(lane, jnp.int32(rows_across))

            def column_terms(column):
                which = lax.rem(column, 2)

                @pl.when(column < mates - 1)
                def _():
                    for copy in copies(column + 1):
                        copy.start()

                for copy in copies(column):
                    copy.wait()
                values = dbuf[which, :, :, pl.ds(0, wide_n)].astype(jnp.float32)
                values = values.reshape(lines * pieces, wide_n)
                if number >= 2:
                    values = jnp.where(lane < n, values, 0.0)
                for side in range(3):
                    moved = values
                    if side == 0:
                        moved = jnp.where(
                            here <= rows_across - 2, pltpu.roll(values, wide_n - 1, 1), 0.0
                        )
                    elif side == 2:
                        moved = jnp.where(here >= 1, pltpu.roll(values, 1, 1), 0.0)
                    for down in range(3):
                        by = moved
                        if down == 0:
                            by = pltpu.roll(moved, wide_n - per_row, 1)
                        elif down == 2:
                            by = pltpu.roll(moved, per_row, 1)
                        by = by.astype(jnp.bfloat16)
                        at = pl.ds((3 * down + side) * pieces, pieces)
                        for line in range(lines):
                            cols[at, pl.ds(line * wide_n, wide_n)] = by[
                                line * pieces : (line + 1) * pieces
                            ]
                terms = dot_nn(cols[pl.ds(0, TAPS * pieces), pl.ds(0, deep)], rows_held(which))

                @pl.when(column == 0)
                def _():
                    for tap in range(TAPS):
                        out[buffer, :, pl.ds(tap * c, c)] = terms[
                            tap * pieces : (tap + 1) * pieces
                        ]

                @pl.when(column > 0)
                def _():
                    for tap in range(TAPS):
                        out[buffer, :, pl.ds(tap * c, c)] += terms[
                            tap * pieces : (tap + 1) * pieces
                        ]

            loop(mates, column_terms)

        def staged_conv(number, slot):
            buffer = turn[0] % 2
            turn[0] += 1
            target = (
                (r_first, r_second)[number] if number < 2
                else r_task.at[pl.ds((number - 2) * pieces, pieces)]
            )
            free(
                buffer,
                lambda: pushed(
                    out.at[buffer], t_send.at[b, number, 0], b, me, t_own.at[number, 0]
                ),
            )
            conv_unit(number, slot, buffer)
            push(
                out.at[buffer], target, t_send.at[b, number, 0], r_recv.at[number], b, me,
                t_own.at[number, 0],
            )

        def flat_terms(kind, staged, parts, lanes, first):
            offset, _ = kinds[kind]
            from_ref = spread_refs(kind)[1]
            copies = [
                fetch(
                    from_ref.at[line, pl.ds(offset + piece * unit, unit), lanes],
                    cols.at[pl.ds(piece * unit, unit), pl.ds(line * wide_n, wide_n)],
                    4 + piece * lines + line,
                )
                for piece in range(tasks)
                for line in range(lines)
            ]
            loads = []
            for at, a_kind in parts:
                for piece in range(tasks):
                    if a_kind is not None:
                        loads.append(a_ref.at[2 + 2 * a_kind + slot_of(piece)])
                    elif piece == 0:
                        loads.append(q_ref.at[1, j])

            def load(number):
                return pltpu.make_async_copy(
                    loads[number], held.at[number % 2, :, pl.ds(first, n)],
                    load_sem.at[number % 2],
                )

            load(0).start()
            for copy in copies:
                copy.wait()
            number = -1
            for at, a_kind in parts:
                for piece in range(tasks):
                    if a_kind is not None or piece == 0:
                        number += 1
                        load(number).wait()
                        if number + 1 < len(loads):
                            load(number + 1).start()
                    terms = dot_nn(
                        cols[pl.ds(piece * unit, unit), pl.ds(0, deep)], rows_held(number % 2)
                    )
                    staged[pl.ds(piece * unit, unit), pl.ds(at, c)] = terms.astype(jnp.bfloat16)

        def flat_push(target, staged, index):
            for mate_at in range(mates):
                push(
                    staged.at[pl.ds(mate_at * own_rows, own_rows)], target.at[j],
                    t_send.at[b, index, mate_at], r_recv.at[index], b, z * mates + mate_at,
                    t_own.at[index, mate_at],
                )

        def flat_sent(staged, index):
            for mate_at in range(mates):
                pushed(
                    staged.at[pl.ds(0, own_rows)], t_send.at[b, index, mate_at], b,
                    z * mates + mate_at, t_own.at[index, mate_at],
                )

        def free(name, waits):
            if name in in_use:
                in_use[name]()
            in_use[name] = waits

        def terms_second():
            deal_got(1)
            shared_got(1)
            staged_conv(1, 1)

        def terms_first():
            deal_got(0)
            shared_got(0)
            staged_conv(0, 0)

        def terms_squeeze():
            spread_got(4)
            got(a_ref.at[0], u_recv.at[b])
            for task in range(tasks):
                task_got(0, task)
            free(2, lambda: flat_sent(stage_flat, 5))
            flat_terms(4, stage_flat, [(0, None), (c, 0)], pl.ds(0, wide_n), 0)
            flat_push(r_squeeze, stage_flat, 5)

        def terms_expand():
            for task in range(tasks):
                task_got(1, task)
            staged = stage_flat.at[:, pl.ds(0, c)]
            free(2, lambda: flat_sent(staged, 6))
            for buffer in range(2):
                held[buffer, :, pl.ds(0, second_at), :] = jnp.zeros(
                    (lines, second_at, c), jnp.bfloat16
                )
            flat_terms(2, staged, [(0, 1)], pl.ds(n - second_at, wide_n), second_at)
            flat_push(r_expand, staged, 6)
            clear_tail()

        def terms_tasks():
            deal_got(2)
            for task in range(tasks):
                task_got(2, task)
            for number in range(own_rows // pieces):
                task = (own_rows * me + number * pieces) // c
                staged_conv(2 + number, 2 + task - plane_tasks(z)[0])

        def terms_got():
            away = range(2, 2 + own_rows // pieces) if leading else range(2)
            for number in away:
                got(r_first, r_recv.at[number])
            senders = pl.ds(0, mates if leading else mates - 1)
            for index, target in ((5, r_squeeze), (6, r_expand)):
                got(target.at[senders], r_recv.at[index])

        def set_up():
            image = lax.div(
                lax.broadcasted_iota(jnp.int32, (per_row, c), 0), jnp.int32(rows_across)
            )
            for k in range(micro):
                masks[k, used, :] = (
                    jnp.where(image == k, 1.0, 0.0)
                    + jnp.where(image == micro, fourth[k], 0.0)
                    + jnp.where(image == micro + 1, fifth[k], 0.0)
                )
            zero = jnp.zeros((per_row, 3 * c), jnp.bfloat16)
            pad[pl.ds(0, per_row), :] = zero
            pad[pl.ds(n + per_row, per_row), :] = zero

        return types.SimpleNamespace(
            forward_start=forward_start, forward=forward, backward=backward, settle=settle,
            set_up=set_up, clear_tail=clear_tail, exchange=exchange_activations,
            exchange_sent=exchange_sent,
            second=terms_second, first=terms_first, squeeze=terms_squeeze, expand=terms_expand,
            task_terms=terms_tasks, terms_got=terms_got, deal=deal, deal_sent=deal_sent,
        )

    weight_copy(W_FIRST).start()
    weight_copy(W_SQUEEZE).start()
    barrier = pltpu.get_barrier_semaphore()
    greeted = (
        [(section, mate(step)) for step in range(1, mates)]
        + [(section, liner(step)) for step in range(1, lines)]
        + [(other, mate(step)) for step in range(mates)]
        + [(other, liner(step)) for step in range(1, lines)]
    )
    for device in greeted:
        pl.semaphore_signal(barrier, inc=1, device_id=device, device_id_type=MESH)
    numbers = [count_ref[0, k] for k in range(micro)]
    double = [jnp.where(number >= 2, jnp.float32(1.0), jnp.float32(0.0)) for number in numbers]
    fourth, fifth = [], []
    before = jnp.float32(0.0)
    for k in range(micro):
        fourth.append(double[k] * (1.0 - before))
        fifth.append(double[k] * before)
        before = before + double[k]
    count_slot = sums_at(F_FIRST)[0]
    count_slot[0, j, 1] = jnp.zeros((8, c), jnp.float32)
    for k in range(micro):
        count_slot[0, j, 1, pl.ds(k, 1), :] = jnp.full((1, c), 1.0) * (1.0 + double[k])
    for index in range(NORMS):
        at = pl.ds(index if index < NARROW else index - NARROW, 1)
        gain[index] = gain_in[at, :] if index < NARROW else narrow_gain[index - NARROW]
        shift[index] = shift_in[at, :] if index < NARROW else narrow_shift[index - NARROW]
    in_use, turn = {}, [0]
    one, two = make_block(0), make_block(1)

    def picked_rows(values, index, h):
        doubles = [values[index, 2 * k + 1, h].astype(jnp.float32) for k in range(micro)]
        rows_of = [values[index, 2 * k, h].astype(jnp.float32) for k in range(micro)]
        for weight in (fourth, fifth):
            picked = doubles[0] * weight[0]
            for k in range(1, micro):
                picked = picked + doubles[k] * weight[k]
            rows_of.append(picked)
        return rows_of

    def compact(index):
        for h in range(high):
            x_one[index, pl.ds(h * live * across, live * across), :] = jnp.concatenate(
                picked_rows(stream, index, h), axis=0
            ).astype(jnp.bfloat16)

    def cotangents():
        for index in range(1 + tasks):
            og_ref[index] = jnp.zeros(og_ref.shape[1:], jnp.float32)
            for i, upstream in enumerate(picked_rows(cotangent, index, 0)):
                og_ref[index, pl.ds(i * (across // 4), across // 4), :] = upstream

    @pl.when(section == 0)
    def _():
        one.set_up()
        loop(1 + tasks, compact)
        pl.semaphore_wait(barrier, len(greeted))
        one.forward_start()
        one.forward()
        one.exchange()
        two.exchange()

        def work(place):
            if place == 0:
                two.clear_tail()
                two.deal(1)
            elif place == 1:
                two.second()
            elif place == 2:
                two.deal(0)
            elif place == 3:
                two.first()
                one.clear_tail()
            elif place == 4:
                one.deal(1)
            else:
                one.second()

        one.backward(work)
        one.deal(0)
        one.first()
        for waits in in_use.values():
            waits()
        in_use.clear()
        for kind in range(2):
            one.deal_sent(kind)
            two.deal_sent(kind)
        one.exchange_sent()
        two.exchange_sent()
        one.settle()
        one.terms_got()

    @pl.when(section == 1)
    def _():
        two.set_up()
        cotangents()
        pl.semaphore_wait(barrier, len(greeted))
        two.forward_start()
        two.forward()
        two.backward(lambda place: None)
        two.deal(2)
        two.clear_tail()
        two.expand()
        two.squeeze()
        two.task_terms()
        one.deal(2)
        one.clear_tail()
        one.expand()
        one.task_terms()
        one.squeeze()
        for waits in in_use.values():
            waits()
        one.deal_sent(2)
        two.deal_sent(2)
        two.settle()
        two.terms_got()


def result_kernel(plan, *refs):
    (
        count_ref, first, second, squeeze, expand, task, pooled, grads, norms, totals,
        first_out, second_out, squeeze_out, expand_out, task_out, feature_out, input_out,
        gain_out, shift_out, narrow_gain_out, narrow_shift_out, rms_out,
    ) = refs
    mates, tasks, c = plan["mates"], plan["tasks"], plan["channels"]
    section = lax.axis_index("section")
    live, micro = plan["live"], plan["micro"]
    images_of = []
    before = jnp.int32(micro)
    for k in range(micro):
        double = count_ref[0, k] >= 2
        images_of.append(jnp.where(double, before, jnp.int32(-1)))
        before = before + jnp.where(double, jnp.int32(1), jnp.int32(0))

    def aligned(values, image, rows, used):
        start = image * rows
        values = pltpu.roll(values, values.shape[0] - start, 0) if start else values
        inside = lax.broadcasted_iota(jnp.int32, (8, c), 0) < used
        return jnp.where(inside, values[:8], 0.0)

    def by_slot(values, rows, used, store):
        two = [aligned(values, micro, rows, used), aligned(values, micro + 1, rows, used)]
        for k in range(micro):
            store(2 * k, aligned(values, k, rows, used))
            which = images_of[k]
            store(
                2 * k + 1,
                jnp.where(which == micro, two[0], jnp.where(which == micro + 1, two[1], 0.0)),
            )

    def place_out(high, across, images, leading):
        per_row = images * across
        for index in range(1 + tasks):
            for h in range(plan["high"]):

                def store(slot, values):
                    input_out[index, slot, h] = values

                if h < high:
                    by_slot(grads[index, pl.ds(h * per_row, per_row), :], across, across, store)
                else:
                    for slot in range(2 * micro):
                        store(slot, jnp.zeros((8, c), jnp.float32))
            for h in range(plan["high"] // 2):

                def store_feature(slot, values):
                    feature_out[index, slot, h] = values[: plan["across"] // 2].astype(
                        jnp.bfloat16
                    )

                if h < high // 2:
                    count = 8 * (across // 2)
                    by_slot(
                        pooled[index, pl.ds(h * count, count), :].astype(jnp.float32),
                        across // 2, across // 2, store_feature,
                    )
                else:
                    for slot in range(2 * micro):
                        store_feature(slot, jnp.zeros((8, c), jnp.float32))
        cells = float(high * across // 4 * c)
        live_total = jnp.sum(totals[0, pl.ds(0, micro), pl.ds(0, 1)], axis=0, keepdims=True)
        lane = lax.broadcasted_iota(jnp.int32, (1, 1 + tasks), 1)
        result = jnp.zeros((1, 1 + tasks), jnp.float32)
        for index in range(1 + tasks):
            square = jnp.sum(totals[1, pl.ds(index, 1), :], axis=1, keepdims=True)
            result = jnp.where(lane == index, jnp.sqrt(square / (live_total * cells)), result)
        rms_out[...] = result
        for index in range(NORMS):
            shift_sum = jnp.sum(norms[index, pl.ds(0, micro), :], axis=0, keepdims=True)
            gain_sum = jnp.sum(norms[index, pl.ds(micro, micro), :], axis=0, keepdims=True)
            if index < NARROW:
                gain_out[pl.ds(index, 1), :] = gain_sum
                shift_out[pl.ds(index, 1), :] = shift_sum
            else:
                narrow_gain_out[index - NARROW] = gain_sum
                narrow_shift_out[index - NARROW] = shift_sum

    @pl.when((pl.program_id(0) == 0) & (section == 0))
    def _():
        place_out(plan["high"], plan["across"], live, True)

    @pl.when((pl.program_id(0) == 0) & (section == 1))
    def _():
        place_out(plan["high"] // 2, plan["across"] // 2, 8, False)

    for terms, target in (
        (first, first_out), (second, second_out), (squeeze, squeeze_out),
        (expand, expand_out), (task, task_out),
    ):
        count, width = terms.shape[-2:]
        per_row = width // 128
        for lane in range(per_row):
            at = pl.ds(lane * 128, 128)
            if len(terms.shape) == 2:
                summed = terms[:, at]
            else:
                summed = terms[0, :, at].astype(jnp.float32)
                for place in range(1, mates):
                    summed = summed + terms[place, :, at].astype(jnp.float32)
            target[pl.ds(lane, count, stride=per_row), :] = summed


def gathered_shards(
    stream_in, image_count, out_grad, first_conv, second_conv, squeeze, expand, task_conv,
    norm_gain, norm_shift, squeeze_gain, squeeze_shift,
):
    maps, images, high, across, c = stream_in.shape
    micro = image_count.shape[1]
    tasks = maps - 1
    groups = lax.axis_size("dp")
    mates = 4
    lines = groups // mates
    live = images - 2
    n = high * live * across
    wide_n = 256
    plan = {
        "lines": lines, "mates": mates, "tasks": tasks, "channels": c,
        "high": high, "across": across, "live": live, "wide": wide_n, "micro": micro,
    }
    conv_rows = c // groups
    task_rows = tasks * c // groups
    bf16, f32 = jnp.bfloat16, jnp.float32
    vmem = pl.BlockSpec(memory_space=pltpu.VMEM)
    whole = pl.BlockSpec(memory_space=pl.ANY)
    shapes = (
        (conv_rows, TAPS * c), (conv_rows, TAPS * c), (task_rows, 2 * c), (task_rows, c),
        (task_rows, TAPS * c),
    )
    formed = (True, True, False, False, True)
    small = 64
    single_rows = (2 + tasks) * c // lines
    out_shape = (
        [
            jax.ShapeDtypeStruct((maps, small, c), bf16),
            jax.ShapeDtypeStruct((maps, n, c), f32),
            jax.ShapeDtypeStruct((NORMS, 8, c), f32),
            jax.ShapeDtypeStruct((2, 8, c), f32),
            jax.ShapeDtypeStruct((8, lines, n, c), bf16),
            jax.ShapeDtypeStruct((8, lines, small, c), bf16),
            jax.ShapeDtypeStruct((lines, single_rows, wide_n), bf16),
            jax.ShapeDtypeStruct((lines, single_rows, 128), bf16),
            jax.ShapeDtypeStruct((lines, mates * task_rows, 2 * n), bf16),
            jax.ShapeDtypeStruct((lines, mates * task_rows, 2 * small), bf16),
        ]
        + [
            jax.ShapeDtypeStruct((4, mates, lines, n, c), bf16),
            jax.ShapeDtypeStruct((4, mates, lines, small, c), bf16),
            jax.ShapeDtypeStruct((mates, lines, 2 * conv_rows + task_rows, wide_n), bf16),
            jax.ShapeDtypeStruct((mates, lines, 2 * conv_rows + task_rows, 128), bf16),
            jax.ShapeDtypeStruct((1 + 2 * tasks, small, c), bf16),
        ]
        + [
            jax.ShapeDtypeStruct(shape, f32) if whole_terms
            else jax.ShapeDtypeStruct((mates,) + shape, bf16)
            for shape, whole_terms in zip(shapes, formed)
        ]
    )
    row = live * across
    scratch = [
        pltpu.VMEM(shape, dtype)
        for shape, dtype in (
            ((c, TAPS * c), bf16),
            ((c, TAPS * c), bf16),
            ((tasks, c, 2 * c), bf16),
            ((tasks, c, c), bf16),
            ((tasks, c, TAPS * c), bf16),
            ((NORMS, 1, c), f32),
            ((NORMS, 1, c), f32),
            ((maps, n, c), bf16),
            ((maps, small, c), bf16),
            ((maps, 16, c), f32),
            ((maps, small, c), bf16),
            ((maps, small, c), bf16),
            ((micro, row, c), f32),
            (((high + 2) * row, 3 * c), bf16),
            ((NORMS, n, c), f32),
            ((NORMS, n, c), f32),
            ((maps, n, c), f32),
            ((n, c), f32),
            ((n, c), bf16),
            ((tasks, n, c), bf16),
            ((tasks, n, c), bf16),
            ((4, n, c), f32),
            ((n, c), f32),
            ((3, row, c), f32),
            ((NORMS, micro, c), f32),
            ((4, 8, c), f32),
            ((8, c), f32),
            ((maps, 1, c), f32),
            ((c // 128, row, 128), f32),
            ((2 * n, c), f32),
            ((2 + tasks, c, wide_n), bf16),
            ((tasks, c, 2 * n), bf16),
            ((3, 2, 4, 2, 8, c), f32),
            ((4, 2, 4, 3, 8, c), f32),
            ((2, 2, 4, 4, 8, c), f32),
            ((2, lines, wide_n, c), bf16),
            ((2, lines, conv_rows, wide_n), bf16),
            ((3 * c // lines, lines * wide_n), bf16),
            ((2, conv_rows, TAPS * c), f32),
            ((mates * task_rows, 2 * c), bf16),
        )
    ] + [
        pltpu.SemaphoreType.DMA(shape)
        for shape in (
            (4 + tasks,), (GROUPS_OF_SUMS, 2), (GROUPS_OF_SUMS, 2), (2 * maps,), (2 * maps,),
            (2, NORMS, 4), (2, NORMS, 2), (2, 8, mates), (2, 8), (2, 4), (1 + 2 * tasks,),
            (1 + 2 * tasks,), (2,), (2,), (5, tasks, lines), (2, 5),
            (2, 3, mates), (2, 3), (2, 7, mates),
            (7, mates), (7,), (4 + tasks * lines,),
        )
    ]
    results = pl.pallas_call(
        functools.partial(main_kernel, plan),
        out_shape=out_shape,
        in_specs=[pl.BlockSpec(memory_space=pltpu.SMEM)] + [vmem] * 6 + [whole] * 5,
        out_specs=[vmem] * 4 + [whole] * 16,
        scratch_shapes=scratch,
        compiler_params=pltpu.CompilerParams(
            collective_id=1, has_side_effects=True, vmem_limit_bytes=62 * 2**20
        ),
        name="blocks",
    )(
        image_count, stream_in, out_grad, norm_gain[0], norm_shift[0],
        jnp.swapaxes(squeeze_gain, 0, 1), jnp.swapaxes(squeeze_shift, 0, 1), first_conv[0], second_conv[0], squeeze[0], expand[0], task_conv[0],
    )
    pooled, grads, norms, totals = results[:4]
    terms = results[15:]
    steps = 2

    def flat(shape):
        return jax.ShapeDtypeStruct((shape[0] * shape[1] // 128, 128), f32)

    results = pl.pallas_call(
        functools.partial(result_kernel, plan),
        grid=(steps,),
        out_shape=[flat(shape) for shape in shapes]
        + [
            jax.ShapeDtypeStruct((maps, images, high // 2, across // 2, c), bf16),
            jax.ShapeDtypeStruct((maps, images, high, across, c), f32),
            jax.ShapeDtypeStruct((NARROW, c), f32),
            jax.ShapeDtypeStruct((NARROW, c), f32),
            jax.ShapeDtypeStruct((tasks, 1, c), f32),
            jax.ShapeDtypeStruct((tasks, 1, c), f32),
            jax.ShapeDtypeStruct((1, maps), f32),
        ],
        in_specs=[pl.BlockSpec(memory_space=pltpu.SMEM)]
        + [
            pl.BlockSpec((shape[0] // steps, shape[1]), lambda i: (i, 0)) if whole_terms
            else pl.BlockSpec((mates, shape[0] // steps, shape[1]), lambda i: (0, i, 0))
            for shape, whole_terms in zip(shapes, formed)
        ]
        + [vmem] * 4,
        out_specs=[
            pl.BlockSpec((shape[0] // steps * shape[1] // 128, 128), lambda i: (i, 0))
            for shape in shapes
        ]
        + [vmem] * 7,
        compiler_params=pltpu.CompilerParams(vmem_limit_bytes=62 * 2**20),
        name="results",
    )(image_count, *terms, pooled, grads, norms, totals)
    first_g, second_g, squeeze_g, expand_g, task_g = (
        grad.reshape(1, -1) for grad in results[:5]
    )
    feature_out, input_out, gain_g, shift_g, narrow_gain_g, narrow_shift_g, rms = results[5:]
    return (
        feature_out[None], input_out[None], first_g, second_g, squeeze_g, expand_g, task_g,
        gain_g[None], shift_g[None], jnp.swapaxes(narrow_gain_g, 0, 1),
        jnp.swapaxes(narrow_shift_g, 0, 1), rms,
    )


def solution(mesh):
    groups = mesh.shape["dp"]
    whole_tiles = groups == 4 * 4
    return jax.shard_map(
        gathered_shards if whole_tiles else shards,
        mesh=mesh,
        in_specs=(
            P(None, "dp", None, None, None),
            P("dp", None),
            P(None, "dp", None, None, None),
            P("section", None, None),
            P("section", None, None),
            P("section", None, None, None),
            P("section", None, None, None),
            P("section", None, None, None),
            P("section", None, None),
            P("section", None, None),
            P("section", None, None),
            P("section", None, None),
        ),
        out_specs=(
            P("section", None, "dp", None, None, None),
            P("section", None, "dp", None, None, None),
            P("section", "dp"),
            P("section", "dp"),
            P("section", "dp"),
            P("section", "dp"),
            P("section", "dp"),
            P("section", None, None),
            P("section", None, None),
            P("section", None, None),
            P("section", None, None),
            P("section", None),
        ),
        check_vma=False,
    )
```

```python
import functools
import types

import jax
import jax.numpy as jnp
from jax import lax
from jax.experimental import pallas as pl
from jax.experimental.pallas import tpu as pltpu
from jax.sharding import PartitionSpec as P

EPSILON = 1e-05
SUM_ROWS = 40


def stages_of(size):
    stages = []
    stride = 1
    while stride < size:
        radix = next(r for r in (4, 2, 3, 5, 7, size // stride) if (size // stride) % r == 0)
        stages.append((radix, stride))
        stride *= radix
    return stages


def sum_kernel(stages, own_ref, out_ref, *scratch):
    slots, (send_sem, recv_sem) = scratch[: len(stages)], scratch[len(stages) :]
    section = lax.axis_index("section")
    me = lax.axis_index("dp")
    barrier = pltpu.get_barrier_semaphore()
    peers = []
    for radix, stride in stages:
        digit = lax.rem(me // stride, radix)
        group = [
            me + (lax.rem(digit + step, radix) - digit) * stride for step in range(1, radix)
        ]
        peers.append((digit, group))
    total = sum(len(group) for _, group in peers)
    for _, group in peers:
        for peer in group:
            pl.semaphore_signal(
                barrier, inc=1, device_id=(section, peer), device_id_type=pl.DeviceIdType.MESH
            )
    pl.semaphore_wait(barrier, total)
    for index, (radix, stride) in enumerate(stages):
        digit, group = peers[index]
        held = slots[index]
        held[digit] = own_ref[...] if index == 0 else out_ref[...]
        copies = []
        for step, peer in enumerate(group):
            copy = pltpu.make_async_remote_copy(
                src_ref=held.at[digit],
                dst_ref=held.at[digit],
                send_sem=send_sem.at[index, step],
                recv_sem=recv_sem.at[index, step],
                device_id=(section, peer),
                device_id_type=pl.DeviceIdType.MESH,
            )
            copy.start()
            copies.append(copy)
        for copy in copies:
            copy.wait_recv()
        summed = held[0]
        for place in range(1, radix):
            summed = summed + held[place]
        out_ref[...] = summed
        for copy in copies:
            copy.wait_send()


def sum_over_groups(rows):
    stages = stages_of(lax.axis_size("dp"))
    widest = max(radix for radix, _ in stages)
    return pl.pallas_call(
        functools.partial(sum_kernel, stages),
        out_shape=jax.ShapeDtypeStruct(rows.shape, jnp.float32),
        in_specs=[pl.BlockSpec(memory_space=pltpu.VMEM)],
        out_specs=pl.BlockSpec(memory_space=pltpu.VMEM),
        scratch_shapes=[pltpu.VMEM((radix,) + rows.shape, jnp.float32) for radix, _ in stages]
        + [
            pltpu.SemaphoreType.DMA((len(stages), widest)),
            pltpu.SemaphoreType.DMA((len(stages), widest)),
        ],
        compiler_params=pltpu.CompilerParams(collective_id=0, has_side_effects=True),
        name="group_sum",
    )(rows)


def from_behind(shard, axis, by):
    size = lax.axis_size(axis)
    pairs = [(i, i + by) for i in range(size) if 0 <= i + by < size]
    return lax.ppermute(shard, axis, pairs)


def broadcast_rows(vector):
    return vector[..., None, None, None, :]


def affine_rows(normed, scale_by, offset_by):
    return normed * broadcast_rows(scale_by) + broadcast_rows(offset_by)


def silu_slope(active):
    sigmoid_of = jax.nn.sigmoid(active)
    return sigmoid_of * (1.0 + active * (1.0 - sigmoid_of))


def pixel_sums(values, pixel_weight):
    weighted = values * pixel_weight
    return jnp.stack(
        [jnp.sum(weighted, axis=(-4, -3, -2)), jnp.sum(weighted * values, axis=(-4, -3, -2))],
        axis=-2,
    )


def gradient_sums(upstream, normed, pixel_weight):
    weighted = upstream * pixel_weight
    return jnp.stack(
        [jnp.sum(weighted, axis=(-4, -3, -2)), jnp.sum(weighted * normed, axis=(-4, -3, -2))],
        axis=-2,
    )


def summed_members(members):
    rows = [member.reshape(-1, member.shape[-1]) for member in members]
    used = sum(row.shape[0] for row in rows)
    packed = jnp.concatenate(
        rows + [jnp.zeros((SUM_ROWS - used, rows[0].shape[-1]), jnp.float32)], axis=0
    )
    summed = sum_over_groups(packed)
    results = []
    offset = 0
    for member, row in zip(members, rows):
        results.append(summed[offset : offset + row.shape[0]].reshape(member.shape))
        offset += row.shape[0]
    return results


def normalize(values, moments, counted):
    average = moments[..., 0, :] / counted
    spread = moments[..., 1, :] / counted - average * average
    inverse = lax.rsqrt(spread + EPSILON)
    return ((values - broadcast_rows(average)) * broadcast_rows(inverse), inverse)


def norm_backward(upstream, normed, inverse, scale_by, sums, counted, pixel_weight):
    shift_part = broadcast_rows(sums[..., 0, :])
    scale_part = broadcast_rows(sums[..., 1, :])
    return (
        broadcast_rows(inverse * scale_by)
        * (upstream - (shift_part + normed * scale_part) / broadcast_rows(counted))
        * pixel_weight
    )


def window_blocks(values):
    leading = values.shape[:-3]
    height, breadth, channels = values.shape[-3:]
    return values.reshape(leading + (height // 2, 2, breadth // 2, 2, channels))


def soft_pool_blocks(blocks):
    summit = jnp.max(blocks, axis=(-4, -2), keepdims=True)
    return summit + jnp.log(jnp.mean(jnp.exp(blocks - summit), axis=(-4, -2), keepdims=True))


def soft_pool(values):
    pooled = soft_pool_blocks(window_blocks(values))
    return pooled.reshape(
        values.shape[:-3] + (values.shape[-3] // 2, values.shape[-2] // 2, values.shape[-1])
    )


def pool_back(upstream, values):
    blocks = window_blocks(values)
    pooled = soft_pool_blocks(blocks)
    weight_share = jnp.exp(blocks - pooled) * 0.25
    spread = upstream.reshape(pooled.shape) * weight_share
    return spread.reshape(values.shape)


def patch_columns(frames):
    height, breadth = (frames.shape[-3], frames.shape[-2])
    padding = [(0, 0)] * (frames.ndim - 3) + [(1, 1), (1, 1), (0, 0)]
    padded = jnp.pad(frames, padding)
    return jnp.concatenate(
        [
            padded[..., down_shift : down_shift + height, side_shift : side_shift + breadth, :]
            for down_shift in range(3)
            for side_shift in range(3)
        ],
        axis=-1,
    )


def columns_back(grad_columns, channels):
    height, breadth = (grad_columns.shape[-3], grad_columns.shape[-2])
    leading = [(0, 0)] * (grad_columns.ndim - 3)
    summed = None
    for tap_index in range(9):
        down_shift, side_shift = (tap_index // 3, tap_index % 3)
        piece_of = grad_columns[..., tap_index * channels : (tap_index + 1) * channels]
        placed = jnp.pad(
            piece_of, leading + [(down_shift, 2 - down_shift), (side_shift, 2 - side_shift), (0, 0)]
        )
        summed = placed if summed is None else summed + placed
    return summed[..., 1 : height + 1, 1 : breadth + 1, :]


def live_rows(pixel_weight, channels):
    live = jnp.sum(pixel_weight, axis=(-4, -3, -2, -1))
    return jnp.broadcast_to(live[:, None], (live.shape[0], channels))


def section_forward(frames, pixel_weight, weights):
    (
        first_conv,
        second_conv,
        squeeze,
        expand,
        task_conv,
        norm_gain,
        norm_shift,
        squeeze_gain,
        squeeze_shift,
    ) = weights
    channels = frames.shape[-1]
    tasks = squeeze.shape[0]
    input_columns = patch_columns(frames[0])
    first_pre = jnp.einsum(
        "mshwk,ok->mshwo", input_columns, first_conv, preferred_element_type=jnp.float32
    )
    first_moments = summed_members(
        [pixel_sums(first_pre, pixel_weight), live_rows(pixel_weight, channels)]
    )
    counted = first_moments[1] * (frames.shape[-3] * frames.shape[-2])
    first_normed, first_inverse = normalize(first_pre, first_moments[0], counted)
    first_output = jax.nn.silu(affine_rows(first_normed, norm_gain[0], norm_shift[0]))
    rounded_first = (first_output).astype(jnp.bfloat16)
    middle_columns = patch_columns(rounded_first)
    second_pre = jnp.einsum(
        "mshwk,ok->mshwo", middle_columns, second_conv, preferred_element_type=jnp.float32
    )
    earlier = frames[1:]
    narrow = jnp.einsum(
        "mshwc,trc->tmshwr",
        rounded_first,
        squeeze[:, :, :channels],
        preferred_element_type=jnp.float32,
    ) + jnp.einsum(
        "tmshwc,trc->tmshwr", earlier, squeeze[:, :, channels:], preferred_element_type=jnp.float32
    )
    middle_moments = summed_members([pixel_sums(second_pre, pixel_weight), pixel_sums(narrow, pixel_weight)])
    second_normed, second_inverse = normalize(second_pre, middle_moments[0], counted)
    narrow_normed, narrow_inverse = normalize(narrow, middle_moments[1], counted)
    shared_out = jax.nn.silu(affine_rows(second_normed, norm_gain[1], norm_shift[1]))
    rounded_hidden = jax.nn.silu(affine_rows(narrow_normed, squeeze_gain[:, None], squeeze_shift[:, None])).astype(
        jnp.bfloat16
    )
    widened = jnp.einsum(
        "tmshwr,tcr->tmshwc", rounded_hidden, expand, preferred_element_type=jnp.float32
    )
    mask_moments = summed_members([pixel_sums(widened, pixel_weight)])
    widened_normed, widened_inverse = normalize(widened, mask_moments[0], counted)
    task_mask = jax.nn.sigmoid(
        affine_rows(widened_normed, norm_gain[2 : 2 + tasks][:, None], norm_shift[2 : 2 + tasks][:, None])
    )
    rounded_attended = (task_mask * shared_out).astype(jnp.bfloat16)
    attended_columns = patch_columns(rounded_attended)
    task_pre = jnp.einsum(
        "tmshwk,tok->tmshwo", attended_columns, task_conv, preferred_element_type=jnp.float32
    )
    task_moments = summed_members([pixel_sums(task_pre, pixel_weight)])
    task_normed, task_inverse = normalize(task_pre, task_moments[0], counted)
    task_out = jax.nn.silu(
        affine_rows(task_normed, norm_gain[2 + tasks :][:, None], norm_shift[2 + tasks :][:, None])
    )
    pooled = jnp.concatenate([soft_pool(shared_out)[None], soft_pool(task_out)], axis=0)
    kept_state = (
        frames,
        counted,
        first_normed,
        first_inverse,
        rounded_first,
        second_normed,
        second_inverse,
        narrow_normed,
        narrow_inverse,
        rounded_hidden,
        widened_normed,
        widened_inverse,
        rounded_attended,
        task_normed,
        task_inverse,
    )
    return (pooled, kept_state)


def section_backward(upstream, kept_state, pixel_weight, squares, weights):
    (
        first_conv,
        second_conv,
        squeeze,
        expand,
        task_conv,
        norm_gain,
        norm_shift,
        squeeze_gain,
        squeeze_shift,
    ) = weights
    (
        frames,
        counted,
        first_normed,
        first_inverse,
        rounded_first,
        second_normed,
        second_inverse,
        narrow_normed,
        narrow_inverse,
        rounded_hidden,
        widened_normed,
        widened_inverse,
        rounded_attended,
        task_normed,
        task_inverse,
    ) = kept_state
    channels = frames.shape[-1]
    tasks = squeeze.shape[0]
    task_gain = norm_gain[2 + tasks :][:, None]
    mask_gain = norm_gain[2 : 2 + tasks][:, None]
    task_active = affine_rows(task_normed, task_gain, norm_shift[2 + tasks :][:, None])
    task_out = jax.nn.silu(task_active)
    grad_task_act = pool_back(upstream[1:], task_out) * silu_slope(task_active)
    task_sums, square_all = summed_members(
        [gradient_sums(grad_task_act, task_normed, pixel_weight), squares]
    )
    grad_task = norm_backward(
        grad_task_act, task_normed, task_inverse, task_gain, task_sums, counted, pixel_weight
    ).astype(jnp.bfloat16)
    attended_columns = patch_columns(rounded_attended)
    task_conv_grad = jnp.einsum(
        "tmshwo,tmshwk->tok", grad_task, attended_columns, preferred_element_type=jnp.float32
    )
    grad_attended = (
        columns_back(
            jnp.einsum(
                "tmshwo,tok->tmshwk", grad_task, task_conv, preferred_element_type=jnp.float32
            ),
            channels,
        )

    )
    second_active = affine_rows(second_normed, norm_gain[1], norm_shift[1])
    shared_out = jax.nn.silu(second_active)
    task_mask = jax.nn.sigmoid(affine_rows(widened_normed, mask_gain, norm_shift[2 : 2 + tasks][:, None]))
    grad_mask_act = grad_attended * shared_out * task_mask * (1.0 - task_mask)
    mask_sums = summed_members([gradient_sums(grad_mask_act, widened_normed, pixel_weight)])[0]
    grad_widened = norm_backward(
        grad_mask_act, widened_normed, widened_inverse, mask_gain, mask_sums, counted, pixel_weight
    ).astype(jnp.bfloat16)
    expand_grad = jnp.einsum(
        "tmshwc,tmshwr->tcr", grad_widened, rounded_hidden, preferred_element_type=jnp.float32
    )
    narrow_active = affine_rows(narrow_normed, squeeze_gain[:, None], squeeze_shift[:, None])
    grad_narrow_act = jnp.einsum(
        "tmshwc,tcr->tmshwr", grad_widened, expand, preferred_element_type=jnp.float32
    ) * silu_slope(narrow_active)
    grad_shared = pool_back(upstream[0], shared_out) + jnp.sum(grad_attended * task_mask, axis=0)
    grad_second_act = grad_shared * silu_slope(second_active)
    second_sums, narrow_sums = summed_members(
        [
            gradient_sums(grad_second_act, second_normed, pixel_weight),
            gradient_sums(grad_narrow_act, narrow_normed, pixel_weight),
        ]
    )
    grad_second = norm_backward(
        grad_second_act,
        second_normed,
        second_inverse,
        norm_gain[1],
        second_sums,
        counted,
        pixel_weight,
    ).astype(jnp.bfloat16)
    grad_narrow = norm_backward(
        grad_narrow_act,
        narrow_normed,
        narrow_inverse,
        squeeze_gain[:, None],
        narrow_sums,
        counted,
        pixel_weight,
    ).astype(jnp.bfloat16)
    middle_columns = patch_columns(rounded_first)
    second_conv_grad = jnp.einsum(
        "mshwo,mshwk->ok", grad_second, middle_columns, preferred_element_type=jnp.float32
    )
    earlier = frames[1:]
    squeeze_grad = jnp.concatenate(
        [
            jnp.einsum(
                "tmshwr,mshwc->trc", grad_narrow, rounded_first, preferred_element_type=jnp.float32
            ),
            jnp.einsum(
                "tmshwr,tmshwc->trc", grad_narrow, earlier, preferred_element_type=jnp.float32
            ),
        ],
        axis=-1,
    )
    grad_joined = jnp.einsum(
        "tmshwr,trc->tmshwc", grad_narrow, squeeze, preferred_element_type=jnp.float32
    )
    grad_first_out = (
        columns_back(
            jnp.einsum(
                "mshwo,ok->mshwk", grad_second, second_conv, preferred_element_type=jnp.float32
            ),
            channels,
        )
        + jnp.sum(grad_joined[..., :channels], axis=0)
    )
    grad_earlier = grad_joined[..., channels:]
    first_active = affine_rows(first_normed, norm_gain[0], norm_shift[0])
    grad_first_act = grad_first_out * silu_slope(first_active)
    first_sums = summed_members([gradient_sums(grad_first_act, first_normed, pixel_weight)])[0]
    grad_first = norm_backward(
        grad_first_act, first_normed, first_inverse, norm_gain[0], first_sums, counted, pixel_weight
    ).astype(jnp.bfloat16)
    input_columns = patch_columns(frames[0])
    first_conv_grad = jnp.einsum(
        "mshwo,mshwk->ok", grad_first, input_columns, preferred_element_type=jnp.float32
    )
    grad_shared_in = (
        columns_back(
            jnp.einsum("mshwo,ok->mshwk", grad_first, first_conv, preferred_element_type=jnp.float32),
            channels,
        )

    )
    grad_frames = jnp.concatenate([grad_shared_in[None], grad_earlier], axis=0)
    first_norm, second_norm, mask_norm, task_norm, narrow_norm = (
        jnp.sum(sums, axis=-3)
        for sums in (first_sums, second_sums, mask_sums, task_sums, narrow_sums)
    )
    norm_rows = jnp.concatenate(
        [first_norm[None], second_norm[None], mask_norm, task_norm], axis=0
    )
    weight_terms = (first_conv_grad, second_conv_grad, squeeze_grad, expand_grad, task_conv_grad)
    norm_terms = (norm_rows[:, 1], norm_rows[:, 0], narrow_norm[:, 1], narrow_norm[:, 0])
    return (grad_frames, weight_terms, norm_terms, square_all)


def shards(
    stream_in,
    image_count,
    out_grad,
    first_conv,
    second_conv,
    squeeze,
    expand,
    task_conv,
    norm_gain,
    norm_shift,
    squeeze_gain,
    squeeze_shift,
):
    weights = (
        first_conv[0],
        second_conv[0],
        squeeze[0],
        expand[0],
        task_conv[0],
        norm_gain[0],
        norm_shift[0],
        squeeze_gain[0],
        squeeze_shift[0],
    )
    maps_count, images, height, breadth, channels = stream_in.shape
    micro_count = image_count.shape[1]
    slot_count = images // micro_count
    leading_section = lax.axis_index("section") == 0
    live = jnp.arange(slot_count)[None, :] < image_count[0][:, None]
    pixel_weight = live.astype(jnp.float32)[:, :, None, None, None]

    def by_micro(maps):
        return maps.reshape((maps_count, micro_count, slot_count) + maps.shape[2:])

    def whole_pool(pooled):
        masked = pooled * pixel_weight
        squares = jnp.sum(masked * masked, axis=(1, 2, 3, 4, 5))
        return masked.astype(jnp.bfloat16), jnp.broadcast_to(squares[:, None], (maps_count, channels))

    one_pooled, one_state = section_forward(by_micro(stream_in), pixel_weight, weights)
    one_features, one_squares = whole_pool(one_pooled)
    arrived = from_behind(one_features, "section", 1)
    two_pooled, two_state = section_forward(arrived, pixel_weight, weights)
    two_features, two_squares = whole_pool(two_pooled)
    two_upstream = by_micro(out_grad).astype(jnp.float32) * pixel_weight
    two_back = section_backward(two_upstream, two_state, pixel_weight, two_squares, weights)
    sendback = two_back[0].astype(jnp.bfloat16)
    returned = from_behind(sendback, "section", -1)
    one_upstream = returned.astype(jnp.float32) * pixel_weight
    one_back = section_backward(one_upstream, one_state, pixel_weight, one_squares, weights)

    half = ((0, 0),) * 3 + ((0, height // 4), (0, breadth // 4), (0, 0))
    full = ((0, 0),) * 3 + ((0, height // 2), (0, breadth // 2), (0, 0))
    feature_out = jnp.where(leading_section, one_features, jnp.pad(two_features, half))
    feature_out = feature_out.reshape((maps_count, images) + feature_out.shape[3:])
    recorded = lax.optimization_barrier(sendback).astype(jnp.float32)
    input_grad_out = jnp.where(leading_section, one_back[0], jnp.pad(recorded, full))
    input_grad_out = input_grad_out.reshape((maps_count, images) + input_grad_out.shape[3:])
    reduced = tuple(
        lax.psum_scatter(
            jnp.where(leading_section, one, two).reshape(-1).astype(jnp.bfloat16),
            "dp",
            scatter_dimension=0,
            tiled=True,
        ).astype(jnp.float32)
        for one, two in zip(one_back[1], two_back[1])
    )
    norm_sums = tuple(
        jnp.where(leading_section, one, two) for one, two in zip(one_back[2], two_back[2])
    )
    live_images = jnp.sum(one_state[1][:, 0]) / (height * breadth)
    feature_pixels = jnp.where(leading_section, height * breadth // 4, height * breadth // 16)
    root_square = jnp.sqrt(
        jnp.where(leading_section, one_back[3], two_back[3])[:, 0]
        / (live_images * feature_pixels * channels)
    )
    return (
        feature_out[None],
        input_grad_out[None],
        reduced[0][None],
        reduced[1][None],
        reduced[2][None],
        reduced[3][None],
        reduced[4][None],
        norm_sums[0][None],
        norm_sums[1][None],
        norm_sums[2][None],
        norm_sums[3][None],
        root_square[None],
    )


TAPS = 9
MESH = pl.DeviceIdType.MESH
FIRST, SECOND, MASK, TASK, NARROW = 0, 1, 2, 5, 8
NORMS = 11
(F_FIRST, F_SECOND, B_FIRST, F_NARROW, F_MASK, F_TASK, B_NARROW, B_TASK, B_MASK) = range(9)
GROUPS_OF_SUMS = 9
(
    P_FIRST, P_FIRST_DONE, P_NARROW_DONE, P_MASK_DONE, P_ATTENDED, P_TASKED, P_SUMMED,
    P_TASK_DONE, P_BTASK_SUMS, P_BTASK_DONE, P_BMASK_START, P_BMASK_SUMS, P_BMASK_DONE,
    P_BNARROW_DONE, P_BFIRST_START, P_BFIRST_SUMS, P_BFIRST_DONE,
) = range(17)


def sigmoid(active):
    return 0.5 * jnp.tanh(0.5 * active) + 0.5


def silu_parts(active):
    sigmoid_of = sigmoid(active)
    return active * sigmoid_of, sigmoid_of * (1.0 + active * (1.0 - sigmoid_of))


def dot_nt(left, right):
    return lax.dot_general(
        left, right, (((1,), (1,)), ((), ())), preferred_element_type=jnp.float32
    )


def dot_nn(left, right):
    return lax.dot_general(
        left, right, (((1,), (0,)), ((), ())), preferred_element_type=jnp.float32
    )


def loop(count, body, start=0):
    lax.fori_loop(start, count, lambda i, _: (body(i), 0)[1], 0)


def main_kernel(plan, *refs):
    (
        count_ref, stream, cotangent, gain_in, shift_in, narrow_gain, narrow_shift,
        w1, w2, sq, ex, tc,
        o_ref, ig_ref, norm_ref, total_ref, a_one, a_two, d_one, d_two, pair_one, pair_two,
        q_one, q_two, dq_one, dq_two, beside, r_first, r_second, r_squeeze, r_expand, r_task,
        w1s, w2s, sqs, exs, tcs, gain, shift, x_one, x_two, og_ref, sg_in, sg_out,
        masks, pad, xh, aux, share, p_act, ub, ab, nb, dr, gp, rows, inv, tot, counts, osq,
        wide, tbuf, turned, joint, slots_one, slots_three, slots_four,
        held, dbuf, cols, out, stage_flat,
        w_load, sync_send, sync_recv, h_send, h_recv, a_send, a_recv, v_send, v_recv, q_recv, s_send, s_recv, u_send, u_recv,
        d_send, d_recv, dq_send, dq_recv, t_send, t_own, r_recv, load_sem,
    ) = refs
    lines, mates, tasks, c = plan["lines"], plan["mates"], plan["tasks"], plan["channels"]
    high, across, live = plan["high"], plan["across"], plan["live"]
    hc = c // 2
    active_of = dr.at[0]
    micro = masks.shape[0]
    section = lax.axis_index("section")
    other = 1 - section
    me = lax.axis_index("dp")
    z, j = me // mates, lax.rem(me, mates)
    unit = c // lines
    pieces = unit // mates
    task_rows = tasks * c // lines
    kinds = ((0, unit), (unit, unit), (0, task_rows), None, (2 * unit, task_rows))

    def plane_tasks(line):
        return (task_rows * line) // c, (task_rows * (line + 1) - 1) // c

    def plane_needs(line, task):
        first, last = plane_tasks(line)
        return (first <= task) & (task <= last)

    def device_needs(device, task):
        own = task_rows // mates
        return ((own * device) // c <= task) & (task <= (own * device + own - 1) // c)

    def mate(step):
        return z * mates + lax.rem(j + step, mates)

    def liner(step):
        return lax.rem(z + step, lines) * mates + j

    def remote(source, target, send, recv, to, device):
        return pltpu.make_async_remote_copy(
            src_ref=source, dst_ref=target, send_sem=send, recv_sem=recv,
            device_id=(to, device), device_id_type=MESH,
        )

    def got(some, recv):
        remote(some, some, sync_send.at[0, 0], recv, section, me).wait_recv()

    def sent(some, send):
        remote(some, some, send, sync_recv.at[0, 0], section, me).wait_send()

    def push(source, target, send, recv, to, device, own=None):
        same = (section == to) & (me == device)

        @pl.when(same)
        def _():
            pltpu.make_async_copy(source, target, recv if own is None else own).start()

        @pl.when(jnp.logical_not(same))
        def _():
            remote(source, target, send, recv, to, device).start()

    def pushed(some, send, to, device, own=None):
        same = (section == to) & (me == device)

        @pl.when(jnp.logical_not(same))
        def _():
            sent(some, send)

        if own is not None:

            @pl.when(same)
            def _():
                pltpu.make_async_copy(some, some, own).wait()

    def across_cores(source, target, send, recv):
        remote(source, target, send, recv, other, me).start()

    def sums_at(group):
        if group < 3:
            ref, at, count = slots_one, group, 2 if group == F_FIRST else 1
        elif group < 7:
            ref, at, count = slots_three, group - 3, 3
        else:
            ref, at, count = slots_four, group - 7, 4
        return ref.at[at], count, group

    def sums_place(group, stage, digits):
        ref, count, _ = sums_at(group)
        return ref.at[stage, digits, pl.ds(0, count)]

    def sums_send(group, stage, digit, devices):
        at = sums_at(group)[2]
        here = sums_place(group, stage, digit)
        for device in devices:
            remote(
                here, here, sync_send.at[at, stage], sync_recv.at[at, stage], section, device
            ).start()

    def sums_got(group, stage, digits):
        ref, count, at = sums_at(group)
        got(sums_place(group, stage, pl.ds(0, digits - 1)), sync_recv.at[at, stage])
        summed = ref[stage, 0, pl.ds(0, count)]
        for digit in range(1, digits):
            summed = summed + ref[stage, digit, pl.ds(0, count)]
        return summed

    def sums_start(group):
        sums_send(group, 0, j, [mate(step) for step in range(1, mates)])

    def sums_mid(group):
        ref, count, _ = sums_at(group)
        ref[1, z, pl.ds(0, count)] = sums_got(group, 0, mates)
        sums_send(group, 1, z, [liner(step) for step in range(1, lines)])

    def sums_end(group):
        count = sums_at(group)[1]
        tot[pl.ds(0, count)] = sums_got(group, 1, lines)

    def sums_sent(group):
        at = sums_at(group)[2]
        for stage, digits in enumerate((mates, lines)):
            sent(
                sums_place(group, stage, pl.ds(0, digits - 1)), sync_send.at[at, stage]
            )

    W_FIRST, W_SQUEEZE, W_SECOND, W_EXPAND, W_TASK = range(5)

    def weight_copy(index):
        if index >= W_TASK:
            source, target = tc.at[index - W_TASK], tcs.at[index - W_TASK]
        else:
            source, target = ((w1, w1s), (sq, sqs), (w2, w2s), (ex, exs))[index]
        return pltpu.make_async_copy(source, target, w_load.at[index])

    def make_block(b):
        leading = b == 0
        rows_high, rows_across, images = (
            (high, across, live) if leading else (high // 2, across // 2, 8)
        )
        per_row = images * rows_across
        n = rows_high * per_row
        wide_n = plan["wide"] if leading else 128
        pixels = float(rows_high * rows_across)
        half = per_row // 2
        source = x_one if leading else x_two
        a_ref, d_ref, pair_ref, q_ref, dq_ref = (
            (a_one, d_one, pair_one, q_one, dq_one) if leading
            else (a_two, d_two, pair_two, q_two, dq_two)
        )
        position = lax.rem(
            lax.broadcasted_iota(jnp.int32, (per_row, c), 0), jnp.int32(rows_across)
        )
        even = lax.rem(position, jnp.int32(2)) == 0
        span = pl.ds(0, n)
        used = pl.ds(0, per_row)

        def each(body):
            for h in range(rows_high):
                body(h)

        def part(h):
            return pl.ds(h * per_row, per_row)

        def shifted(values):
            left = jnp.where(position >= 1, pltpu.roll(values, 1, 0), 0.0)
            right = jnp.where(position <= rows_across - 2, pltpu.roll(values, per_row - 1, 0), 0.0)
            return [v.astype(jnp.bfloat16) for v in (left, values, right)]

        def put_pad(h, values, backward=False):
            sides = shifted(values)
            for side, v in enumerate(reversed(sides) if backward else sides):
                pad[pl.ds((h + 1) * per_row, per_row), pl.ds(side * c, c)] = v

        def conv_to(weight, store_at):
            for out in range(2):
                total_of = None
                for dy in range(3):
                    one = dot_nt(
                        pad[pl.ds(dy * per_row, n), :],
                        weight[pl.ds(out * hc, hc), pl.ds(dy * 3 * c, 3 * c)],
                    )
                    total_of = one if total_of is None else total_of + one
                store_at[:, pl.ds(out * hc, hc)] = total_of

        def conv_back_to(weight, store_at):
            for out in range(2):
                total_of = None
                for dy in range(3):
                    for side in range(3):
                        one = dot_nn(
                            pad[pl.ds((2 - dy) * per_row, n), pl.ds(side * c, c)],
                            weight[:, pl.ds((dy * 3 + side) * c + out * hc, hc)],
                        )
                        total_of = one if total_of is None else total_of + one
                store_at[:, pl.ds(out * hc, hc)] = total_of

        def write_stats(group, member, first, second):
            ref = sums_at(group)[0]
            for k in range(micro):
                weight = masks[k, used, :]
                ref[0, j, member, pl.ds(k, 1), :] = jnp.sum(first * weight, 0, keepdims=True)
                ref[0, j, member, pl.ds(micro + k, 1), :] = jnp.sum(
                    second * weight, 0, keepdims=True
                )

        def moments(group, member, values_ref):
            first = second = None
            for h in range(rows_high):
                v = values_ref[pl.ds(h * per_row, per_row), :]
                first = v if h == 0 else first + v
                second = v * v if h == 0 else second + v * v
            write_stats(group, member, first, second)

        def start(group):
            sums_start(group)

        def mid(group):
            sums_mid(group)

        def end(group):
            sums_end(group)

        def row(ref, k):
            return ref[pl.ds(k, 1), :]

        def total(member, k):
            return tot[member, pl.ds(k, 1), :]

        def norm_rows(index, member):
            mean_rows = inv_rows = None
            for k in range(micro):
                n_k = row(counts, k) * pixels
                mean = total(member, k) / n_k
                spread_of = total(member, micro + k) / n_k - mean * mean
                inverse = lax.rsqrt(spread_of + EPSILON)
                inv[index, pl.ds(k, 1), :] = inverse
                weight = masks[k, used, :]
                mean_rows = weight * mean if k == 0 else mean_rows + weight * mean
                inv_rows = weight * inverse if k == 0 else inv_rows + weight * inverse
            rows[0, used, :] = mean_rows
            rows[1, used, :] = inv_rows

        def normalized(index, h, raw):
            normed = (raw - rows[0, used, :]) * rows[1, used, :]
            xh[index, part(h), :] = normed
            return normed * gain[index] + shift[index]

        def back_rows(index, member):
            norm_ref[index] = tot[member]
            scale_rows = shift_rows = slope_rows = None
            for k in range(micro):
                n_k = row(counts, k) * pixels
                weight = masks[k, used, :]
                scale = inv[index, pl.ds(k, 1), :] * gain[index]
                by_shift = total(member, k) / n_k
                by_gain = total(member, micro + k) / n_k
                scale_rows = weight * scale if k == 0 else scale_rows + weight * scale
                shift_rows = weight * by_shift if k == 0 else shift_rows + weight * by_shift
                slope_rows = weight * by_gain if k == 0 else slope_rows + weight * by_gain
            rows[0, used, :] = scale_rows
            rows[1, used, :] = shift_rows
            rows[2, used, :] = slope_rows

        def partner(v):
            return jnp.where(even, pltpu.roll(v, per_row - 1, 0), pltpu.roll(v, 1, 0))

        def soft_pool(index, read):
            squares = None
            for pair in range(rows_high // 2):
                upper, lower = read(2 * pair), read(2 * pair + 1)
                top = jnp.maximum(upper, lower)
                top = jnp.maximum(top, partner(top))
                upper, lower = jnp.exp(upper - top), jnp.exp(lower - top)
                summed = upper + lower
                summed = summed + partner(summed)
                share[index, pl.ds(2 * pair * per_row, per_row), :] = upper / summed
                share[index, pl.ds((2 * pair + 1) * per_row, per_row), :] = lower / summed
                pooled = top + jnp.log(summed * 0.25)
                for lane in range(c // 128):
                    wide[lane, used, :] = pooled[:, lane * 128 : (lane + 1) * 128]
                pooled = jnp.concatenate(
                    [wide[lane, pl.ds(0, half, stride=2), :] for lane in range(c // 128)], axis=1
                )
                if leading:
                    kept = pooled
                    pooled = jnp.concatenate(
                        [pooled, jnp.zeros((32 - half, c), jnp.float32)], axis=0
                    )
                    o_ref[index, pl.ds(32 * pair, 32), :] = pooled.astype(jnp.bfloat16)
                else:
                    alive = lax.broadcasted_iota(jnp.int32, (half, c), 0) < live * (
                        rows_across // 2
                    )
                    kept = jnp.where(alive, pooled, 0.0)
                    o_ref[index, pl.ds(half * pair, half), :] = kept.astype(jnp.bfloat16)
                square = jnp.sum(kept * kept, 0, keepdims=True)
                squares = square if squares is None else squares + square
            osq[index] = squares
            if leading:
                across_cores(
                    o_ref.at[index], x_two.at[index], h_send.at[index], h_recv.at[index]
                )

        def widened(index, pair):
            if leading:
                upstream = sg_in[index, pl.ds(pl.multiple_of(32 * pair, 32), 32), :]
                upstream = upstream.astype(jnp.float32)[:half]
            else:
                upstream = og_ref[index]
            for lane in range(c // 128):
                piece = upstream[:, lane * 128 : (lane + 1) * 128]
                wide[lane, pl.ds(0, half, stride=2), :] = piece
                wide[lane, pl.ds(1, half, stride=2), :] = piece
            return jnp.concatenate(
                [wide[lane, used, :] for lane in range(c // 128)], axis=1
            )

        pair_at = 2 * (z // 2)
        far_at = lines - 2 - pair_at
        inner = (z == 1) | (z == 2)

        def send_shared(which):
            from_ref = shared_source(which)
            neighbour = 2 * pair_at + 1 - z
            for at, plane in enumerate((z, neighbour)):
                push(
                    from_ref, a_ref.at[which, z], a_send.at[b, which, at],
                    a_recv.at[b, which, 0], 0, plane * mates + j,
                )

        def shared_source(which):
            if leading:
                return source.at[0] if which == 0 else ub.at[span]
            return o_ref.at[0] if which == 0 else beside.at[0]

        def pair_lines(which, first):
            return a_ref.at[which, pl.ds(first, 2)]

        def relay_pair(which):
            got(pair_lines(which, 0), a_recv.at[b, which, 0])

            @pl.when(inner)
            def _():
                here = pair_lines(which, pair_at)
                remote(
                    here, here, a_send.at[b, which, 2], a_recv.at[b, which, 1], 0,
                    (lines - 1 - z) * mates + j,
                ).start()

        def relay_far(which):
            got(pair_lines(which, 0), a_recv.at[b, which, 1])

            @pl.when(inner)
            def _():
                here = pair_lines(which, far_at)
                remote(
                    here, here, a_send.at[b, which, 3], a_recv.at[b, which, 1], 0,
                    (2 * pair_at + 1 - z) * mates + j,
                ).start()

        def task_planes(task):
            first = (c * task) // task_rows
            return first, first + 1

        def task_slot(kind, task, plane):
            return 2 + 2 * kind + task - plane_tasks(plane)[0]

        def task_source(kind, task):
            if leading:
                return (
                    source.at[1 + task] if kind == 0
                    else ab.at[task, span] if kind == 1 else nb.at[task, span]
                )
            return o_ref.at[1 + task] if kind == 0 else beside.at[tasks * kind - 2 + task]

        def send_task(kind, task):
            first, last = task_planes(task)
            near = jnp.clip(z, first, last)
            passed_on = (z < first) | (z > last)
            tensor = 2 + tasks * kind + task
            push(
                task_source(kind, task), a_ref.at[task_slot(kind, task, near), z],
                a_send.at[b, tensor, 0],
                a_recv.at[b, tensor, jnp.where(passed_on, jnp.int32(0), jnp.int32(1))],
                0, near * mates + j,
            )

            @pl.when(jnp.logical_not(passed_on))
            def _():
                opposite = first + last - z
                push(
                    task_source(kind, task), a_ref.at[task_slot(kind, task, opposite), z],
                    a_send.at[b, tensor, 1], a_recv.at[b, tensor, 1], 0, opposite * mates + j,
                )

        def task_passes(task):
            first, last = task_planes(task)
            passes = []
            if first > 0:
                passes.append((first, 0, first, last))
            if last < lines - 1:
                passes.append((last, last + 1, lines - 1 - last, first))
            return passes

        def relay_task(kind, task):
            tensor = 2 + tasks * kind + task
            for plane, first, count, to_plane in task_passes(task):

                @pl.when(z == plane)
                def _():
                    some = pl.ds(first, count)
                    here = a_ref.at[task_slot(kind, task, plane), some]
                    got(here, a_recv.at[b, tensor, 0])
                    remote(
                        here, a_ref.at[task_slot(kind, task, to_plane), some],
                        a_send.at[b, tensor, 2], a_recv.at[b, tensor, 1], 0,
                        to_plane * mates + j,
                    ).start()

        def core_of(kind):
            return 0 if leading and kind < 2 else 1

        def deliver(at, slot, task=None):
            for step in range(mates):

                def send():
                    push(
                        a_ref.at[at], q_ref.at[slot, j], v_send.at[b, at, step],
                        q_recv.at[b, slot], core_of(at), mate(step),
                    )

                if task is None:
                    send()
                else:
                    pl.when(device_needs(mate(step), task))(send)

        def delivered(at, task=None):
            for step in range(mates):

                def wait():
                    pushed(a_ref.at[0], v_send.at[b, at, step], core_of(at), mate(step))

                if task is None:
                    wait()
                else:
                    pl.when(device_needs(mate(step), task))(wait)

        def task_done(kind, task):
            tensor = 2 + tasks * kind + task
            first, last = task_planes(task)
            for plane, count in ((first, lines - first), (last, last + 1)):

                @pl.when(z == plane)
                def _():
                    got(a_ref.at[0, pl.ds(0, count)], a_recv.at[b, tensor, 1])
                    at = task_slot(kind, task, plane)
                    if kind == 2:
                        deliver(at, at - 4, task)
                    else:
                        across_cores(
                            a_ref.at[at], a_ref.at[at], v_send.at[b, at, 0], v_recv.at[b, at]
                        )

        def task_got(kind, task):
            for plane in task_planes(task):
                at = task_slot(kind, task, plane)
                if kind == 2:

                    @pl.when((z == plane) & device_needs(me, task))
                    def _():
                        got(q_ref.at[0], q_recv.at[b, at - 4])

                else:

                    @pl.when(z == plane)
                    def _():
                        got(a_ref.at[0], v_recv.at[b, at])

        def shared_got(which):
            got(q_ref.at[0], q_recv.at[b, which])

        def relays(kind):
            for task in range(tasks):
                relay_task(kind, task)

        def done(kind):
            for task in range(tasks):
                task_done(kind, task)

        def exchange_activations():
            def here(index):
                if not leading:
                    got(beside.at[0], s_recv.at[index])

            def send_tasks(kind):
                for task in range(tasks):
                    if kind:
                        here(tasks * kind - 2 + task)
                    send_task(kind, task)

            send_shared(0)
            send_tasks(0)
            here(0)
            send_shared(1)
            relay_pair(0)
            relays(0)
            relay_pair(1)
            send_tasks(1)
            relay_far(0)
            deliver(0, 0)
            done(0)
            relays(1)
            relay_far(1)
            deliver(1, 1)
            if leading:
                across_cores(a_ref.at[1], q_ref.at[1, j], u_send.at[0], u_recv.at[0])
            send_tasks(2)
            done(1)
            relays(2)
            done(2)

        def exchange_sent():
            one_piece = a_ref.at[0, 0]
            for which in range(2):
                for at, plane in enumerate((z, 2 * pair_at + 1 - z)):
                    pushed(one_piece, a_send.at[b, which, at], 0, plane * mates + j)

                @pl.when(inner)
                def _():
                    for at in (2, 3):
                        sent(pair_lines(which, 0), a_send.at[b, which, at])

                delivered(which)
            if leading:
                sent(a_ref.at[0], u_send.at[0])
            for kind in range(3):
                for task in range(tasks):
                    first, last = task_planes(task)
                    tensor = 2 + tasks * kind + task
                    near = jnp.clip(z, first, last)
                    pushed(one_piece, a_send.at[b, tensor, 0], 0, near * mates + j)

                    @pl.when((z == first) | (z == last))
                    def _():
                        pushed(
                            one_piece, a_send.at[b, tensor, 1], 0, (first + last - z) * mates + j
                        )

                    for plane, _, count, _ in task_passes(task):

                        @pl.when(z == plane)
                        def _():
                            sent(a_ref.at[0, pl.ds(0, count)], a_send.at[b, tensor, 2])

                    for plane in (first, last):

                        @pl.when(z == plane)
                        def _():
                            at = task_slot(kind, task, plane)
                            if kind == 2:
                                delivered(at, task)
                            else:
                                sent(a_ref.at[0], v_send.at[b, at, 0])

        def spread_place(kind, task, k):
            offset, _ = kinds[kind]
            if kind < 2:
                return kind, k, offset
            number = lines * task + k
            at = pl.multiple_of(offset + lax.rem(number, tasks) * unit, unit)
            return (2 if kind == 4 else 0) + task, number // tasks, at

        def spread_refs(kind):
            return (joint, pair_ref) if kind == 2 else (turned, d_ref)

        def spread_lanes(kind):
            return pl.ds(0, 2 * n if kind == 2 else wide_n)

        def spread(kind, task=0):
            from_ref, target = spread_refs(kind)
            for k in range(lines):
                index, plane, offset = spread_place(kind, task, k)
                push(
                    from_ref.at[index, pl.ds(k * unit, unit), spread_lanes(kind)],
                    target.at[z, pl.ds(offset, unit)],
                    d_send.at[kind, task, k], d_recv.at[b, kind], core_of(kind), plane * mates + j,
                )

        def spread_sent(kind, task=0):
            from_ref, _ = spread_refs(kind)
            for k in range(lines):
                _, plane, _ = spread_place(kind, task, k)
                pushed(
                    from_ref.at[0, pl.ds(k * unit, unit), spread_lanes(kind)],
                    d_send.at[kind, task, k], core_of(kind), plane * mates + j,
                )

        def spread_got(kind):
            offset, count = kinds[kind]
            got(spread_refs(kind)[1].at[:, pl.ds(offset, count)], d_recv.at[b, kind])

        def rounded(index, member, slot, target, before=None):
            back_rows(index, member)
            first = 0 if before is None else n

            def body(h):
                value = rows[0, used, :] * (
                    dr[slot, part(h), :] - rows[1, used, :] - xh[index, part(h), :] * rows[2, used, :]
                )
                if target is None:
                    xh[index, part(h), :] = value
                else:
                    tbuf[pl.ds(first + h * per_row, per_row), :] = value
                put_pad(h, value, True)

            each(body)
            if target is None:
                return
            if before is None:
                tbuf[pl.ds(n, wide_n - n), :] = jnp.zeros((wide_n - n, c), jnp.float32)
                count = wide_n
            else:
                tbuf[span, :] = before[...]
                count = 2 * n
            target[:, pl.ds(0, count)] = jnp.transpose(tbuf[pl.ds(0, count), :]).astype(jnp.bfloat16)

        def middle():
            return pad[pl.ds(per_row, n), pl.ds(c, c)]

        def beside_core(from_ref, index):
            if not leading:
                across_cores(from_ref, beside.at[index], s_send.at[index], s_recv.at[index])

        def forward_start():
            if not leading:
                got(x_two.at[0], h_recv.at[0])
            each(lambda h: put_pad(h, source[0, part(h), :].astype(jnp.float32)))
            weight_copy(W_FIRST).wait()
            conv_to(w1s, xh.at[FIRST, span])
            moments(F_FIRST, 0, xh.at[FIRST])
            start(F_FIRST)

        def forward():
            for index in range(W_SECOND, W_TASK + tasks):
                weight_copy(index).start()
            if not leading:
                for index in range(1, 1 + tasks):
                    got(x_two.at[0], h_recv.at[index])
            weight_copy(W_SQUEEZE).wait()

            def outer_narrow(task):
                xh[NARROW + task, span] = dot_nt(source[1 + task], sqs[task, :, pl.ds(c, c)])

            outer_narrow(0)
            mid(F_FIRST)
            loop(tasks, outer_narrow, 1)
            end(F_FIRST)
            counts[...] = tot[1]
            total_ref[0] = tot[1]
            norm_rows(FIRST, 0)

            def first_act(h):
                active, slope = silu_parts(normalized(FIRST, h, xh[FIRST, part(h), :]))
                aux[FIRST, part(h), :] = slope
                ub[part(h), :] = active.astype(jnp.bfloat16)
                put_pad(h, active)

            each(first_act)
            beside_core(ub.at[span], 0)

            def narrow(task):
                xh[NARROW + task, span] += dot_nt(middle(), sqs[task, :, pl.ds(0, c)])
                moments(F_NARROW, task, xh.at[NARROW + task])

            loop(tasks, narrow)
            start(F_NARROW)
            weight_copy(W_SECOND).wait()
            conv_to(w2s, xh.at[SECOND, span])
            mid(F_NARROW)
            moments(F_SECOND, 0, xh.at[SECOND])
            start(F_SECOND)
            weight_copy(W_EXPAND).wait()
            end(F_NARROW)

            def mask_of(task):
                norm_rows(NARROW + task, task)

                def act(h):
                    active, slope = silu_parts(
                        normalized(NARROW + task, h, xh[NARROW + task, part(h), :])
                    )
                    aux[NARROW + task, part(h), :] = slope
                    ab[task, part(h), :] = active.astype(jnp.bfloat16)

                each(act)
                beside_core(ab.at[task, span], 1 + task)
                xh[MASK + task, span] = dot_nt(ab[task, span], exs[task])
                moments(F_MASK, task, xh.at[MASK + task])

            mask_of(0)
            mid(F_SECOND)
            loop(tasks, mask_of, 1)
            start(F_MASK)
            end(F_SECOND)
            norm_rows(SECOND, 0)

            def second_act(h):
                active, slope = silu_parts(normalized(SECOND, h, xh[SECOND, part(h), :]))
                aux[SECOND, part(h), :] = slope
                p_act[part(h), :] = active

            each(second_act)
            mid(F_MASK)
            soft_pool(0, lambda h: p_act[part(h), :])
            end(F_MASK)

            def task_conv(task):
                norm_rows(MASK + task, task)

                def act(h):
                    active = normalized(MASK + task, h, xh[MASK + task, part(h), :])
                    sigmoid_of = sigmoid(active)
                    aux[MASK + task, part(h), :] = sigmoid_of
                    attended = sigmoid_of * p_act[part(h), :]
                    nb[task, part(h), :] = attended.astype(jnp.bfloat16)
                    put_pad(h, attended)

                each(act)
                beside_core(nb.at[task, span], 1 + tasks + task)
                pltpu.make_async_copy(tc.at[task], tcs.at[task], w_load.at[W_TASK + task]).wait()
                conv_to(tcs.at[task], xh.at[TASK + task, span])
                moments(F_TASK, task, xh.at[TASK + task])

            loop(tasks, task_conv)
            start(F_TASK)
            mid(F_TASK)
            end(F_TASK)

            def task_pool(task):
                norm_rows(TASK + task, task)

                def act(h):
                    active, slope = silu_parts(
                        normalized(TASK + task, h, xh[TASK + task, part(h), :])
                    )
                    aux[TASK + task, part(h), :] = slope
                    active_of[part(h), :] = active

                each(act)
                soft_pool(1 + task, lambda h: active_of[part(h), :])

            loop(tasks, task_pool)
            squares = sums_at(B_TASK)[0]
            squares[0, j, tasks] = jnp.zeros((8, c), jnp.float32)
            for index in range(1 + tasks):
                squares[0, j, tasks, pl.ds(index, 1), :] = osq[index]

        def handed(index):
            if leading:
                got(sg_in.at[0], h_recv.at[1 + tasks + index])

        def backward(work):
            def task_start(task):
                handed(1 + task)
                first = second = None
                for pair in range(rows_high // 2):
                    upstream = widened(1 + task, pair)
                    for h in (2 * pair, 2 * pair + 1):
                        at = part(h)
                        up = upstream * share[1 + task, at, :] * aux[TASK + task, at, :]
                        dr[task, at, :] = up
                        by = up * xh[TASK + task, at, :]
                        first = up if first is None else first + up
                        second = by if second is None else second + by
                write_stats(B_TASK, task, first, second)

            loop(tasks, task_start)
            start(B_TASK)
            mid(B_TASK)
            end(B_TASK)
            total_ref[1] = tot[tasks]

            def task_back(task):
                rounded(TASK + task, task, task, None)
                conv_back_to(tcs.at[task], dr.at[task, span])
                first = second = None
                for h in range(rows_high):
                    at = part(h)
                    m, p = aux[MASK + task, at, :], p_act[at, :]
                    through = dr[task, at, :] * m

                    @pl.when(task == 0)
                    def _():
                        gp[at, :] = through

                    @pl.when(task > 0)
                    def _():
                        gp[at, :] += through

                    up = through * p * (1.0 - m)
                    dr[task, at, :] = up
                    by = up * xh[MASK + task, at, :]
                    first = up if first is None else first + up
                    second = by if second is None else second + by
                write_stats(B_MASK, task, first, second)

            loop(tasks, task_back)
            handed(0)
            first = second = None
            for pair in range(rows_high // 2):
                upstream = widened(0, pair)
                for h in (2 * pair, 2 * pair + 1):
                    at = part(h)
                    up = (gp[at, :] + upstream * share[0, at, :]) * aux[SECOND, at, :]
                    dr[3, at, :] = up
                    by = up * xh[SECOND, at, :]
                    first = up if first is None else first + up
                    second = by if second is None else second + by
            write_stats(B_MASK, tasks, first, second)
            start(B_MASK)
            mid(B_MASK)
            end(B_MASK)

            def mask_back(task):
                rounded(MASK + task, task, task, joint.at[task], xh.at[TASK + task, span])
                spread(2, task)
                dr[task, span] = dot_nn(middle(), exs[task])
                first = second = None
                for h in range(rows_high):
                    at = part(h)
                    up = dr[task, at, :] * aux[NARROW + task, at, :]
                    dr[task, at, :] = up
                    by = up * xh[NARROW + task, at, :]
                    first = up if first is None else first + up
                    second = by if second is None else second + by
                write_stats(B_NARROW, task, first, second)

            loop(tasks, mask_back)
            start(B_NARROW)
            rounded(SECOND, tasks, 3, turned.at[1])
            spread(1)
            mid(B_NARROW)
            conv_back_to(w2s, gp.at[span])
            end(B_NARROW)

            def narrow_back(task):
                rounded(NARROW + task, task, task, turned.at[2 + task])
                spread(4, task)
                gp[span, :] += dot_nn(middle(), sqs[task, :, pl.ds(0, c)])
                grad = dot_nn(middle(), sqs[task, :, pl.ds(c, c)])
                outer_grad(1 + task, grad)

            def outer_grad(index, grad):
                if leading:
                    ig_ref[index, span, :] = grad
                else:
                    low = grad.astype(jnp.bfloat16)
                    sg_out[index] = low
                    ig_ref[index, span, :] = low.astype(jnp.float32)
                    at = 1 + tasks + index
                    across_cores(
                        sg_out.at[index], sg_in.at[index], h_send.at[at], h_recv.at[at]
                    )

            loop(tasks, narrow_back)
            first = second = None
            for h in range(rows_high):
                at = part(h)
                up = gp[at, :] * aux[FIRST, at, :]
                dr[3, at, :] = up
                by = up * xh[FIRST, at, :]
                first = up if first is None else first + up
                second = by if second is None else second + by
            write_stats(B_FIRST, 0, first, second)
            start(B_FIRST)
            work(0)
            mid(B_FIRST)
            work(1)
            end(B_FIRST)
            rounded(FIRST, 0, 3, turned.at[0])
            if leading:
                spread(0)
            conv_back_to(w1s, dr.at[0, span])
            outer_grad(0, dr[0, span, :])
            if not leading:
                spread(0)

        def settle():
            if not leading:
                loop(1 + 2 * tasks, lambda i: sent(beside.at[0], s_send.at[i]))
            for kind in range(2):
                spread_sent(kind)
            for kind in (2, 4):
                for task in range(tasks):
                    spread_sent(kind, task)
            for group in range(GROUPS_OF_SUMS):
                sums_sent(group)
            for index in range(1 + tasks):
                if leading:
                    sent(o_ref.at[0], h_send.at[index])
                else:
                    sent(sg_out.at[0], h_send.at[1 + tasks + index])

        deep = lines * wide_n

        def fetch(from_ref, target, index):
            copy = pltpu.make_async_copy(from_ref, target, load_sem.at[index])
            copy.start()
            return copy

        def rows_held(buffer):
            return held[buffer, :, pl.ds(0, wide_n), :].reshape(deep, c)

        def slot_of(piece):
            return (task_rows * z + piece * unit) // c - plane_tasks(z)[0]

        def clear_tail():
            for buffer in range(2):
                held[buffer, :, pl.ds(n, wide_n - n), :] = jnp.zeros(
                    (lines, wide_n - n, c), jnp.bfloat16
                )

        second_at = n % 128
        own_rows = task_rows // mates

        def dealt(kind):
            return (pieces * kind, pieces) if kind < 2 else (2 * pieces, own_rows)

        def deal(kind):
            spread_got(kind)
            offset, _ = kinds[kind]
            at, count = dealt(kind)
            for step in range(mates):
                first = pl.multiple_of(offset + lax.rem(j + step, mates) * count, pieces)
                push(
                    spread_refs(kind)[1].at[:, pl.ds(first, count), pl.ds(0, wide_n)],
                    dq_ref.at[j, :, pl.ds(at, count)], dq_send.at[b, kind, step],
                    dq_recv.at[b, kind], core_of(kind), mate(step),
                )

        def deal_sent(kind):
            _, count = dealt(kind)
            for step in range(mates):
                pushed(
                    dq_ref.at[0, :, pl.ds(0, count)], dq_send.at[b, kind, step], core_of(kind),
                    mate(step),
                )

        def deal_got(kind):
            at, count = dealt(kind)
            got(dq_ref.at[:, :, pl.ds(at, count)], dq_recv.at[b, kind])

        def conv_unit(number, slot, buffer):
            def copies(column):
                which = lax.rem(column, 2)
                return (
                    pltpu.make_async_copy(
                        q_ref.at[slot, column], held.at[which, :, pl.ds(0, n)],
                        load_sem.at[which],
                    ),
                    pltpu.make_async_copy(
                        dq_ref.at[column, :, pl.ds(number * pieces, pieces)],
                        dbuf.at[which, :, :, pl.ds(0, wide_n)], load_sem.at[2 + which],
                    ),
                )

            for copy in copies(jnp.int32(0)):
                copy.start()
            lane = lax.broadcasted_iota(jnp.int32, (lines * pieces, wide_n), 1)
            here = lax.rem(lane, jnp.int32(rows_across))

            def column_terms(column):
                which = lax.rem(column, 2)

                @pl.when(column < mates - 1)
                def _():
                    for copy in copies(column + 1):
                        copy.start()

                for copy in copies(column):
                    copy.wait()
                values = dbuf[which, :, :, pl.ds(0, wide_n)].astype(jnp.float32)
                values = values.reshape(lines * pieces, wide_n)
                if number >= 2:
                    values = jnp.where(lane < n, values, 0.0)
                for side in range(3):
                    moved = values
                    if side == 0:
                        moved = jnp.where(
                            here <= rows_across - 2, pltpu.roll(values, wide_n - 1, 1), 0.0
                        )
                    elif side == 2:
                        moved = jnp.where(here >= 1, pltpu.roll(values, 1, 1), 0.0)
                    for down in range(3):
                        by = moved
                        if down == 0:
                            by = pltpu.roll(moved, wide_n - per_row, 1)
                        elif down == 2:
                            by = pltpu.roll(moved, per_row, 1)
                        by = by.astype(jnp.bfloat16)
                        at = pl.ds((3 * down + side) * pieces, pieces)
                        for line in range(lines):
                            cols[at, pl.ds(line * wide_n, wide_n)] = by[
                                line * pieces : (line + 1) * pieces
                            ]
                terms = dot_nn(cols[pl.ds(0, TAPS * pieces), pl.ds(0, deep)], rows_held(which))

                @pl.when(column == 0)
                def _():
                    for tap in range(TAPS):
                        out[buffer, :, pl.ds(tap * c, c)] = terms[
                            tap * pieces : (tap + 1) * pieces
                        ]

                @pl.when(column > 0)
                def _():
                    for tap in range(TAPS):
                        out[buffer, :, pl.ds(tap * c, c)] += terms[
                            tap * pieces : (tap + 1) * pieces
                        ]

            loop(mates, column_terms)

        def staged_conv(number, slot):
            buffer = turn[0] % 2
            turn[0] += 1
            target = (
                (r_first, r_second)[number] if number < 2
                else r_task.at[pl.ds((number - 2) * pieces, pieces)]
            )
            free(
                buffer,
                lambda: pushed(
                    out.at[buffer], t_send.at[b, number, 0], b, me, t_own.at[number, 0]
                ),
            )
            conv_unit(number, slot, buffer)
            push(
                out.at[buffer], target, t_send.at[b, number, 0], r_recv.at[number], b, me,
                t_own.at[number, 0],
            )

        def flat_terms(kind, staged, parts, lanes, first):
            offset, _ = kinds[kind]
            from_ref = spread_refs(kind)[1]
            copies = [
                fetch(
                    from_ref.at[line, pl.ds(offset + piece * unit, unit), lanes],
                    cols.at[pl.ds(piece * unit, unit), pl.ds(line * wide_n, wide_n)],
                    4 + piece * lines + line,
                )
                for piece in range(tasks)
                for line in range(lines)
            ]
            loads = []
            for at, a_kind in parts:
                for piece in range(tasks):
                    if a_kind is not None:
                        loads.append(a_ref.at[2 + 2 * a_kind + slot_of(piece)])
                    elif piece == 0:
                        loads.append(q_ref.at[1, j])

            def load(number):
                return pltpu.make_async_copy(
                    loads[number], held.at[number % 2, :, pl.ds(first, n)],
                    load_sem.at[number % 2],
                )

            load(0).start()
            for copy in copies:
                copy.wait()
            number = -1
            for at, a_kind in parts:
                for piece in range(tasks):
                    if a_kind is not None or piece == 0:
                        number += 1
                        load(number).wait()
                        if number + 1 < len(loads):
                            load(number + 1).start()
                    terms = dot_nn(
                        cols[pl.ds(piece * unit, unit), pl.ds(0, deep)], rows_held(number % 2)
                    )
                    staged[pl.ds(piece * unit, unit), pl.ds(at, c)] = terms.astype(jnp.bfloat16)

        def flat_push(target, staged, index):
            for mate_at in range(mates):
                push(
                    staged.at[pl.ds(mate_at * own_rows, own_rows)], target.at[j],
                    t_send.at[b, index, mate_at], r_recv.at[index], b, z * mates + mate_at,
                    t_own.at[index, mate_at],
                )

        def flat_sent(staged, index):
            for mate_at in range(mates):
                pushed(
                    staged.at[pl.ds(0, own_rows)], t_send.at[b, index, mate_at], b,
                    z * mates + mate_at, t_own.at[index, mate_at],
                )

        def free(name, waits):
            if name in in_use:
                in_use[name]()
            in_use[name] = waits

        def terms_second():
            deal_got(1)
            shared_got(1)
            staged_conv(1, 1)

        def terms_first():
            deal_got(0)
            shared_got(0)
            staged_conv(0, 0)

        def terms_squeeze():
            spread_got(4)
            if leading:
                got(a_ref.at[0], u_recv.at[0])
            for task in range(tasks):
                task_got(0, task)
            free(2, lambda: flat_sent(stage_flat, 5))
            flat_terms(4, stage_flat, [(0, None), (c, 0)], pl.ds(0, wide_n), 0)
            flat_push(r_squeeze, stage_flat, 5)

        def terms_expand():
            for task in range(tasks):
                task_got(1, task)
            staged = stage_flat.at[:, pl.ds(0, c)]
            free(2, lambda: flat_sent(staged, 6))
            for buffer in range(2):
                held[buffer, :, pl.ds(0, second_at), :] = jnp.zeros(
                    (lines, second_at, c), jnp.bfloat16
                )
            flat_terms(2, staged, [(0, 1)], pl.ds(n - second_at, wide_n), second_at)
            flat_push(r_expand, staged, 6)
            clear_tail()

        def terms_tasks():
            deal_got(2)
            for task in range(tasks):
                task_got(2, task)
            for number in range(own_rows // pieces):
                task = (own_rows * me + number * pieces) // c
                staged_conv(2 + number, 2 + task - plane_tasks(z)[0])

        def terms_got():
            if leading:
                for number in range(own_rows // pieces):
                    got(r_first, r_recv.at[2 + number])
            senders = pl.ds(0, mates if leading else mates - 1)
            for index, target in ((5, r_squeeze), (6, r_expand)):
                got(target.at[senders], r_recv.at[index])

        def set_up():
            image = lax.div(
                lax.broadcasted_iota(jnp.int32, (per_row, c), 0), jnp.int32(rows_across)
            )
            for k in range(micro):
                masks[k, used, :] = (
                    jnp.where(image == k, 1.0, 0.0)
                    + jnp.where(image == micro, fourth[k], 0.0)
                    + jnp.where(image == micro + 1, fifth[k], 0.0)
                )
            zero = jnp.zeros((per_row, 3 * c), jnp.bfloat16)
            pad[pl.ds(0, per_row), :] = zero
            pad[pl.ds(n + per_row, per_row), :] = zero

        return types.SimpleNamespace(
            forward_start=forward_start, forward=forward, backward=backward, settle=settle,
            set_up=set_up, clear_tail=clear_tail, exchange=exchange_activations,
            exchange_sent=exchange_sent,
            second=terms_second, first=terms_first, squeeze=terms_squeeze, expand=terms_expand,
            task_terms=terms_tasks, terms_got=terms_got, deal=deal, deal_sent=deal_sent,
        )

    weight_copy(W_FIRST).start()
    weight_copy(W_SQUEEZE).start()
    barrier = pltpu.get_barrier_semaphore()
    greeted = (
        [(section, mate(step)) for step in range(1, mates)]
        + [(section, liner(step)) for step in range(1, lines)]
        + [(other, mate(step)) for step in range(mates)]
        + [(other, liner(step)) for step in range(1, lines)]
    )
    for device in greeted:
        pl.semaphore_signal(barrier, inc=1, device_id=device, device_id_type=MESH)
    numbers = [count_ref[0, k] for k in range(micro)]
    double = [jnp.where(number >= 2, jnp.float32(1.0), jnp.float32(0.0)) for number in numbers]
    fourth, fifth = [], []
    before = jnp.float32(0.0)
    for k in range(micro):
        fourth.append(double[k] * (1.0 - before))
        fifth.append(double[k] * before)
        before = before + double[k]
    count_slot = sums_at(F_FIRST)[0]
    count_slot[0, j, 1] = jnp.zeros((8, c), jnp.float32)
    for k in range(micro):
        count_slot[0, j, 1, pl.ds(k, 1), :] = jnp.full((1, c), 1.0) * (1.0 + double[k])
    for index in range(NORMS):
        at = pl.ds(index if index < NARROW else index - NARROW, 1)
        gain[index] = gain_in[at, :] if index < NARROW else narrow_gain[index - NARROW]
        shift[index] = shift_in[at, :] if index < NARROW else narrow_shift[index - NARROW]
    in_use, turn = {}, [0]
    one, two = make_block(0), make_block(1)

    def picked_rows(values, index, h):
        doubles = [values[index, 2 * k + 1, h].astype(jnp.float32) for k in range(micro)]
        rows_of = [values[index, 2 * k, h].astype(jnp.float32) for k in range(micro)]
        for weight in (fourth, fifth):
            picked = doubles[0] * weight[0]
            for k in range(1, micro):
                picked = picked + doubles[k] * weight[k]
            rows_of.append(picked)
        return rows_of

    def compact(index):
        for h in range(high):
            x_one[index, pl.ds(h * live * across, live * across), :] = jnp.concatenate(
                picked_rows(stream, index, h), axis=0
            ).astype(jnp.bfloat16)

    def cotangents():
        for index in range(1 + tasks):
            og_ref[index] = jnp.zeros(og_ref.shape[1:], jnp.float32)
            for i, upstream in enumerate(picked_rows(cotangent, index, 0)):
                og_ref[index, pl.ds(i * (across // 4), across // 4), :] = upstream

    @pl.when(section == 0)
    def _():
        one.set_up()
        loop(1 + tasks, compact)
        pl.semaphore_wait(barrier, len(greeted))
        one.forward_start()
        one.forward()
        one.exchange()
        two.exchange()
        one.clear_tail()
        one.backward(lambda place: one.second() if place else one.deal(1))
        one.deal(0)
        one.first()
        for waits in in_use.values():
            waits()
        in_use.clear()
        for kind in range(2):
            one.deal_sent(kind)
        one.exchange_sent()
        two.exchange_sent()
        one.settle()
        one.terms_got()

    @pl.when(section == 1)
    def _():
        two.set_up()
        cotangents()
        pl.semaphore_wait(barrier, len(greeted))
        two.forward_start()
        two.forward()
        two.backward(lambda place: None)
        for kind in range(3):
            two.deal(kind)
        two.clear_tail()
        two.expand()
        two.second()
        two.squeeze()
        two.task_terms()
        two.first()
        one.deal(2)
        one.clear_tail()
        one.expand()
        one.task_terms()
        one.squeeze()
        for waits in in_use.values():
            waits()
        one.deal_sent(2)
        for kind in range(3):
            two.deal_sent(kind)
        two.settle()
        two.terms_got()


def result_kernel(plan, *refs):
    (
        count_ref, first, second, squeeze, expand, task, pooled, grads, norms, totals,
        first_out, second_out, squeeze_out, expand_out, task_out, feature_out, input_out,
        gain_out, shift_out, narrow_gain_out, narrow_shift_out, rms_out,
    ) = refs
    mates, tasks, c = plan["mates"], plan["tasks"], plan["channels"]
    section = lax.axis_index("section")
    live, micro = plan["live"], plan["micro"]
    images_of = []
    before = jnp.int32(micro)
    for k in range(micro):
        double = count_ref[0, k] >= 2
        images_of.append(jnp.where(double, before, jnp.int32(-1)))
        before = before + jnp.where(double, jnp.int32(1), jnp.int32(0))

    def aligned(values, image, rows, used):
        start = image * rows
        values = pltpu.roll(values, values.shape[0] - start, 0) if start else values
        inside = lax.broadcasted_iota(jnp.int32, (8, c), 0) < used
        return jnp.where(inside, values[:8], 0.0)

    def by_slot(values, rows, used, store):
        two = [aligned(values, micro, rows, used), aligned(values, micro + 1, rows, used)]
        for k in range(micro):
            store(2 * k, aligned(values, k, rows, used))
            which = images_of[k]
            store(
                2 * k + 1,
                jnp.where(which == micro, two[0], jnp.where(which == micro + 1, two[1], 0.0)),
            )

    def place_out(high, across, images, leading):
        per_row = images * across
        for index in range(1 + tasks):
            for h in range(plan["high"]):

                def store(slot, values):
                    input_out[index, slot, h] = values

                if h < high:
                    by_slot(grads[index, pl.ds(h * per_row, per_row), :], across, across, store)
                else:
                    for slot in range(2 * micro):
                        store(slot, jnp.zeros((8, c), jnp.float32))
            for h in range(plan["high"] // 2):

                def store_feature(slot, values):
                    feature_out[index, slot, h] = values[: plan["across"] // 2].astype(
                        jnp.bfloat16
                    )

                if h < high // 2:
                    count = 8 * (across // 2)
                    by_slot(
                        pooled[index, pl.ds(h * count, count), :].astype(jnp.float32),
                        across // 2, across // 2, store_feature,
                    )
                else:
                    for slot in range(2 * micro):
                        store_feature(slot, jnp.zeros((8, c), jnp.float32))
        cells = float(high * across // 4 * c)
        live_total = jnp.sum(totals[0, pl.ds(0, micro), pl.ds(0, 1)], axis=0, keepdims=True)
        lane = lax.broadcasted_iota(jnp.int32, (1, 1 + tasks), 1)
        result = jnp.zeros((1, 1 + tasks), jnp.float32)
        for index in range(1 + tasks):
            square = jnp.sum(totals[1, pl.ds(index, 1), :], axis=1, keepdims=True)
            result = jnp.where(lane == index, jnp.sqrt(square / (live_total * cells)), result)
        rms_out[...] = result
        for index in range(NORMS):
            shift_sum = jnp.sum(norms[index, pl.ds(0, micro), :], axis=0, keepdims=True)
            gain_sum = jnp.sum(norms[index, pl.ds(micro, micro), :], axis=0, keepdims=True)
            if index < NARROW:
                gain_out[pl.ds(index, 1), :] = gain_sum
                shift_out[pl.ds(index, 1), :] = shift_sum
            else:
                narrow_gain_out[index - NARROW] = gain_sum
                narrow_shift_out[index - NARROW] = shift_sum

    @pl.when((pl.program_id(0) == 0) & (section == 0))
    def _():
        place_out(plan["high"], plan["across"], live, True)

    @pl.when((pl.program_id(0) == 0) & (section == 1))
    def _():
        place_out(plan["high"] // 2, plan["across"] // 2, 8, False)

    for terms, target in (
        (first, first_out), (second, second_out), (squeeze, squeeze_out),
        (expand, expand_out), (task, task_out),
    ):
        count, width = terms.shape[-2:]
        per_row = width // 128
        for lane in range(per_row):
            at = pl.ds(lane * 128, 128)
            if len(terms.shape) == 2:
                summed = terms[:, at]
            else:
                summed = terms[0, :, at].astype(jnp.float32)
                for place in range(1, mates):
                    summed = summed + terms[place, :, at].astype(jnp.float32)
            target[pl.ds(lane, count, stride=per_row), :] = summed


def gathered_shards(
    stream_in, image_count, out_grad, first_conv, second_conv, squeeze, expand, task_conv,
    norm_gain, norm_shift, squeeze_gain, squeeze_shift,
):
    maps, images, high, across, c = stream_in.shape
    micro = image_count.shape[1]
    tasks = maps - 1
    groups = lax.axis_size("dp")
    mates = 4
    lines = groups // mates
    live = images - 2
    n = high * live * across
    wide_n = 256
    plan = {
        "lines": lines, "mates": mates, "tasks": tasks, "channels": c,
        "high": high, "across": across, "live": live, "wide": wide_n, "micro": micro,
    }
    conv_rows = c // groups
    task_rows = tasks * c // groups
    bf16, f32 = jnp.bfloat16, jnp.float32
    vmem = pl.BlockSpec(memory_space=pltpu.VMEM)
    whole = pl.BlockSpec(memory_space=pl.ANY)
    shapes = (
        (conv_rows, TAPS * c), (conv_rows, TAPS * c), (task_rows, 2 * c), (task_rows, c),
        (task_rows, TAPS * c),
    )
    formed = (True, True, False, False, True)
    small = 64
    single_rows = (2 + tasks) * c // lines
    out_shape = (
        [
            jax.ShapeDtypeStruct((maps, small, c), bf16),
            jax.ShapeDtypeStruct((maps, n, c), f32),
            jax.ShapeDtypeStruct((NORMS, 8, c), f32),
            jax.ShapeDtypeStruct((2, 8, c), f32),
            jax.ShapeDtypeStruct((8, lines, n, c), bf16),
            jax.ShapeDtypeStruct((8, lines, small, c), bf16),
            jax.ShapeDtypeStruct((lines, single_rows, wide_n), bf16),
            jax.ShapeDtypeStruct((lines, single_rows, 128), bf16),
            jax.ShapeDtypeStruct((lines, mates * task_rows, 2 * n), bf16),
            jax.ShapeDtypeStruct((lines, mates * task_rows, 2 * small), bf16),
        ]
        + [
            jax.ShapeDtypeStruct((4, mates, lines, n, c), bf16),
            jax.ShapeDtypeStruct((4, mates, lines, small, c), bf16),
            jax.ShapeDtypeStruct((mates, lines, 2 * conv_rows + task_rows, wide_n), bf16),
            jax.ShapeDtypeStruct((mates, lines, 2 * conv_rows + task_rows, 128), bf16),
            jax.ShapeDtypeStruct((1 + 2 * tasks, small, c), bf16),
        ]
        + [
            jax.ShapeDtypeStruct(shape, f32) if whole_terms
            else jax.ShapeDtypeStruct((mates,) + shape, bf16)
            for shape, whole_terms in zip(shapes, formed)
        ]
    )
    row = live * across
    scratch = [
        pltpu.VMEM(shape, dtype)
        for shape, dtype in (
            ((c, TAPS * c), bf16),
            ((c, TAPS * c), bf16),
            ((tasks, c, 2 * c), bf16),
            ((tasks, c, c), bf16),
            ((tasks, c, TAPS * c), bf16),
            ((NORMS, 1, c), f32),
            ((NORMS, 1, c), f32),
            ((maps, n, c), bf16),
            ((maps, small, c), bf16),
            ((maps, 16, c), f32),
            ((maps, small, c), bf16),
            ((maps, small, c), bf16),
            ((micro, row, c), f32),
            (((high + 2) * row, 3 * c), bf16),
            ((NORMS, n, c), f32),
            ((NORMS, n, c), f32),
            ((maps, n, c), f32),
            ((n, c), f32),
            ((n, c), bf16),
            ((tasks, n, c), bf16),
            ((tasks, n, c), bf16),
            ((4, n, c), f32),
            ((n, c), f32),
            ((3, row, c), f32),
            ((NORMS, micro, c), f32),
            ((4, 8, c), f32),
            ((8, c), f32),
            ((maps, 1, c), f32),
            ((c // 128, row, 128), f32),
            ((2 * n, c), f32),
            ((2 + tasks, c, wide_n), bf16),
            ((tasks, c, 2 * n), bf16),
            ((3, 2, 4, 2, 8, c), f32),
            ((4, 2, 4, 3, 8, c), f32),
            ((2, 2, 4, 4, 8, c), f32),
            ((2, lines, wide_n, c), bf16),
            ((2, lines, conv_rows, wide_n), bf16),
            ((3 * c // lines, lines * wide_n), bf16),
            ((2, conv_rows, TAPS * c), f32),
            ((mates * task_rows, 2 * c), bf16),
        )
    ] + [
        pltpu.SemaphoreType.DMA(shape)
        for shape in (
            (4 + tasks,), (GROUPS_OF_SUMS, 2), (GROUPS_OF_SUMS, 2), (2 * maps,), (2 * maps,),
            (2, NORMS, 4), (2, NORMS, 2), (2, 8, mates), (2, 8), (2, 4), (1 + 2 * tasks,),
            (1 + 2 * tasks,), (2,), (2,), (5, tasks, lines), (2, 5),
            (2, 3, mates), (2, 3), (2, 7, mates),
            (7, mates), (7,), (4 + tasks * lines,),
        )
    ]
    results = pl.pallas_call(
        functools.partial(main_kernel, plan),
        out_shape=out_shape,
        in_specs=[pl.BlockSpec(memory_space=pltpu.SMEM)] + [vmem] * 6 + [whole] * 5,
        out_specs=[vmem] * 4 + [whole] * 16,
        scratch_shapes=scratch,
        compiler_params=pltpu.CompilerParams(
            collective_id=1, has_side_effects=True, vmem_limit_bytes=62 * 2**20
        ),
        name="blocks",
    )(
        image_count, stream_in, out_grad, norm_gain[0], norm_shift[0],
        jnp.swapaxes(squeeze_gain, 0, 1), jnp.swapaxes(squeeze_shift, 0, 1), first_conv[0], second_conv[0], squeeze[0], expand[0], task_conv[0],
    )
    pooled, grads, norms, totals = results[:4]
    terms = results[15:]
    steps = 2

    def flat(shape):
        return jax.ShapeDtypeStruct((shape[0] * shape[1] // 128, 128), f32)

    results = pl.pallas_call(
        functools.partial(result_kernel, plan),
        grid=(steps,),
        out_shape=[flat(shape) for shape in shapes]
        + [
            jax.ShapeDtypeStruct((maps, images, high // 2, across // 2, c), bf16),
            jax.ShapeDtypeStruct((maps, images, high, across, c), f32),
            jax.ShapeDtypeStruct((NARROW, c), f32),
            jax.ShapeDtypeStruct((NARROW, c), f32),
            jax.ShapeDtypeStruct((tasks, 1, c), f32),
            jax.ShapeDtypeStruct((tasks, 1, c), f32),
            jax.ShapeDtypeStruct((1, maps), f32),
        ],
        in_specs=[pl.BlockSpec(memory_space=pltpu.SMEM)]
        + [
            pl.BlockSpec((shape[0] // steps, shape[1]), lambda i: (i, 0)) if whole_terms
            else pl.BlockSpec((mates, shape[0] // steps, shape[1]), lambda i: (0, i, 0))
            for shape, whole_terms in zip(shapes, formed)
        ]
        + [vmem] * 4,
        out_specs=[
            pl.BlockSpec((shape[0] // steps * shape[1] // 128, 128), lambda i: (i, 0))
            for shape in shapes
        ]
        + [vmem] * 7,
        compiler_params=pltpu.CompilerParams(vmem_limit_bytes=62 * 2**20),
        name="results",
    )(image_count, *terms, pooled, grads, norms, totals)
    first_g, second_g, squeeze_g, expand_g, task_g = (
        grad.reshape(1, -1) for grad in results[:5]
    )
    feature_out, input_out, gain_g, shift_g, narrow_gain_g, narrow_shift_g, rms = results[5:]
    return (
        feature_out[None], input_out[None], first_g, second_g, squeeze_g, expand_g, task_g,
        gain_g[None], shift_g[None], jnp.swapaxes(narrow_gain_g, 0, 1),
        jnp.swapaxes(narrow_shift_g, 0, 1), rms,
    )


def solution(mesh):
    groups = mesh.shape["dp"]
    four_by_four = groups == 4 * 4
    return jax.shard_map(
        gathered_shards if four_by_four else shards,
        mesh=mesh,
        in_specs=(
            P(None, "dp", None, None, None),
            P("dp", None),
            P(None, "dp", None, None, None),
            P("section", None, None),
            P("section", None, None),
            P("section", None, None, None),
            P("section", None, None, None),
            P("section", None, None, None),
            P("section", None, None),
            P("section", None, None),
            P("section", None, None),
            P("section", None, None),
        ),
        out_specs=(
            P("section", None, "dp", None, None, None),
            P("section", None, "dp", None, None, None),
            P("section", "dp"),
            P("section", "dp"),
            P("section", "dp"),
            P("section", "dp"),
            P("section", "dp"),
            P("section", None, None),
            P("section", None, None),
            P("section", None, None),
            P("section", None, None),
            P("section", None),
        ),
        check_vma=False,
    )
```
